32 devices in a mesh: dp: 8 (over y, x, core), ctx: 4 (over z).
Axes of the slice: x: 2, y: 2, z: 4, core: 2. Of those that a mesh axis runs over, the one named last changes fastest.
Arguments:
- tokens_in: bfloat16 [8, 2048, 1280], P('dp', 'ctx'), may hold values from -6 to 6
- block_ids: int32 [8, 2048], P('dp'), may hold values from 0 to 15, never falling along the last dimension, each value on 1 to 256 neighbouring positions
- w_qkv: bfloat16 [1280, 3840], P('dp'), may hold values from -0.15625 to 0.15625
- w_out: bfloat16 [1280, 1280], P('dp'), may hold values from -1.25 to 1.25
- w_in: bfloat16 [1280, 1280], P('dp'), may hold values from -0.15625 to 0.15625
- w_down: bfloat16 [1280, 1280], P('dp'), may hold values from -0.15625 to 0.15625
- gain_attn: bfloat16 [1280], replicated, may hold values from 0.5 to 1.5
- gain_mlp: bfloat16 [1280], replicated, may hold values from 0.5 to 1.5
- bias_in: bfloat16 [1280], replicated, may hold values from -3 to 3
- bias_down: bfloat16 [1280], replicated, may hold values from -2 to 2
- query_scale: bfloat16 [80], replicated, may hold values from 0 to 1.5
- cotangent: bfloat16 [8, 2048, 1280], P('dp', 'ctx'), may hold values from -6 to 6
Outputs:
- output: bfloat16 [8, 2048, 1280], P('dp', 'ctx')
- grad_tokens: float32 [8, 2048, 1280], P('dp', 'ctx')
- grad_w_qkv: float32 [1280, 3840], P('dp')
- grad_w_out: float32 [1280, 1280], P('dp')
- grad_w_in: float32 [1280, 1280], P('dp')
- grad_w_down: float32 [1280, 1280], P('dp')
- grad_gain_attn: float32 [1280], replicated
- grad_gain_mlp: float32 [1280], replicated
- grad_bias_in: float32 [1280], replicated
- grad_bias_down: float32 [1280], replicated
- grad_query_scale: float32 [80], replicated
The draws below stay inside these ranges and needn't reach their ends.
Inputs may be any that keep to these rules, and one draw needn't show every extreme that they name: `block_ids`: each sequence's block numbers never fall along positions, start at 0, take every value up to 15, and each block spans 1 to 256 positions.
All inputs are finite; a program needn't handle non-finite values.
Results may differ from the reference program's by a relative error of at most 0.02.
Values may be sent and summed in bfloat16 or wider, within the bound.
No kernel may reach another device: no remote copies, remote signals or barrier semaphores. Data moves between devices by JAX's collectives and lax.ppermute only.
A program may use at most 256 MiB of HBM per device.

```python
import math
import jax
import jax.numpy as jnp
import numpy as np
from jax import lax

D = 1280
H = 16
HD = 80
FF = 1280
TOK_DEV = 512
KEY_BLOCK = 512
MOST_BLOCK = 256
SEQS = 8
LEN = 2048
BLOCKS = 16
N_CTX = 4


def levels(own_key, shape, cuts, low, high):
    level = 1.0
    for axis_at, blocks in cuts:
        heights = jax.random.uniform(jax.random.fold_in(jax.random.fold_in(own_key, 6), axis_at), (blocks,), jnp.float32, low / len(cuts), high / len(cuts))
        level = level * jnp.repeat(jnp.exp(heights), shape[axis_at] // blocks).reshape((-1,) + (1,) * (len(shape) - 1 - axis_at))
    return level


def split_up(number_of, total, reach, skew):
    loads = [(1 << 20) // math.isqrt(standing ** skew) + 1 for standing in range(2, number_of + 1)]
    rest, counts = total - reach - (number_of - 1), [1] * (number_of - 1)
    while rest > 0:
        candidates = [i for i in range(number_of - 1) if counts[i] < reach]
        pool, left = sum([loads[i] for i in candidates]), rest
        for i in candidates:
            extra = min(reach - counts[i], max(1, left * loads[i] // pool), rest)
            counts[i] = counts[i] + extra
            rest = rest - extra
    return np.array([reach] + counts)


def ragged(key, number_of, total, bound, slope):
    if number_of == 2:
        one = jax.random.randint(key, (), max(1, total - bound), min(bound, total - 1) + 1)
        return jnp.stack([one, total - one])
    tallies = jnp.asarray(split_up(number_of, total, bound, slope), jnp.int32)
    pairs = (number_of - 1) // 2
    source_of, sink = tallies[1:1 + 2 * pairs:2], tallies[2:2 + 2 * pairs:2]
    margin = jnp.minimum(source_of - 1, bound - sink)
    moved = jax.random.randint(jax.random.fold_in(key, 1), (pairs,), 0, 1 << 20) % (margin + 1)
    tallies = tallies.at[1:1 + 2 * pairs:2].set(source_of - moved).at[2:2 + 2 * pairs:2].set(sink + moved)
    return tallies[jax.random.permutation(jax.random.fold_in(key, 2), number_of)]


def normal_values(key, shape, deviation, bound, cuts=(), kind=jnp.bfloat16):
    values = jax.random.normal(key, shape, jnp.float32) * deviation
    if len(cuts) > 0:
        values = levels(key, shape, cuts, -0.22, 0.18) * values
    return jnp.clip(values, min=-bound, max=bound).astype(kind)


def setup_inputs(seed: int = 0) -> dict:
    seeds = jax.random.split(jax.random.key(seed), 13)
    tokens_in = normal_values(seeds[0], (SEQS, LEN, D), 1.0, 6.0, ((0, 8), (1, 4)))
    block_ids = jax.vmap(lambda own: jnp.searchsorted(jnp.cumsum(ragged(own, BLOCKS, LEN, MOST_BLOCK, 0)), jnp.arange(LEN), side="right"))(jax.random.split(seeds[1], SEQS)).reshape((SEQS, LEN)).astype(jnp.int32)
    w_qkv = normal_values(seeds[2], (D, 3 * D), D ** -0.5, 0.15625, ((0, 8),))
    w_out = normal_values(seeds[3], (D, D), (D // 64) ** -0.5, 1.25, ((0, 8),))
    w_in = normal_values(seeds[4], (D, FF), D ** -0.5, 0.15625, ((0, 8),))
    w_down = normal_values(seeds[5], (FF, D), FF ** -0.5, 0.15625, ((0, 8),))
    gain_attn = jnp.clip(1.0 + 0.1 * jax.random.normal(seeds[6], (D,), jnp.float32), 0.5, 1.5).astype(jnp.bfloat16)
    gain_mlp = jnp.clip(1.0 + 0.1 * jax.random.normal(seeds[7], (D,), jnp.float32), 0.5, 1.5).astype(jnp.bfloat16)
    bias_in = normal_values(seeds[8], (FF,), 0.5, 3.0)
    bias_down = normal_values(seeds[9], (D,), 0.3, 2.0)
    query_scale = jnp.clip(jax.random.uniform(seeds[10], (HD,), jnp.float32, 0.0, 1.5), 0.0, 1.5).astype(jnp.bfloat16)
    cotangent = normal_values(seeds[11], (SEQS, LEN, D), 1.0, 6.0, ((0, 8), (1, 4)))
    return {"tokens_in": tokens_in, "block_ids": block_ids, "w_qkv": w_qkv, "w_out": w_out, "w_in": w_in, "w_down": w_down, "gain_attn": gain_attn, "gain_mlp": gain_mlp, "bias_in": bias_in, "bias_down": bias_down, "query_scale": query_scale, "cotangent": cotangent}


HIGHEST = lax.Precision.HIGHEST
EPSILON = 1e-06
SOFT_FACTOR = 1.442695041
MASKED = -1e+30

@jax.custom_vjp
def low(v):
    return lax.optimization_barrier(v.astype(jnp.bfloat16)).astype(jnp.float32)

@jax.custom_vjp
def low_back(v):
    return v

def low_keep(v):
    return (low(v), None)

def low_pass(kept, grad):
    return (grad,)

def back_keep(v):
    return (v, None)

def back_low(kept, grad):
    return (low(grad),)
low.defvjp(low_keep, low_pass)
low_back.defvjp(back_keep, back_low)

def dealt_blocks(block_row, groups, row_count):
    half = row_count // 2
    lower = np.arange(groups)
    sequence_order = np.stack([lower, 2 * groups - 1 - lower], 1).reshape(-1)
    stretches = block_row.reshape(2 * groups, half)
    return stretches[sequence_order].reshape(2 * groups * half)

def rms_norm(values, gain):
    inverse = lax.rsqrt(lax.optimization_barrier(jnp.mean(values * values, -1, keepdims=True)) + EPSILON)
    return values * inverse * gain

def layer(params, tokens, block_row):
    w_qkv, w_out, w_in, w_down, gain_attn, gain_mlp, bias_in, bias_down, query_scale = params
    key_ids = dealt_blocks(block_row, N_CTX, TOK_DEV)
    normed_one = low(rms_norm(tokens, gain_attn))
    qkv = low_back(jnp.dot(normed_one, w_qkv, precision=HIGHEST))
    scale_dim = SOFT_FACTOR / math.sqrt(HD) * jnp.log1p(jnp.exp(query_scale))
    scale_vec = jnp.tile(scale_dim, H)
    query = low(qkv[:, :D] * scale_vec).reshape(LEN, H, HD)
    keys = low(qkv[:, D:2 * D]).reshape(LEN, H, HD)
    values = low(qkv[:, 2 * D:]).reshape(LEN, H, HD)
    query_blocks = query.reshape(LEN // KEY_BLOCK, KEY_BLOCK, H, HD)
    id_blocks = key_ids.reshape(LEN // KEY_BLOCK, KEY_BLOCK)

    def attend(pair):
        query_part, id_part = pair
        scores = low_back(jnp.einsum('qhd,khd->hqk', query_part, keys, precision=HIGHEST))
        allowed = key_ids[None, None, :] <= id_part[None, :, None]
        scores = jnp.where(allowed, scores, MASKED)
        maximum = lax.optimization_barrier(jnp.max(scores, -1, keepdims=True))
        expo = jnp.exp(scores - maximum)
        probs = expo / lax.optimization_barrier(jnp.sum(expo, -1, keepdims=True))
        return jnp.einsum('hqk,khd->qhd', low(probs), values, precision=HIGHEST)
    attended = lax.map(jax.checkpoint(attend), (query_blocks, id_blocks)).reshape(LEN, D)
    attended_low = low(low_back(attended))
    branch_one = low_back(jnp.dot(attended_low, w_out, precision=HIGHEST))
    middle = tokens + branch_one
    normed_two = low(rms_norm(middle, gain_mlp))
    hidden_pre = low_back(jnp.dot(normed_two, w_in, precision=HIGHEST) + bias_in)
    hidden = low(hidden_pre / (1.0 + jnp.exp(-hidden_pre)))
    branch_two = low_back(jnp.dot(hidden, w_down, precision=HIGHEST) + bias_down)
    return middle + branch_two

def reference(tokens_in, block_ids, w_qkv, w_out, w_in, w_down, gain_attn, gain_mlp, bias_in, bias_down, query_scale, cotangent):
    params = (w_qkv.astype(jnp.float32), w_out.astype(jnp.float32), w_in.astype(jnp.float32), w_down.astype(jnp.float32), gain_attn.astype(jnp.float32), gain_mlp.astype(jnp.float32), bias_in.astype(jnp.float32), bias_down.astype(jnp.float32), query_scale.astype(jnp.float32))
    tokens = tokens_in.astype(jnp.float32)

    def forward(weights, inputs):
        return lax.map(lambda pair: layer(weights, pair[0], pair[1]), (inputs, block_ids))
    result, pullback = jax.vjp(forward, params, tokens)
    grads, grad_tokens = pullback(cotangent.astype(jnp.float32))
    return (result.astype(jnp.bfloat16), grad_tokens, grads[0], grads[1], grads[2], grads[3], grads[4], grads[5], grads[6], grads[7], grads[8])
```

```python
import functools
import math

import jax
import jax.numpy as jnp
import numpy as np
from jax import lax
from jax.experimental import pallas as pl
from jax.experimental.pallas import tpu as pltpu
from jax.sharding import PartitionSpec as P

EPSILON = 1e-06
SOFT_FACTOR = 1.442695041
LOG2E = 1.4426950408889634
MASKED = -1e30
HEADS_AT_ONCE = 4
AXES = ("dp", "ctx")
BF = jnp.bfloat16
F32 = jnp.float32


def nn(a, b):
    return lax.dot_general(a, b, (((1,), (0,)), ((), ())), preferred_element_type=F32)


def nt(a, b):
    return lax.dot_general(a, b, (((1,), (1,)), ((), ())), preferred_element_type=F32)


def tile_counts(ids_ref, stretch, tile, tiles):
    low = ids_ref[stretch * tile]
    high = ids_ref[stretch * tile + tile - 1]
    full = jnp.int32(0)
    need = jnp.int32(0)
    for t in range(tiles):
        full += (ids_ref[t * tile + tile - 1] <= low).astype(jnp.int32)
        need += (ids_ref[t * tile] <= high).astype(jnp.int32)
    return full, need


def forward_kernel(
    hd, tile, ids_ref, place_ref, row_ref, col_ref, qt_ref, kt_ref, vt_ref, ot_ref, lse_ref,
    knat, acc, m_ref, l_ref,
):
    tiles = kt_ref.shape[1] // tile
    group = qt_ref.shape[0] // hd
    for h in range(group):
        knat[h] = kt_ref[h * hd : (h + 1) * hd, :].T

    def one_tile(qi, carry):
        stretch = place_ref[tiles + qi]
        full, need = tile_counts(ids_ref, stretch, tile, tiles)
        qcol = pl.ds(pl.multiple_of(qi * tile, tile), tile)
        qpos = pl.ds(pl.multiple_of(stretch * tile, tile), tile)
        m_ref[...] = jnp.full(m_ref.shape, MASKED, F32)
        l_ref[...] = jnp.zeros(l_ref.shape, F32)
        acc[...] = jnp.zeros(acc.shape, F32)

        def step(t, masked):
            off = pl.ds(pl.multiple_of(place_ref[t] * tile, tile), tile)
            if masked:
                kpos = pl.ds(pl.multiple_of(t * tile, tile), tile)
                allowed = col_ref[kpos, :] <= row_ref[:, qpos]
            scores = [
                nn(knat[h, off, :], qt_ref[h * hd : (h + 1) * hd, qcol]) for h in range(group)
            ]
            for h in range(group):
                s = scores[h]
                if masked:
                    s = jnp.where(allowed, s, MASKED)
                old = m_ref[h]
                new = jnp.maximum(old, jnp.max(s, 0, keepdims=True))
                p = jnp.exp2(s - new)
                alpha = jnp.exp2(old - new)
                l_ref[h] = l_ref[h] * alpha + jnp.sum(p, 0, keepdims=True)
                m_ref[h] = new
                acc[h] = acc[h] * alpha + nn(vt_ref[h * hd : (h + 1) * hd, off], p.astype(BF))

        def full_step(t, c):
            step(t, False)
            return c

        def mask_step(t, c):
            step(t, True)
            return c

        lax.fori_loop(0, full, full_step, 0)
        lax.fori_loop(full, need, mask_step, 0)
        for h in range(group):
            ot_ref[h * hd : (h + 1) * hd, qcol] = acc[h] / l_ref[h]
            lse_ref[h, :, qcol] = m_ref[h] + jnp.log2(l_ref[h])
        return carry

    lax.fori_loop(0, qt_ref.shape[1] // tile, one_tile, 0)


def backward_kernel(
    hd, tile, ids_ref, place_ref, row_ref, col_ref, qt_ref, kt_ref, vt_ref, dot_ref, ot_ref,
    lse_ref, dqt_ref, dkt_ref, dvt_ref, knat, vnat, dq, dk, dv, delta,
):
    tiles = kt_ref.shape[1] // tile
    group = qt_ref.shape[0] // hd
    for h in range(group):
        hs = slice(h * hd, (h + 1) * hd)
        knat[h] = kt_ref[hs, :].T
        vnat[h] = vt_ref[hs, :].T
        delta[h] = jnp.sum(dot_ref[hs, :].astype(F32) * ot_ref[hs, :], 0, keepdims=True)
    dk[...] = jnp.zeros(dk.shape, F32)
    dv[...] = jnp.zeros(dv.shape, F32)

    def one_tile(qi, carry):
        stretch = place_ref[tiles + qi]
        full, need = tile_counts(ids_ref, stretch, tile, tiles)
        qcol = pl.ds(pl.multiple_of(qi * tile, tile), tile)
        qpos = pl.ds(pl.multiple_of(stretch * tile, tile), tile)
        dq[...] = jnp.zeros(dq.shape, F32)

        def step(t, masked):
            off = pl.ds(pl.multiple_of(place_ref[t] * tile, tile), tile)
            if masked:
                kpos = pl.ds(pl.multiple_of(t * tile, tile), tile)
                allowed = col_ref[kpos, :] <= row_ref[:, qpos]
            for h in range(group):
                hs = slice(h * hd, (h + 1) * hd)
                qh, doh = qt_ref[hs, qcol], dot_ref[hs, qcol]
                s = nn(knat[h, off, :], qh)
                dp = nn(vnat[h, off, :], doh)
                if masked:
                    s = jnp.where(allowed, s, MASKED)
                p = jnp.exp2(s - lse_ref[h, :, qcol])
                ds = (p * (dp - delta[h, :, qcol])).astype(BF)
                dv[h, :, off] += nt(doh, p.astype(BF))
                dk[h, :, off] += nt(qh, ds)
                dq[h] += nn(kt_ref[hs, off], ds)

        def full_step(t, c):
            step(t, False)
            return c

        def mask_step(t, c):
            step(t, True)
            return c

        lax.fori_loop(0, full, full_step, 0)
        lax.fori_loop(full, need, mask_step, 0)
        for h in range(group):
            dqt_ref[h * hd : (h + 1) * hd, qcol] = dq[h]
        return carry

    lax.fori_loop(0, qt_ref.shape[1] // tile, one_tile, 0)
    for h in range(group):
        hs = slice(h * hd, (h + 1) * hd)
        dkt_ref[hs, :] = (dk[h] * (1.0 / LOG2E)).astype(BF)
        dvt_ref[hs, :] = dv[h].astype(BF)


def attention_specs(qt, kt, hd, group):
    nq, nk = qt.shape[1], kt.shape[1]
    small = [
        pl.BlockSpec(memory_space=pltpu.SMEM),
        pl.BlockSpec(memory_space=pltpu.SMEM),
        pl.BlockSpec((1, nk), lambda i: (0, 0)),
        pl.BlockSpec((nk, 1), lambda i: (0, 0)),
    ]
    qs = pl.BlockSpec((group * hd, nq), lambda i: (i, 0))
    ks = pl.BlockSpec((group * hd, nk), lambda i: (i, 0))
    rows = pl.BlockSpec((group, 1, nq), lambda i: (i, 0, 0))
    return small, qs, ks, rows


def attention_forward(ids, place, qt, kt, vt, hd, tile):
    heads = qt.shape[0] // hd
    nq, nk = qt.shape[1], kt.shape[1]
    group = HEADS_AT_ONCE
    small, qs, ks, rows = attention_specs(qt, kt, hd, group)
    pairs = heads * nq * nk * 0.6
    return pl.pallas_call(
        functools.partial(forward_kernel, hd, tile),
        grid=(heads // group,),
        in_specs=[*small, qs, ks, ks],
        out_specs=[qs, rows],
        out_shape=[
            jax.ShapeDtypeStruct((heads * hd, nq), F32),
            jax.ShapeDtypeStruct((heads, 1, nq), F32),
        ],
        scratch_shapes=[
            pltpu.VMEM((group, nk, hd), BF),
            pltpu.VMEM((group, hd, tile), F32),
            pltpu.VMEM((group, 1, tile), F32),
            pltpu.VMEM((group, 1, tile), F32),
        ],
        compiler_params=pltpu.CompilerParams(vmem_limit_bytes=48 << 20),
        cost_estimate=pl.CostEstimate(
            flops=int(pairs * 1024), bytes_accessed=16 << 20, transcendentals=int(pairs)
        ),
    )(ids, place, ids.reshape(1, -1), ids.reshape(-1, 1), qt, kt, vt)


def attention_backward(ids, place, qt, kt, vt, dot, ot, lse, hd, tile):
    heads = qt.shape[0] // hd
    nq, nk = qt.shape[1], kt.shape[1]
    group = HEADS_AT_ONCE
    small, qs, ks, rows = attention_specs(qt, kt, hd, group)
    pairs = heads * nq * nk * 0.6
    return pl.pallas_call(
        functools.partial(backward_kernel, hd, tile),
        grid=(heads // group,),
        in_specs=[*small, qs, ks, ks, qs, qs, rows],
        out_specs=[qs, ks, ks],
        out_shape=[
            jax.ShapeDtypeStruct((heads * hd, nq), F32),
            jax.ShapeDtypeStruct((heads * hd, nk), BF),
            jax.ShapeDtypeStruct((heads * hd, nk), BF),
        ],
        scratch_shapes=[
            pltpu.VMEM((group, nk, hd), BF),
            pltpu.VMEM((group, nk, hd), BF),
            pltpu.VMEM((group, hd, tile), F32),
            pltpu.VMEM((group, hd, nk), F32),
            pltpu.VMEM((group, hd, nk), F32),
            pltpu.VMEM((group, 1, nq), F32),
        ],
        compiler_params=pltpu.CompilerParams(vmem_limit_bytes=56 << 20),
        cost_estimate=pl.CostEstimate(
            flops=int(pairs * 2560), bytes_accessed=32 << 20, transcendentals=int(pairs)
        ),
    )(ids, place, ids.reshape(1, -1), ids.reshape(-1, 1), qt, kt, vt, dot, ot, lse)


class Plan:
    def __init__(self, dp, ctx):
        self.dp, self.ctx = dp, ctx
        self.half = ctx // 2

    def index(self, pair, core, z):
        return (pair * 2 + core) * self.ctx + z

    def perm(self, to):
        out = []
        for d in range(self.dp):
            for z in range(self.ctx):
                got = to(d // 2, d % 2, z)
                if got is not None:
                    out.append((self.index(d // 2, d % 2, z), self.index(*got)))
        return out

    def home(self, core, z):
        return core == z // self.half

    def turned(self, z, k):
        first = z // self.half * self.half
        return first + (z - first + k) % self.half

    def core_swap(self):
        return self.perm(lambda p, c, z: (p, 1 - c, z))

    def pair_swap(self, mask):
        return self.perm(lambda p, c, z: (p ^ mask, c, z))

    def z_turn(self, k):
        return self.perm(lambda p, c, z: (p, c, (z + k) % self.ctx))

    def mirror(self):
        return self.perm(
            lambda p, c, z: (p, c, z) if self.home(c, z) else (p, 1 - c, self.ctx - 1 - z)
        )

    def mirror_or_turn(self, k):
        return self.perm(
            lambda p, c, z: (p, c, self.turned(z, k))
            if self.home(c, z)
            else (p, 1 - c, self.ctx - 1 - z)
        )

    def turn(self, k, away_only):
        return self.perm(
            lambda p, c, z: None
            if away_only and self.home(c, z)
            else (p, c, self.turned(z, k))
        )

    def shard(self, core, z, k, mine):
        chip = self.turned(z, -k)
        at_home = self.home(core, z) if mine else not self.home(core, z)
        return chip if at_home else self.ctx - 1 - chip

    def places(self):
        table = np.zeros((self.dp, self.ctx, 4 * self.ctx), np.int32)
        for d in range(self.dp):
            for z in range(self.ctx):
                slots = [
                    self.shard(d % 2, z, k, mine) for k in range(self.half) for mine in (True, False)
                ]
                stretches = [s for shard in slots for s in (shard, 2 * self.ctx - 1 - shard)]
                for block, stretch in enumerate(stretches):
                    table[d, z, stretch] = block
                    table[d, z, 2 * self.ctx + block] = stretch
        return table.reshape(self.dp * self.ctx, 4 * self.ctx)


def send(value, pairs):
    return lax.ppermute(value, AXES, pairs)


def inverse_of(values):
    return lax.rsqrt(jnp.mean(values * values, -1, keepdims=True) + EPSILON)


def body(
    tokens_in, block_ids, w_qkv, w_out, w_in, w_down, gain_attn, gain_mlp, bias_in, bias_down,
    query_scale, cotangent,
):
    n = lax.axis_size("ctx")
    plan = Plan(lax.axis_size("dp"), n)
    half = plan.half
    z = lax.axis_index("ctx")
    core = lax.axis_index("dp") % 2
    pair = lax.axis_index("dp") // 2
    pairs = plan.dp // 2
    home = core == z // half
    rows = tokens_in.shape[1]
    width = tokens_in.shape[2]
    hd = query_scale.shape[0]
    heads = width // hd
    part = width // 2
    tile = rows // 2
    wrows = w_qkv.shape[0]
    core_swap = plan.core_swap()

    own = tokens_in[0]
    first = send(own, plan.mirror_or_turn(1))
    token0 = jnp.where(home, own, first)
    second = send(token0, plan.turn(1, True))
    mine = [token0, jnp.where(home, first, second)]
    for k in range(2, half):
        mine.append(send(token0, plan.turn(k, False)))
    theirs = [send(m, core_swap) for m in mine]
    x_low = jnp.concatenate([a for both in zip(mine, theirs) for a in both], 0)

    ids = jnp.where(home, block_ids[0], send(block_ids[0], core_swap))
    place = lax.dynamic_index_in_dim(
        jnp.asarray(plan.places()), lax.axis_index("dp") * n + z, 0, False
    )

    split = w_qkv.reshape(wrows, 3, 2, part)
    keep = lax.dynamic_index_in_dim(split, core, 2, False).reshape(wrows, 3 * part)
    give = lax.dynamic_index_in_dim(split, 1 - core, 2, False).reshape(wrows, 3 * part)
    got = send(give, core_swap)
    block = jnp.concatenate([jnp.where(core == 0, keep, got), jnp.where(core == 0, got, keep)], 0)
    w_half = jnp.zeros((width, 3 * part), BF)
    w_half = lax.dynamic_update_slice(w_half, block, (pair * 2 * wrows, 0))
    for mask in range(1, pairs):
        w_half = lax.dynamic_update_slice(
            w_half, send(block, plan.pair_swap(mask)), ((pair ^ mask) * 2 * wrows, 0)
        )
    full_out = lax.all_gather(w_out, "dp", axis=0, tiled=True)
    full_in = lax.all_gather(w_in, "dp", axis=0, tiled=True)
    full_down = lax.all_gather(w_down, "dp", axis=0, tiled=True)

    gain_one = gain_attn.astype(F32)
    gain_two = gain_mlp.astype(F32)
    x = x_low.astype(F32)
    inverse_one = inverse_of(x)
    normed_low = (x * inverse_one * gain_one).astype(BF)
    scale_exp = jnp.exp(query_scale.astype(F32))
    scale_dim = SOFT_FACTOR / math.sqrt(hd) * jnp.log1p(scale_exp)
    scale_vec = jnp.tile(scale_dim, heads // 2)[:, None]
    wq, wkv = w_half[:, :part], w_half[:, part:]
    raw = jnp.einsum("de,td->et", wq, normed_low[: 2 * rows], preferred_element_type=F32)
    qt = (raw * (scale_vec * LOG2E)).astype(BF)
    kvt = jnp.einsum("de,td->et", wkv, normed_low, preferred_element_type=F32).astype(BF)
    kt, vt = kvt[:part], kvt[part:]
    ot, lse = attention_forward(ids, place, qt, kt, vt, hd, tile)

    o_got = send(ot[:, rows:].astype(BF), core_swap)
    o_mine = ot[:, :rows].astype(BF)
    att = jnp.concatenate(
        [jnp.where(core == 0, o_mine, o_got), jnp.where(core == 0, o_got, o_mine)], 0
    )
    tokens = token0.astype(F32)
    grad_low = send(cotangent[0], plan.mirror())
    middle = tokens + jnp.einsum("dt,de->te", att, full_out, preferred_element_type=F32)
    inverse_two = inverse_of(middle)
    normed_two_low = (middle * inverse_two * gain_two).astype(BF)
    hidden_pre = jnp.dot(normed_two_low, full_in, preferred_element_type=F32) + bias_in.astype(F32)
    sigmoid_val = 1.0 / (1.0 + jnp.exp(-hidden_pre))
    hidden_low = (hidden_pre * sigmoid_val).astype(BF)
    branch_two = jnp.dot(hidden_low, full_down, preferred_element_type=F32) + bias_down.astype(F32)
    output = send((middle + branch_two).astype(BF), plan.mirror())

    grad_out = grad_low.astype(F32)
    grad_wdown = jnp.einsum("tf,td->fd", hidden_low, grad_low, preferred_element_type=F32)
    grad_bdown = jnp.sum(grad_out, 0)
    grad_hidden = jnp.einsum("td,fd->tf", grad_low, full_down, preferred_element_type=F32)
    grad_pre = (grad_hidden * sigmoid_val * (1.0 + hidden_pre * (1.0 - sigmoid_val))).astype(BF)
    grad_win = jnp.einsum("td,tf->df", normed_two_low, grad_pre, preferred_element_type=F32)
    grad_bin = jnp.sum(grad_pre.astype(F32), 0)
    g_two = jnp.einsum("tf,df->td", grad_pre, full_in, preferred_element_type=F32)
    u_two = g_two * gain_two
    n_two = middle * inverse_two
    grad_gain_two = jnp.sum(g_two * n_two, 0)
    grad_middle = grad_out + inverse_two * (
        u_two - n_two * jnp.mean(u_two * n_two, -1, keepdims=True)
    )
    grad_mid_low = grad_middle.astype(BF)
    grad_wout = jnp.einsum("dt,te->de", att, grad_mid_low, preferred_element_type=F32)
    grad_att = jnp.einsum("de,te->dt", full_out, grad_mid_low, preferred_element_type=F32).astype(
        BF
    )
    to_keep = lax.dynamic_slice_in_dim(grad_att, core * part, part, 0)
    to_give = lax.dynamic_slice_in_dim(grad_att, (1 - core) * part, part, 0)
    dot = jnp.concatenate([to_keep, send(to_give, core_swap)], 1)

    owned = [
        lax.psum(lax.psum_scatter(g.astype(BF), "dp", scatter_dimension=0, tiled=True), "ctx")
        for g in (grad_wout, grad_win, grad_wdown)
    ]

    dq, dkt, dvt = attention_backward(ids, place, qt, kt, vt, dot, ot, lse, hd, tile)
    grad_scale = jnp.sum((dq * qt.astype(F32)).reshape(heads // 2, hd, 2 * rows), (0, 2))
    scale_slope = SOFT_FACTOR / math.sqrt(hd) * scale_exp / (1.0 + scale_exp)
    grad_scale = grad_scale * scale_slope / (scale_dim * LOG2E)
    dqt = (dq * scale_vec).astype(BF)
    dkv = jnp.concatenate([dkt, dvt], 0)

    grad_wq = jnp.einsum("td,et->de", normed_low[: 2 * rows], dqt, preferred_element_type=F32)
    grad_wkv = jnp.einsum("td,et->de", normed_low, dkv, preferred_element_type=F32)
    grad_whalf = jnp.concatenate([grad_wq.astype(BF), grad_wkv.astype(BF)], 1)

    g_kv = jnp.einsum("et,de->td", dkv, wkv, preferred_element_type=F32)
    g_q = jnp.einsum("et,de->td", dqt, wq, preferred_element_type=F32)
    g_one = g_kv + jnp.concatenate([g_q, jnp.zeros((g_kv.shape[0] - 2 * rows, width), F32)], 0)
    n_one = x * inverse_one
    grad_gain_one = jnp.sum(g_one * n_one, 0)
    u_one = g_one * gain_one
    dx = inverse_one * (u_one - n_one * jnp.mean(u_one * n_one, -1, keepdims=True))
    slots = [dx[i * rows : (i + 1) * rows] for i in range(n)]
    slots[0] = slots[0] + grad_middle
    sums = [
        slots[2 * k] + send(slots[2 * k + 1].astype(BF), core_swap).astype(F32)
        for k in range(half)
    ]
    for k in range(2, half):
        sums[0] = sums[0] + send(sums[k].astype(BF), plan.turn(-k, False)).astype(F32)
    from_away = sums[0] + send(sums[1].astype(BF), plan.turn(-1, True)).astype(F32)
    last = send(
        jnp.where(home, sums[1], from_away).astype(BF), plan.mirror_or_turn(-1)
    ).astype(F32)
    grad_tokens = jnp.where(home, sums[0] + last, last)

    def piece(p):
        return lax.dynamic_slice_in_dim(grad_whalf, p * 2 * wrows, 2 * wrows, 0)

    total = piece(pair).astype(F32)
    for mask in range(1, pairs):
        total = total + send(piece(pair ^ mask), plan.pair_swap(mask)).astype(F32)
    total = lax.psum(total.astype(BF), "ctx")
    to_keep = lax.dynamic_slice_in_dim(total, core * wrows, wrows, 0)
    to_give = lax.dynamic_slice_in_dim(total, (1 - core) * wrows, wrows, 0)
    came = send(to_give, core_swap)
    low_part = jnp.where(core == 0, to_keep, came).reshape(wrows, 3, 1, part)
    high_part = jnp.where(core == 0, came, to_keep).reshape(wrows, 3, 1, part)
    owned_qkv = jnp.concatenate([low_part, high_part], 2).reshape(wrows, 3 * width).astype(F32)

    small = lax.psum(
        (grad_gain_one, grad_gain_two, grad_bin, grad_bdown, grad_scale), ("dp", "ctx")
    )
    return (
        output[None],
        grad_tokens[None],
        owned_qkv,
        owned[0].astype(F32),
        owned[1].astype(F32),
        owned[2].astype(F32),
        small[0],
        small[1],
        small[2],
        small[3],
        small[4],
    )


def solution(mesh):
    split = P("dp", "ctx", None)
    weight = P("dp", None)
    return jax.shard_map(
        body,
        mesh=mesh,
        in_specs=(split, weight, weight, weight, weight, weight, P(), P(), P(), P(), P(), split),
        out_specs=(split, split, weight, weight, weight, weight, P(), P(), P(), P(), P()),
        check_vma=False,
    )
```

```python
import functools
import math

import jax
import jax.numpy as jnp
import numpy as np
from jax import lax
from jax.experimental import pallas as pl
from jax.experimental.pallas import tpu as pltpu
from jax.sharding import PartitionSpec as P

EPSILON = 1e-06
SOFT_FACTOR = 1.442695041
LOG2E = 1.4426950408889634
MASKED = -1e30
HEADS_AT_ONCE = 4
AXES = ("dp", "ctx")
BF = jnp.bfloat16
F32 = jnp.float32


def nn(a, b):
    return lax.dot_general(a, b, (((1,), (0,)), ((), ())), preferred_element_type=F32)


def nt(a, b):
    return lax.dot_general(a, b, (((1,), (1,)), ((), ())), preferred_element_type=F32)


def tile_counts(ids_ref, stretch, tile, tiles):
    low = ids_ref[stretch * tile]
    high = ids_ref[stretch * tile + tile - 1]
    full = jnp.int32(0)
    need = jnp.int32(0)
    for t in range(tiles):
        full += (ids_ref[t * tile + tile - 1] <= low).astype(jnp.int32)
        need += (ids_ref[t * tile] <= high).astype(jnp.int32)
    return full, need


def load_keys(parts, place_ref, hd, tile, group, knat, kt=None):
    blocks = parts[0].shape[1] // tile
    tiles = len(parts) * blocks
    for s, ref in enumerate(parts):
        for b in range(blocks):
            stretch = place_ref[tiles + s * blocks + b]
            piece = ref[:, b * tile : (b + 1) * tile]
            if kt is not None:
                kt[stretch] = piece
            if knat is not None:
                for h in range(group):
                    knat[h, stretch] = piece[h * hd : (h + 1) * hd, :].T


def forward_kernel(hd, tile, n, *refs):
    ids_ref, place_ref, row_ref, col_ref, qt_ref = refs[:5]
    k_refs, v_refs = refs[5 : 5 + n], refs[5 + n : 5 + 2 * n]
    ot_ref, lse_ref, knat, vt, acc, m_ref, l_ref = refs[5 + 2 * n :]
    group = qt_ref.shape[0] // hd
    tiles = vt.shape[0]
    load_keys(k_refs, place_ref, hd, tile, group, knat)
    load_keys(v_refs, place_ref, hd, tile, group, None, vt)

    def one_tile(qi, carry):
        stretch = place_ref[tiles + qi]
        full, need = tile_counts(ids_ref, stretch, tile, tiles)
        qcol = pl.ds(pl.multiple_of(qi * tile, tile), tile)
        qpos = pl.ds(pl.multiple_of(stretch * tile, tile), tile)
        m_ref[...] = jnp.full(m_ref.shape, MASKED, F32)
        l_ref[...] = jnp.zeros(l_ref.shape, F32)
        acc[...] = jnp.zeros(acc.shape, F32)

        def step(t, masked):
            if masked:
                kpos = pl.ds(pl.multiple_of(t * tile, tile), tile)
                allowed = col_ref[kpos, :] <= row_ref[:, qpos]
            scores = [nn(knat[h, t], qt_ref[h * hd : (h + 1) * hd, qcol]) for h in range(group)]
            for h in range(group):
                s = scores[h]
                if masked:
                    s = jnp.where(allowed, s, MASKED)
                old = m_ref[h]
                new = jnp.maximum(old, jnp.max(s, 0, keepdims=True))
                p = jnp.exp2(s - new)
                alpha = jnp.exp2(old - new)
                l_ref[h] = l_ref[h] * alpha + jnp.sum(p, 0, keepdims=True)
                m_ref[h] = new
                acc[h] = acc[h] * alpha + nn(vt[t, h * hd : (h + 1) * hd, :], p.astype(BF))

        def full_step(t, c):
            step(t, False)
            return c

        def mask_step(t, c):
            step(t, True)
            return c

        lax.fori_loop(0, full, full_step, 0)
        lax.fori_loop(full, need, mask_step, 0)
        for h in range(group):
            ot_ref[h * hd : (h + 1) * hd, qcol] = acc[h] / l_ref[h]
            lse_ref[h, :, qcol] = m_ref[h] + jnp.log2(l_ref[h])
        return carry

    lax.fori_loop(0, qt_ref.shape[1] // tile, one_tile, 0)


def backward_kernel(hd, tile, n, *refs):
    ids_ref, place_ref, row_ref, col_ref, qt_ref = refs[:5]
    k_refs, v_refs = refs[5 : 5 + n], refs[5 + n : 5 + 2 * n]
    dot_ref, ot_ref, lse_ref, scale_ref = refs[5 + 2 * n : 9 + 2 * n]
    dqt_ref, dkt_ref, dvt_ref, gs_ref = refs[9 + 2 * n : 13 + 2 * n]
    knat, vnat, kt, dq, dk, dv, delta = refs[13 + 2 * n :]
    group = qt_ref.shape[0] // hd
    tiles = kt.shape[0]
    load_keys(k_refs, place_ref, hd, tile, group, knat, kt)
    load_keys(v_refs, place_ref, hd, tile, group, vnat)
    for h in range(group):
        hs = slice(h * hd, (h + 1) * hd)
        delta[h] = jnp.sum(dot_ref[hs, :].astype(F32) * ot_ref[hs, :], 0, keepdims=True)
    dk[...] = jnp.zeros(dk.shape, F32)
    dv[...] = jnp.zeros(dv.shape, F32)
    gs_ref[...] = jnp.zeros(gs_ref.shape, F32)

    def one_tile(qi, carry):
        stretch = place_ref[tiles + qi]
        full, need = tile_counts(ids_ref, stretch, tile, tiles)
        qcol = pl.ds(pl.multiple_of(qi * tile, tile), tile)
        qpos = pl.ds(pl.multiple_of(stretch * tile, tile), tile)
        dq[...] = jnp.zeros(dq.shape, F32)

        def step(t, masked):
            if masked:
                kpos = pl.ds(pl.multiple_of(t * tile, tile), tile)
                allowed = col_ref[kpos, :] <= row_ref[:, qpos]
            for h in range(group):
                hs = slice(h * hd, (h + 1) * hd)
                qh, doh = qt_ref[hs, qcol], dot_ref[hs, qcol]
                s = nn(knat[h, t], qh)
                dp = nn(vnat[h, t], doh)
                if masked:
                    s = jnp.where(allowed, s, MASKED)
                p = jnp.exp2(s - lse_ref[h, :, qcol])
                ds = (p * (dp - delta[h, :, qcol])).astype(BF)
                dv[t, hs, :] += nt(doh, p.astype(BF))
                dk[t, hs, :] += nt(qh, ds)
                dq[hs, :] += nn(kt[t, hs, :], ds)

        def full_step(t, c):
            step(t, False)
            return c

        def mask_step(t, c):
            step(t, True)
            return c

        lax.fori_loop(0, full, full_step, 0)
        lax.fori_loop(full, need, mask_step, 0)
        gs_ref[...] += jnp.sum(dq[...] * qt_ref[:, qcol].astype(F32), 1, keepdims=True)
        dqt_ref[:, qcol] = (dq[...] * scale_ref[...]).astype(BF)
        return carry

    lax.fori_loop(0, qt_ref.shape[1] // tile, one_tile, 0)
    for b in range(tiles):
        stretch = place_ref[tiles + b]
        dkt_ref[:, b * tile : (b + 1) * tile] = (dk[stretch] * (1.0 / LOG2E)).astype(BF)
        dvt_ref[:, b * tile : (b + 1) * tile] = dv[stretch].astype(BF)


def attention_specs(qt, n, nk, hd, group):
    nq = qt.shape[1]
    size = group * hd
    values = qt.shape[0] // size
    small = [
        pl.BlockSpec(memory_space=pltpu.SMEM),
        pl.BlockSpec(memory_space=pltpu.SMEM),
        pl.BlockSpec((1, nk), lambda i: (0, 0)),
        pl.BlockSpec((nk, 1), lambda i: (0, 0)),
    ]
    qs = pl.BlockSpec((size, nq), lambda i: (i, 0))
    keys = [pl.BlockSpec((size, nk // n), lambda i: (i, 0))] * n
    vals = [pl.BlockSpec((size, nk // n), lambda i: (i + values, 0))] * n
    ks = pl.BlockSpec((size, nk), lambda i: (i, 0))
    rows = pl.BlockSpec((group, 1, nq), lambda i: (i, 0, 0))
    return small, qs, keys, vals, ks, rows


def attention_forward(ids, col, place, qt, kvs, hd, tile):
    heads = qt.shape[0] // hd
    nq, nk, n = qt.shape[1], ids.shape[0], len(kvs)
    group = HEADS_AT_ONCE
    small, qs, keys, vals, ks, rows = attention_specs(qt, n, nk, hd, group)
    pairs = heads * nq * nk * 0.6
    return pl.pallas_call(
        functools.partial(forward_kernel, hd, tile, n),
        grid=(heads // group,),
        in_specs=[*small, qs, *keys, *vals],
        out_specs=[qs, rows],
        out_shape=[
            jax.ShapeDtypeStruct((heads * hd, nq), F32),
            jax.ShapeDtypeStruct((heads, 1, nq), F32),
        ],
        scratch_shapes=[
            pltpu.VMEM((group, nk // tile, tile, hd), BF),
            pltpu.VMEM((nk // tile, group * hd, tile), BF),
            pltpu.VMEM((group, hd, tile), F32),
            pltpu.VMEM((group, 1, tile), F32),
            pltpu.VMEM((group, 1, tile), F32),
        ],
        compiler_params=pltpu.CompilerParams(vmem_limit_bytes=56 << 20),
        cost_estimate=pl.CostEstimate(
            flops=int(pairs * 1024), bytes_accessed=16 << 20, transcendentals=int(pairs)
        ),
        name="attention_forward",
    )(ids, place, ids.reshape(1, -1), col, qt, *kvs, *kvs)


def attention_backward(ids, col, place, qt, kvs, dot, ot, lse, scale_vec, hd, tile):
    heads = qt.shape[0] // hd
    nq, nk, n = qt.shape[1], ids.shape[0], len(kvs)
    group = HEADS_AT_ONCE
    small, qs, keys, vals, ks, rows = attention_specs(qt, n, nk, hd, group)
    one = pl.BlockSpec((group * hd, 1), lambda i: (i, 0))
    pairs = heads * nq * nk * 0.6
    return pl.pallas_call(
        functools.partial(backward_kernel, hd, tile, n),
        grid=(heads // group,),
        in_specs=[*small, qs, *keys, *vals, qs, qs, rows, one],
        out_specs=[qs, ks, ks, one],
        out_shape=[
            jax.ShapeDtypeStruct((heads * hd, nq), BF),
            jax.ShapeDtypeStruct((heads * hd, nk), BF),
            jax.ShapeDtypeStruct((heads * hd, nk), BF),
            jax.ShapeDtypeStruct((heads * hd, 1), F32),
        ],
        scratch_shapes=[
            pltpu.VMEM((group, nk // tile, tile, hd), BF),
            pltpu.VMEM((group, nk // tile, tile, hd), BF),
            pltpu.VMEM((nk // tile, group * hd, tile), BF),
            pltpu.VMEM((group * hd, tile), F32),
            pltpu.VMEM((nk // tile, group * hd, tile), F32),
            pltpu.VMEM((nk // tile, group * hd, tile), F32),
            pltpu.VMEM((group, 1, nq), F32),
        ],
        compiler_params=pltpu.CompilerParams(vmem_limit_bytes=60 << 20),
        cost_estimate=pl.CostEstimate(
            flops=int(pairs * 2560), bytes_accessed=32 << 20, transcendentals=int(pairs)
        ),
        name="attention_backward",
    )(ids, place, ids.reshape(1, -1), col, qt, *kvs, *kvs, dot, ot, lse, scale_vec)


def dx_kernel(part, query_tiles, dq_ref, dk_ref, dv_ref, w_ref, x_ref, gain_ref, dx_ref, gg_ref, g_ref):
    i = pl.program_id(0)
    width = x_ref.shape[1]
    step = width // 5
    dk = dk_ref[...].T
    dv = dv_ref[...].T
    for c in range(5):
        cols = slice(c * step, (c + 1) * step)
        g_ref[:, cols] = nt(dk, w_ref[cols, part : 2 * part]) + nt(dv, w_ref[cols, 2 * part :])

    @pl.when(i < query_tiles)
    def _():
        dq = dq_ref[...].T
        for c in range(5):
            cols = slice(c * step, (c + 1) * step)
            g_ref[:, cols] += nt(dq, w_ref[cols, :part])

    @pl.when(i == 0)
    def _():
        gg_ref[...] = jnp.zeros(gg_ref.shape, F32)

    x = x_ref[...].astype(F32)
    inverse = lax.rsqrt(jnp.mean(x * x, -1, keepdims=True) + EPSILON)
    normed = x * inverse
    g = g_ref[...]
    gn = g * normed
    gg_ref[...] += jnp.sum(gn, 0, keepdims=True)
    scaled = g * gain_ref[...]
    mean = jnp.mean(gn * gain_ref[...], -1, keepdims=True)
    dx_ref[...] = (inverse * (scaled - normed * mean)).astype(BF)


def input_gradient(dqt, dkt, dvt, w_half, x_low, gain):
    part, nq = dqt.shape
    nk, width = x_low.shape
    tile = 256
    query_tiles = nq // tile
    return pl.pallas_call(
        functools.partial(dx_kernel, part, query_tiles),
        grid=(nk // tile,),
        in_specs=[
            pl.BlockSpec((part, tile), lambda i: (0, jnp.minimum(i, query_tiles - 1))),
            pl.BlockSpec((part, tile), lambda i: (0, i)),
            pl.BlockSpec((part, tile), lambda i: (0, i)),
            pl.BlockSpec((width, 3 * part), lambda i: (0, 0)),
            pl.BlockSpec((tile, width), lambda i: (i, 0)),
            pl.BlockSpec((1, width), lambda i: (0, 0)),
        ],
        out_specs=[
            pl.BlockSpec((tile, width), lambda i: (i, 0)),
            pl.BlockSpec((1, width), lambda i: (0, 0)),
        ],
        out_shape=[
            jax.ShapeDtypeStruct((nk, width), BF),
            jax.ShapeDtypeStruct((1, width), F32),
        ],
        scratch_shapes=[pltpu.VMEM((tile, width), F32)],
        compiler_params=pltpu.CompilerParams(vmem_limit_bytes=40 << 20),
        cost_estimate=pl.CostEstimate(
            flops=2 * width * part * (2 * nk + nq), bytes_accessed=24 << 20, transcendentals=0
        ),
        name="input_gradient",
    )(dqt, dkt, dvt, w_half, x_low, gain)


class Plan:
    def __init__(self, dp, ctx):
        self.dp, self.ctx = dp, ctx
        self.half = ctx // 2

    def index(self, pair, core, z):
        return (pair * 2 + core) * self.ctx + z

    def perm(self, to):
        out = []
        for d in range(self.dp):
            for z in range(self.ctx):
                got = to(d // 2, d % 2, z)
                if got is not None:
                    out.append((self.index(d // 2, d % 2, z), self.index(*got)))
        return out

    def home(self, core, z):
        return core == z // self.half

    def turned(self, z, k):
        first = z // self.half * self.half
        return first + (z - first + k) % self.half

    def core_swap(self):
        return self.perm(lambda p, c, z: (p, 1 - c, z))

    def pair_swap(self, mask):
        return self.perm(lambda p, c, z: (p ^ mask, c, z))

    def z_turn(self, k):
        return self.perm(lambda p, c, z: (p, c, (z + k) % self.ctx))

    def line_in(self, s):
        last = self.ctx - 1
        to = {s: s + 1, last - s: last - s - 1}
        return self.perm(lambda p, c, z: (p, c, to[z]) if z in to else None)

    def line_out(self, s):
        last = self.ctx - 1
        to = {s + 1: s, last - s - 1: last - s}
        return self.perm(lambda p, c, z: (p, c, to[z]) if z in to else None)

    def line_middle(self):
        to = {self.half - 1: self.half, self.half: self.half - 1}
        return self.perm(lambda p, c, z: (p, c, to[z]) if z in to else None)

    def mirror(self):
        return self.perm(
            lambda p, c, z: (p, c, z) if self.home(c, z) else (p, 1 - c, self.ctx - 1 - z)
        )

    def mirror_or_turn(self, k):
        return self.perm(
            lambda p, c, z: (p, c, self.turned(z, k))
            if self.home(c, z)
            else (p, 1 - c, self.ctx - 1 - z)
        )

    def turn(self, k, away_only):
        return self.perm(
            lambda p, c, z: None
            if away_only and self.home(c, z)
            else (p, c, self.turned(z, k))
        )

    def shard(self, core, z, k, mine):
        chip = self.turned(z, -k)
        at_home = self.home(core, z) if mine else not self.home(core, z)
        return chip if at_home else self.ctx - 1 - chip

    def places(self):
        table = np.zeros((self.dp, self.ctx, 4 * self.ctx), np.int32)
        for d in range(self.dp):
            for z in range(self.ctx):
                slots = [
                    self.shard(d % 2, z, k, mine) for k in range(self.half) for mine in (True, False)
                ]
                stretches = [s for shard in slots for s in (shard, 2 * self.ctx - 1 - shard)]
                for block, stretch in enumerate(stretches):
                    table[d, z, stretch] = block
                    table[d, z, 2 * self.ctx + block] = stretch
        return table.reshape(self.dp * self.ctx, 4 * self.ctx)


def send(value, pairs):
    return lax.ppermute(value, AXES, pairs)


def line_sum(value, plan, z, kind):
    total = value.astype(F32)
    for s in range(plan.half - 1):
        total = total + send(total.astype(kind), plan.line_in(s)).astype(F32)
    sent = total.astype(kind)
    total = (sent.astype(F32) + send(sent, plan.line_middle()).astype(F32)).astype(kind)
    for s in reversed(range(plan.half - 1)):
        back = send(total, plan.line_out(s))
        total = jnp.where((z == s) | (z == plan.ctx - 1 - s), back, total)
    return total


def inverse_of(values):
    return lax.rsqrt(jnp.mean(values * values, -1, keepdims=True) + EPSILON)


def body(
    tokens_in, block_ids, w_qkv, w_out, w_in, w_down, gain_attn, gain_mlp, bias_in, bias_down,
    query_scale, cotangent,
):
    n = lax.axis_size("ctx")
    plan = Plan(lax.axis_size("dp"), n)
    half = plan.half
    z = lax.axis_index("ctx")
    core = lax.axis_index("dp") % 2
    pair = lax.axis_index("dp") // 2
    pairs = plan.dp // 2
    home = core == z // half
    rows = tokens_in.shape[1]
    width = tokens_in.shape[2]
    hd = query_scale.shape[0]
    heads = width // hd
    part = width // 2
    tile = rows // 2
    wrows = w_qkv.shape[0]
    core_swap = plan.core_swap()

    def columns(which):
        return jnp.concatenate(
            [
                lax.dynamic_slice(w_qkv, (0, i * width + which * part), (wrows, part))
                for i in range(3)
            ],
            1,
        )

    got = send(columns(1 - core), core_swap)
    keep = columns(core)
    block = jnp.concatenate([jnp.where(core == 0, keep, got), jnp.where(core == 0, got, keep)], 0)
    arrived = [send(block, plan.pair_swap(mask)) for mask in range(1, pairs)]
    w_half = jnp.zeros((width, 3 * part), BF)
    w_half = lax.dynamic_update_slice(w_half, block, (pair * 2 * wrows, 0))
    for mask, piece in enumerate(arrived, 1):
        w_half = lax.dynamic_update_slice(w_half, piece, ((pair ^ mask) * 2 * wrows, 0))

    own = tokens_in[0]
    first = send(own, plan.mirror_or_turn(1))
    token0 = jnp.where(home, own, first)
    second = send(token0, plan.turn(1, True))
    mine = [token0, jnp.where(home, first, second)]
    for k in range(2, half):
        mine.append(send(token0, plan.turn(k, False)))
    theirs = [send(m, core_swap) for m in mine]
    slots = [a for both in zip(mine, theirs) for a in both]
    x_low = jnp.concatenate(slots, 0)

    ids = jnp.where(home, block_ids[0], send(block_ids[0], core_swap))
    place = lax.dynamic_index_in_dim(
        jnp.asarray(plan.places()), lax.axis_index("dp") * n + z, 0, False
    )
    col = ids.reshape(-1, 1)

    late_out, late_in, late_down, w_half = lax.optimization_barrier((w_out, w_in, w_down, w_half))
    full_out = lax.all_gather(late_out, "dp", axis=0, tiled=True)
    full_in = lax.all_gather(late_in, "dp", axis=0, tiled=True)
    full_down = lax.all_gather(late_down, "dp", axis=0, tiled=True)

    gain_one = gain_attn.astype(F32)
    gain_two = gain_mlp.astype(F32)
    scale_exp = jnp.exp(query_scale.astype(F32))
    scale_dim = SOFT_FACTOR / math.sqrt(hd) * jnp.log1p(scale_exp)
    scale_vec = jnp.tile(scale_dim, heads // 2)[:, None]
    wq, wkv = w_half[:, :part], w_half[:, part:]

    def normed(values):
        v = values.astype(F32)
        return (v * inverse_of(v) * gain_one).astype(BF)

    normed_slots = [normed(s) for s in slots]
    kvs = [
        jnp.einsum("de,td->et", wkv, s, preferred_element_type=F32).astype(BF)
        for s in normed_slots
    ]
    normed_low = jnp.concatenate(normed_slots, 0)
    raw = jnp.einsum("de,td->et", wq, normed_low[: 2 * rows], preferred_element_type=F32)
    qt = (raw * (scale_vec * LOG2E)).astype(BF)
    ot, lse = attention_forward(ids, col, place, qt, kvs, hd, tile)

    o_got = send(ot[:, rows:].astype(BF), core_swap)
    o_mine = ot[:, :rows].astype(BF)
    att = jnp.concatenate(
        [jnp.where(core == 0, o_mine, o_got), jnp.where(core == 0, o_got, o_mine)], 0
    )
    tokens = token0.astype(F32)
    grad_low = send(cotangent[0], plan.mirror())
    middle = tokens + jnp.einsum("dt,de->te", att, full_out, preferred_element_type=F32)
    inverse_two = inverse_of(middle)
    normed_two_low = (middle * inverse_two * gain_two).astype(BF)
    hidden_pre = jnp.dot(normed_two_low, full_in, preferred_element_type=F32) + bias_in.astype(F32)
    sigmoid_val = 1.0 / (1.0 + jnp.exp(-hidden_pre))
    hidden_low = (hidden_pre * sigmoid_val).astype(BF)
    branch_two = jnp.dot(hidden_low, full_down, preferred_element_type=F32) + bias_down.astype(F32)
    output = send((middle + branch_two).astype(BF), plan.mirror())

    grad_out = grad_low.astype(F32)
    grad_wdown = jnp.einsum("tf,td->fd", hidden_low, grad_low, preferred_element_type=F32)
    grad_bdown = jnp.sum(grad_out, 0)
    grad_hidden = jnp.einsum("td,fd->tf", grad_low, full_down, preferred_element_type=F32)
    grad_pre = (grad_hidden * sigmoid_val * (1.0 + hidden_pre * (1.0 - sigmoid_val))).astype(BF)
    grad_win = jnp.einsum("td,tf->df", normed_two_low, grad_pre, preferred_element_type=F32)
    grad_bin = jnp.sum(grad_pre.astype(F32), 0)
    g_two = jnp.einsum("tf,df->td", grad_pre, full_in, preferred_element_type=F32)
    u_two = g_two * gain_two
    n_two = middle * inverse_two
    grad_gain_two = jnp.sum(g_two * n_two, 0)
    grad_middle = grad_out + inverse_two * (
        u_two - n_two * jnp.mean(u_two * n_two, -1, keepdims=True)
    )
    grad_mid_low = grad_middle.astype(BF)
    grad_wout = jnp.einsum("dt,te->de", att, grad_mid_low, preferred_element_type=F32)
    grad_att = jnp.einsum("de,te->dt", full_out, grad_mid_low, preferred_element_type=F32).astype(
        BF
    )
    to_keep = lax.dynamic_slice_in_dim(grad_att, core * part, part, 0)
    to_give = lax.dynamic_slice_in_dim(grad_att, (1 - core) * part, part, 0)
    dot = jnp.concatenate([to_keep, send(to_give, core_swap)], 1)

    joined = jnp.concatenate([g.astype(BF) for g in (grad_wdown, grad_win, grad_wout)], 1)
    scattered = lax.psum_scatter(joined, "dp", scatter_dimension=0, tiled=True)

    dqt, dkt, dvt, gs = attention_backward(
        ids, col, place, qt, kvs, dot, ot, lse, scale_vec, hd, tile
    )
    grad_scale = jnp.sum(gs.reshape(heads // 2, hd), 0)
    scale_slope = SOFT_FACTOR / math.sqrt(hd) * scale_exp / (1.0 + scale_exp)
    grad_scale = grad_scale * scale_slope / (scale_dim * LOG2E)

    query_rows = normed_low[: 2 * rows]
    grads = [
        jnp.einsum("td,et->de", a, g, preferred_element_type=F32).astype(BF)
        for a, g in ((query_rows, dqt), (normed_low, dkt), (normed_low, dvt))
    ]
    grad_whalf = jnp.concatenate(grads, 1)

    def piece_of(p):
        return lax.dynamic_slice_in_dim(grad_whalf, p * 2 * wrows, 2 * wrows, 0)

    pieces = [send(piece_of(pair ^ mask), plan.pair_swap(mask)) for mask in range(1, pairs)]

    dx, grad_gain_one = input_gradient(dqt, dkt, dvt, w_half, x_low, gain_one.reshape(1, -1))
    parts = [dx[i * rows : (i + 1) * rows] for i in range(n)]
    sums = [
        parts[2 * k].astype(F32) + send(parts[2 * k + 1], core_swap).astype(F32)
        for k in range(half)
    ]
    sums[0] = sums[0] + grad_middle
    for k in range(2, half):
        sums[0] = sums[0] + send(sums[k].astype(BF), plan.turn(-k, False)).astype(F32)
    from_away = sums[0] + send(sums[1].astype(BF), plan.turn(-1, True)).astype(F32)
    last = send(
        jnp.where(home, sums[1], from_away).astype(BF), plan.mirror_or_turn(-1)
    ).astype(F32)
    grad_tokens = jnp.where(home, sums[0] + last, last)

    total = piece_of(pair).astype(F32)
    for piece in pieces:
        total = total + piece.astype(F32)
    others = [
        line_sum(scattered[:, i * width : (i + 1) * width], plan, z, BF).astype(F32)
        for i in range(3)
    ]
    swapped = []
    for i in range(3):
        one = line_sum(total[:, i * part : (i + 1) * part], plan, z, BF)
        to_keep = lax.dynamic_slice_in_dim(one, core * wrows, wrows, 0)
        to_give = lax.dynamic_slice_in_dim(one, (1 - core) * wrows, wrows, 0)
        came = send(to_give, core_swap)
        swapped.append(jnp.where(core == 0, to_keep, came))
        swapped.append(jnp.where(core == 0, came, to_keep))
    owned_qkv = jnp.concatenate(swapped, 1).astype(F32)

    small = jnp.concatenate(
        [grad_gain_one.reshape(-1), grad_gain_two, grad_bin, grad_bdown, grad_scale]
    )
    small_size = small.shape[0]
    small = jnp.pad(small, (0, -small_size % 1024)).reshape(-1, 128)
    small = small + send(small, core_swap)
    mask = 1
    while mask < pairs:
        small = small + send(small, plan.pair_swap(mask))
        mask *= 2
    small = line_sum(small, plan, z, F32).reshape(-1)
    return (
        output[None],
        grad_tokens[None],
        owned_qkv,
        others[2],
        others[1],
        others[0],
        small[:width],
        small[width : 2 * width],
        small[2 * width : 3 * width],
        small[3 * width : 4 * width],
        small[4 * width : small_size],
    )


def solution(mesh):
    split = P("dp", "ctx", None)
    weight = P("dp", None)
    return jax.shard_map(
        body,
        mesh=mesh,
        in_specs=(split, weight, weight, weight, weight, weight, P(), P(), P(), P(), P(), split),
        out_specs=(split, split, weight, weight, weight, weight, P(), P(), P(), P(), P()),
        check_vma=False,
    )
```

```python
import functools
import math

import jax
import jax.numpy as jnp
import numpy as np
from jax import lax
from jax.experimental import pallas as pl
from jax.experimental.pallas import tpu as pltpu
from jax.sharding import PartitionSpec as P

EPSILON = 1e-06
SOFT_FACTOR = 1.442695041
LOG2E = 1.4426950408889634
MASKED = -1e30
HEADS_AT_ONCE = 4
AXES = ("dp", "ctx")
BF = jnp.bfloat16
F32 = jnp.float32


def nn(a, b):
    return lax.dot_general(a, b, (((1,), (0,)), ((), ())), preferred_element_type=F32)


def nt(a, b):
    return lax.dot_general(a, b, (((1,), (1,)), ((), ())), preferred_element_type=F32)


def tile_counts(ids_ref, stretch, tile, tiles):
    low = ids_ref[stretch * tile]
    high = ids_ref[stretch * tile + tile - 1]
    full = jnp.int32(0)
    need = jnp.int32(0)
    for t in range(tiles):
        full += (ids_ref[t * tile + tile - 1] <= low).astype(jnp.int32)
        need += (ids_ref[t * tile] <= high).astype(jnp.int32)
    return full, need


def project_kernel(part, query_slots, n, core_ref, gain_ref, scale_ref, *refs):
    x_refs, w_refs = refs[:n], refs[n : n + 3]
    qt_ref, kt_ref, vt_ref, xt_ref, wt, xs = refs[n + 3 :]
    i = pl.program_id(0)

    @pl.when(i == 0)
    def _():
        for j, ref in enumerate(w_refs):
            wt[j * part : (j + 1) * part, :] = ref[...].T

    for s in range(n):

        @pl.when(i == s)
        def _(s=s):
            xs[...] = x_refs[s][...]

    x = xs[...].astype(F32)
    inverse = lax.rsqrt(jnp.mean(x * x, -1, keepdims=True) + EPSILON)
    xt_ref[...] = (x * inverse * gain_ref[...]).astype(BF).T
    kt_ref[...] = nn(wt[part : 2 * part, :], xt_ref[...]).astype(BF)
    vt_ref[...] = nn(wt[2 * part :, :], xt_ref[...]).astype(BF)

    @pl.when(i < query_slots)
    def _():
        qt_ref[...] = (nn(wt[:part, :], xt_ref[...]) * scale_ref[...]).astype(BF)


def project(slots, w_full, core, gain, scale):
    n = len(slots)
    rows, width = slots[0].shape
    part = width // 2
    query_slots = 2
    once = pl.Buffered(1)
    return pl.pallas_call(
        functools.partial(project_kernel, part, query_slots, n),
        grid_spec=pltpu.PrefetchScalarGridSpec(
            num_scalar_prefetch=1,
            grid=(n,),
            in_specs=[
                pl.BlockSpec((1, width), lambda i, c: (0, 0)),
                pl.BlockSpec((part, 1), lambda i, c: (0, 0)),
                *[pl.BlockSpec((rows, width), lambda i, c: (0, 0), pipeline_mode=once)] * n,
                *[
                    pl.BlockSpec(
                        (width, part), lambda i, c, j=j: (0, 2 * j + c[0]), pipeline_mode=once
                    )
                    for j in range(3)
                ],
            ],
            out_specs=[
                pl.BlockSpec((part, rows), lambda i, c: (0, jnp.minimum(i, query_slots - 1))),
                pl.BlockSpec((part, rows), lambda i, c: (0, i)),
                pl.BlockSpec((part, rows), lambda i, c: (0, i)),
                pl.BlockSpec((width, rows), lambda i, c: (0, i)),
            ],
            scratch_shapes=[pltpu.VMEM((3 * part, width), BF), pltpu.VMEM((rows, width), BF)],
        ),
        out_shape=[
            jax.ShapeDtypeStruct((part, query_slots * rows), BF),
            jax.ShapeDtypeStruct((part, n * rows), BF),
            jax.ShapeDtypeStruct((part, n * rows), BF),
            jax.ShapeDtypeStruct((width, n * rows), BF),
        ],
        compiler_params=pltpu.CompilerParams(vmem_limit_bytes=60 << 20),
        cost_estimate=pl.CostEstimate(
            flops=2 * width * part * rows * (2 * n + query_slots),
            bytes_accessed=24 << 20,
            transcendentals=0,
        ),
        name="project",
    )(core, gain, scale, *slots, *[w_full] * 3)


def mlp_kernel(
    part, core_ref, near_ref, far_ref, w_ref, x_ref, cot_ref, gain_ref, bin_ref, bdown_ref,
    out_ref, keep_ref, give_ref, gmid_ref, ht_ref, nt_ref, gpre_ref, gml_ref, gain_out, bin_out,
    bdown_out, middle, normed, hidden, slope, g_ref,
):
    width = x_ref.shape[1]
    step = width // 5
    chunks = [slice(c * step, (c + 1) * step) for c in range(5)]
    down, inner = 0, width
    outer = 2 * width
    core = core_ref[0]
    near_rows = pl.ds(pl.multiple_of(core * part, part), part)
    far_rows = pl.ds(pl.multiple_of((1 - core) * part, part), part)

    @pl.when(pl.program_id(0) == 0)
    def _():
        for ref in (gain_out, bin_out, bdown_out):
            ref[...] = jnp.zeros(ref.shape, F32)

    near, far = near_ref[0].T, far_ref[...].T
    for cols in chunks:
        at = slice(outer + cols.start, outer + cols.stop)
        middle[:, cols] = (
            x_ref[:, cols].astype(F32) + nn(near, w_ref[near_rows, at]) + nn(far, w_ref[far_rows, at])
        )
    mid = middle[...]
    inverse = lax.rsqrt(jnp.mean(mid * mid, -1, keepdims=True) + EPSILON)
    normed[...] = (mid * inverse * gain_ref[...]).astype(BF)
    nt_ref[...] = normed[...].T
    for cols in chunks:
        at = slice(inner + cols.start, inner + cols.stop)
        pre = nn(normed[...], w_ref[:, at]) + bin_ref[:, cols]
        sigma = 1.0 / (1.0 + jnp.exp(-pre))
        hidden[:, cols] = (pre * sigma).astype(BF)
        slope[:, cols] = sigma * (1.0 + pre * (1.0 - sigma))
    ht_ref[...] = hidden[...].T
    for cols in chunks:
        at = slice(down + cols.start, down + cols.stop)
        out_ref[:, cols] = (
            middle[:, cols] + nn(hidden[...], w_ref[:, at]) + bdown_ref[:, cols]
        ).astype(BF)
    for cols in chunks:
        gpre_ref[:, cols] = (
            nt(cot_ref[...], w_ref[cols, down : down + width]) * slope[:, cols]
        ).astype(BF)
    for cols in chunks:
        g_ref[:, cols] = nt(gpre_ref[...], w_ref[cols, inner : inner + width])
    bin_out[...] += jnp.sum(gpre_ref[...].astype(F32), 0, keepdims=True)
    cot = cot_ref[...].astype(F32)
    bdown_out[...] += jnp.sum(cot, 0, keepdims=True)
    turned = middle[...] * inverse
    gn = g_ref[...] * turned
    gain_out[...] += jnp.sum(gn, 0, keepdims=True)
    mean = jnp.mean(gn * gain_ref[...], -1, keepdims=True)
    gmid = cot + inverse * (g_ref[...] * gain_ref[...] - turned * mean)
    gmid_ref[...] = gmid
    gml_ref[...] = gmid.astype(BF)
    low = gml_ref[...]
    keep_ref[...] = nt(w_ref[near_rows, outer : outer + width], low).astype(BF)
    give_ref[...] = nt(w_ref[far_rows, outer : outer + width], low).astype(BF)


def mlp(halves, far, weights, x, cot, core, gain, bias_in, bias_down):
    part, rows = far.shape
    width = x.shape[1]
    tile = 256
    once = pl.Buffered(1)
    row = pl.BlockSpec((tile, width), lambda i, c: (i, 0))
    feature = pl.BlockSpec((part, tile), lambda i, c: (0, i))
    wide = pl.BlockSpec((width, tile), lambda i, c: (0, i))
    vector = pl.BlockSpec((1, width), lambda i, c: (0, 0))
    return pl.pallas_call(
        functools.partial(mlp_kernel, part),
        grid_spec=pltpu.PrefetchScalarGridSpec(
            num_scalar_prefetch=1,
            grid=(rows // tile,),
            in_specs=[
                pl.BlockSpec((1, part, tile), lambda i, c: (0, 0, i)),
                feature,
                pl.BlockSpec(weights.shape, lambda i, c: (0, 0), pipeline_mode=once),
                row, row, vector, vector, vector,
            ],
            out_specs=[
                row, feature, feature, row, wide, wide, row, row, vector, vector, vector
            ],
            scratch_shapes=[
                pltpu.VMEM((tile, width), F32),
                pltpu.VMEM((tile, width), BF),
                pltpu.VMEM((tile, width), BF),
                pltpu.VMEM((tile, width), F32),
                pltpu.VMEM((tile, width), F32),
            ],
        ),
        out_shape=[
            jax.ShapeDtypeStruct((rows, width), BF),
            jax.ShapeDtypeStruct((part, rows), BF),
            jax.ShapeDtypeStruct((part, rows), BF),
            jax.ShapeDtypeStruct((rows, width), F32),
            jax.ShapeDtypeStruct((width, rows), BF),
            jax.ShapeDtypeStruct((width, rows), BF),
            jax.ShapeDtypeStruct((rows, width), BF),
            jax.ShapeDtypeStruct((rows, width), BF),
            jax.ShapeDtypeStruct((1, width), F32),
            jax.ShapeDtypeStruct((1, width), F32),
            jax.ShapeDtypeStruct((1, width), F32),
        ],
        compiler_params=pltpu.CompilerParams(vmem_limit_bytes=56 << 20),
        cost_estimate=pl.CostEstimate(
            flops=12 * rows * width * width, bytes_accessed=24 << 20, transcendentals=rows * width
        ),
        name="mlp",
    )(core, halves, far, weights, x, cot, gain, bias_in, bias_down)


def mlp_weight_kernel(part, core_ref, near_ref, far_ref, ht_ref, nt_ref, cot_ref, gpre_ref, gml_ref, out_ref):
    width = ht_ref.shape[0]
    core = core_ref[0]

    def half(i, carry):
        own = pl.ds(pl.multiple_of(i * part, part), part)
        out_ref[own, :width] = nn(ht_ref[own, :], cot_ref[...]).astype(BF)
        out_ref[own, width : 2 * width] = nn(nt_ref[own, :], gpre_ref[...]).astype(BF)
        return carry

    lax.fori_loop(0, 2, half, 0)
    near_rows = pl.ds(pl.multiple_of(core * part, part), part)
    far_rows = pl.ds(pl.multiple_of((1 - core) * part, part), part)
    out_ref[near_rows, 2 * width :] = nn(near_ref[0], gml_ref[...]).astype(BF)
    out_ref[far_rows, 2 * width :] = nn(far_ref[...], gml_ref[...]).astype(BF)


def mlp_weights(halves, far, ht, nrt, cot, gpre, gml, core):
    part, rows = far.shape
    width = cot.shape[1]
    whole = pl.BlockSpec(memory_space=pltpu.VMEM)
    return pl.pallas_call(
        functools.partial(mlp_weight_kernel, part),
        grid=(1,),
        in_specs=[
            pl.BlockSpec(memory_space=pltpu.SMEM),
            pl.BlockSpec((1, part, rows), lambda i: (0, 0, 0)),
            *[whole] * 6,
        ],
        out_specs=whole,
        out_shape=jax.ShapeDtypeStruct((width, 3 * width), BF),
        compiler_params=pltpu.CompilerParams(vmem_limit_bytes=48 << 20),
        cost_estimate=pl.CostEstimate(
            flops=6 * rows * width * width, bytes_accessed=20 << 20, transcendentals=0
        ),
        name="mlp_weights",
    )(core, halves, far, ht, nrt, cot, gpre, gml)


def load_keys(ref, place_ref, hd, tile, group, knat, kt=None):
    tiles = ref.shape[1] // tile
    for b in range(tiles):
        stretch = place_ref[tiles + b]
        piece = ref[:, b * tile : (b + 1) * tile]
        if kt is not None:
            kt[stretch] = piece
        if knat is not None:
            for h in range(group):
                knat[h, stretch] = piece[h * hd : (h + 1) * hd, :].T


def forward_kernel(
    hd, tile, ids_ref, place_ref, row_ref, col_ref, qt_ref, kt_ref, vt_ref, ot_ref, lse_ref,
    knat, vt, acc, m_ref, l_ref,
):
    group = qt_ref.shape[0] // hd
    tiles = vt.shape[0]
    load_keys(kt_ref, place_ref, hd, tile, group, knat)
    load_keys(vt_ref, place_ref, hd, tile, group, None, vt)
    per_half = ot_ref.shape[2] // tile

    def one_tile(qi, carry):
        stretch = place_ref[tiles + qi]
        full, need = tile_counts(ids_ref, stretch, tile, tiles)
        qcol = pl.ds(pl.multiple_of(qi * tile, tile), tile)
        qpos = pl.ds(pl.multiple_of(stretch * tile, tile), tile)
        m_ref[...] = jnp.full(m_ref.shape, MASKED, F32)
        l_ref[...] = jnp.zeros(l_ref.shape, F32)
        acc[...] = jnp.zeros(acc.shape, F32)

        def step(t, masked):
            if masked:
                kpos = pl.ds(pl.multiple_of(t * tile, tile), tile)
                allowed = col_ref[kpos, :] <= row_ref[:, qpos]
            scores = [nn(knat[h, t], qt_ref[h * hd : (h + 1) * hd, qcol]) for h in range(group)]
            for h in range(group):
                s = scores[h]
                if masked:
                    s = jnp.where(allowed, s, MASKED)
                old = m_ref[h]
                new = jnp.maximum(old, jnp.max(s, 0, keepdims=True))
                p = jnp.exp2(s - new)
                alpha = jnp.exp2(old - new)
                l_ref[h] = l_ref[h] * alpha + jnp.sum(p, 0, keepdims=True)
                m_ref[h] = new
                acc[h] = acc[h] * alpha + nn(vt[t, h * hd : (h + 1) * hd, :], p.astype(BF))

        def full_step(t, c):
            step(t, False)
            return c

        def mask_step(t, c):
            step(t, True)
            return c

        lax.fori_loop(0, full, full_step, 0)
        lax.fori_loop(full, need, mask_step, 0)
        for h in range(group):
            inner = pl.ds(pl.multiple_of((qi % per_half) * tile, tile), tile)
            ot_ref[qi // per_half, h * hd : (h + 1) * hd, inner] = (acc[h] / l_ref[h]).astype(BF)
            lse_ref[h, :, qcol] = m_ref[h] + jnp.log2(l_ref[h])
        return carry

    lax.fori_loop(0, qt_ref.shape[1] // tile, one_tile, 0)


def backward_kernel(
    hd, tile, ids_ref, place_ref, row_ref, col_ref, qt_ref, kt_ref, vt_ref, near_ref, far_ref,
    ot_ref, lse_ref, scale_ref, dqt_ref, dkvt_ref, gs_ref, knat, vnat, kt, dq, dk, dv, delta, dot,
):
    group = qt_ref.shape[0] // hd
    tiles = kt.shape[0]
    load_keys(kt_ref, place_ref, hd, tile, group, knat, kt)
    load_keys(vt_ref, place_ref, hd, tile, group, vnat)
    per_half = near_ref.shape[1] // tile
    for half, ref in enumerate((near_ref, far_ref)):
        for b in range(per_half):
            cols = slice(b * tile, (b + 1) * tile)
            dot[half * per_half + b] = ref[:, cols]
            product = ref[:, cols].astype(F32) * ot_ref[half, :, cols].astype(F32)
            for h in range(group):
                delta[half * per_half + b, h] = jnp.sum(
                    product[h * hd : (h + 1) * hd], 0, keepdims=True
                )
    dk[...] = jnp.zeros(dk.shape, F32)
    dv[...] = jnp.zeros(dv.shape, F32)
    gs_ref[...] = jnp.zeros(gs_ref.shape, F32)

    def one_tile(qi, carry):
        stretch = place_ref[tiles + qi]
        full, need = tile_counts(ids_ref, stretch, tile, tiles)
        qcol = pl.ds(pl.multiple_of(qi * tile, tile), tile)
        qpos = pl.ds(pl.multiple_of(stretch * tile, tile), tile)
        dq[...] = jnp.zeros(dq.shape, F32)

        def step(t, masked):
            if masked:
                kpos = pl.ds(pl.multiple_of(t * tile, tile), tile)
                allowed = col_ref[kpos, :] <= row_ref[:, qpos]
            for h in range(group):
                hs = slice(h * hd, (h + 1) * hd)
                qh, doh = qt_ref[hs, qcol], dot[qi, hs, :]
                s = nn(knat[h, t], qh)
                dp = nn(vnat[h, t], doh)
                if masked:
                    s = jnp.where(allowed, s, MASKED)
                p = jnp.exp2(s - lse_ref[h, :, qcol])
                ds = (p * (dp - delta[qi, h])).astype(BF)
                dv[t, hs, :] += nt(doh, p.astype(BF))
                dk[t, hs, :] += nt(qh, ds)
                dq[hs, :] += nn(kt[t, hs, :], ds)

        def full_step(t, c):
            step(t, False)
            return c

        def mask_step(t, c):
            step(t, True)
            return c

        lax.fori_loop(0, full, full_step, 0)
        lax.fori_loop(full, need, mask_step, 0)
        gs_ref[...] += jnp.sum(dq[...] * qt_ref[:, qcol].astype(F32), 1, keepdims=True)
        dqt_ref[:, qcol] = (dq[...] * scale_ref[...]).astype(BF)
        return carry

    lax.fori_loop(0, qt_ref.shape[1] // tile, one_tile, 0)
    for b in range(tiles):
        stretch = place_ref[tiles + b]
        cols = slice(b * tile, (b + 1) * tile)
        dkvt_ref[: group * hd, cols] = (dk[stretch] * (1.0 / LOG2E)).astype(BF)
        dkvt_ref[group * hd :, cols] = dv[stretch].astype(BF)


def attention_specs(nq, nk, hd, group, at):
    size = group * hd
    return (
        [
            pl.BlockSpec(memory_space=pltpu.SMEM),
            pl.BlockSpec(memory_space=pltpu.SMEM),
            pl.BlockSpec((1, nk), lambda i: (0, 0)),
            pl.BlockSpec((nk, 1), lambda i: (0, 0)),
            pl.BlockSpec((size, nq), lambda i: (i + at, 0)),
            pl.BlockSpec((size, nk), lambda i: (i + at, 0)),
            pl.BlockSpec((size, nk), lambda i: (i + at, 0)),
        ],
        pl.BlockSpec((2, size, nq // 2), lambda i: (0, i + at, 0)),
        pl.BlockSpec((group, 1, nq), lambda i: (i + at, 0, 0)),
    )


def attention_forward(ids, col, place, qt, kt, vt, hd, tile):
    heads = qt.shape[0] // hd
    nq, nk = qt.shape[1], kt.shape[1]
    group = HEADS_AT_ONCE
    common, halves, rows = attention_specs(nq, nk, hd, group, 0)
    pairs = heads * nq * nk * 0.6
    return pl.pallas_call(
        functools.partial(forward_kernel, hd, tile),
        grid=(heads // group,),
        in_specs=common,
        out_specs=[halves, rows],
        out_shape=[
            jax.ShapeDtypeStruct((2, heads * hd, nq // 2), BF),
            jax.ShapeDtypeStruct((heads, 1, nq), F32),
        ],
        scratch_shapes=[
            pltpu.VMEM((group, nk // tile, tile, hd), BF),
            pltpu.VMEM((nk // tile, group * hd, tile), BF),
            pltpu.VMEM((group, hd, tile), F32),
            pltpu.VMEM((group, 1, tile), F32),
            pltpu.VMEM((group, 1, tile), F32),
        ],
        compiler_params=pltpu.CompilerParams(vmem_limit_bytes=56 << 20),
        cost_estimate=pl.CostEstimate(
            flops=int(pairs * 1024), bytes_accessed=16 << 20, transcendentals=int(pairs)
        ),
        name="attention_forward",
    )(ids, place, ids.reshape(1, -1), col, qt, kt, vt)


def attention_backward(ids, col, place, qt, kt, vt, near, far, ot, lse, scale_vec, hd, tile, at):
    nq, nk = qt.shape[1], kt.shape[1]
    group = HEADS_AT_ONCE
    size = group * hd
    common, halves, rows = attention_specs(nq, nk, hd, group, at)
    grads = pl.BlockSpec((size, nq // 2), lambda i: (i + at, 0))
    pairs = group * nq * nk * 0.6
    return pl.pallas_call(
        functools.partial(backward_kernel, hd, tile),
        grid=(1,),
        in_specs=[
            *common, grads, grads, halves, rows, pl.BlockSpec((size, 1), lambda i: (i + at, 0))
        ],
        out_specs=[
            pl.BlockSpec((size, nq), lambda i: (0, 0)),
            pl.BlockSpec((2 * size, nk), lambda i: (0, 0)),
            pl.BlockSpec((size, 1), lambda i: (0, 0)),
        ],
        out_shape=[
            jax.ShapeDtypeStruct((size, nq), BF),
            jax.ShapeDtypeStruct((2 * size, nk), BF),
            jax.ShapeDtypeStruct((size, 1), F32),
        ],
        scratch_shapes=[
            pltpu.VMEM((group, nk // tile, tile, hd), BF),
            pltpu.VMEM((group, nk // tile, tile, hd), BF),
            pltpu.VMEM((nk // tile, size, tile), BF),
            pltpu.VMEM((size, tile), F32),
            pltpu.VMEM((nk // tile, size, tile), F32),
            pltpu.VMEM((nk // tile, size, tile), F32),
            pltpu.VMEM((nq // tile, group, 1, tile), F32),
            pltpu.VMEM((nq // tile, size, tile), BF),
        ],
        compiler_params=pltpu.CompilerParams(vmem_limit_bytes=60 << 20),
        cost_estimate=pl.CostEstimate(
            flops=int(pairs * 2560), bytes_accessed=16 << 20, transcendentals=int(pairs)
        ),
        name="attention_backward",
    )(ids, place, ids.reshape(1, -1), col, qt, kt, vt, near, far, ot, lse, scale_vec)


def weight_kernel(size, nq, rows, at_ref, xt_ref, dqt_ref, dkvt_ref, *out_refs):
    for m, ref in enumerate(out_refs):
        own = pl.ds(pl.multiple_of(at_ref[m] * rows, rows), rows)
        x = xt_ref[own, :]
        ref[:, : 2 * size] = nt(x, dkvt_ref[...]).astype(BF)
        ref[:, 2 * size :] = nt(x[:, :nq], dqt_ref[...]).astype(BF)


def weight_gradient(xt, dqt, dkvt, at, pieces):
    width, nk = xt.shape
    size, nq = dqt.shape
    rows = width // pieces
    return pl.pallas_call(
        functools.partial(weight_kernel, size, nq, rows),
        in_specs=[
            pl.BlockSpec(memory_space=pltpu.SMEM),
            *[pl.BlockSpec(memory_space=pltpu.VMEM)] * 3,
        ],
        out_specs=[pl.BlockSpec(memory_space=pltpu.VMEM)] * pieces,
        out_shape=[jax.ShapeDtypeStruct((rows, 3 * size), BF)] * pieces,
        compiler_params=pltpu.CompilerParams(vmem_limit_bytes=40 << 20),
        cost_estimate=pl.CostEstimate(
            flops=2 * width * size * (2 * nk + nq), bytes_accessed=12 << 20, transcendentals=0
        ),
        name="weight_gradient",
    )(at, xt, dqt, dkvt)


def dx_kernel(part, queries, n, core_ref, *refs):
    dka, dkb, wk_ref, wv_ref, gain_ref = refs[:5]
    x_refs = refs[5 : 5 + n]
    rest = refs[5 + n :]
    if queries:
        dqa, dqb, wq_ref = rest[:3]
        rest = rest[3:]
    dx_ref, gg_ref, g_ref, xs = rest
    i = pl.program_id(0)
    size = part // 2
    width = dx_ref.shape[1]
    tile = dx_ref.shape[0]
    step = width // 5
    dk = jnp.concatenate([dka[:size, :], dkb[:size, :]], 0).T
    dv = jnp.concatenate([dka[size:, :], dkb[size:, :]], 0).T
    if queries:
        dq = jnp.concatenate([dqa[...], dqb[...]], 0).T
    for c in range(5):
        cols = slice(c * step, (c + 1) * step)
        g = nt(dk, wk_ref[cols, :]) + nt(dv, wv_ref[cols, :])
        if queries:
            g = g + nt(dq, wq_ref[cols, :])
        g_ref[:, cols] = g

    @pl.when(i == 0)
    def _():
        gg_ref[...] = jnp.zeros(gg_ref.shape, F32)

    per_slot = x_refs[0].shape[0] // tile
    for s in range(n):

        @pl.when(i // per_slot == s)
        def _(s=s):
            xs[...] = x_refs[s][pl.ds(pl.multiple_of((i % per_slot) * tile, tile), tile), :]

    x = xs[...].astype(F32)
    inverse = lax.rsqrt(jnp.mean(x * x, -1, keepdims=True) + EPSILON)
    normed = x * inverse
    g = g_ref[...]
    gn = g * normed
    gg_ref[...] += jnp.sum(gn, 0, keepdims=True)
    scaled = g * gain_ref[...]
    mean = jnp.mean(gn * gain_ref[...], -1, keepdims=True)
    dx_ref[...] = (inverse * (scaled - normed * mean)).astype(BF)


def input_gradient(dkvs, dqs, w_full, slots, first_slot, core, gain):
    part = dkvs[0].shape[0]
    size = part // 2
    n = len(slots)
    rows, width = slots[0].shape
    tile = 256
    first = first_slot * rows // tile
    once = pl.Buffered(1)
    dkv = pl.BlockSpec((part, tile), lambda i, c: (0, i + first))
    dq = pl.BlockSpec((size, tile), lambda i, c: (0, i))

    def weight(j):
        return pl.BlockSpec(
            (width, part), lambda i, c, j=j: (0, 2 * j + c[0]), pipeline_mode=once
        )

    specs = [
        dkv, dkv, weight(1), weight(2), pl.BlockSpec((1, width), lambda i, c: (0, 0)),
        *[pl.BlockSpec((rows, width), lambda i, c: (0, 0), pipeline_mode=once)] * n,
    ]
    operands = [*dkvs, w_full, w_full, gain, *slots]
    if dqs:
        specs += [dq, dq, weight(0)]
        operands += [*dqs, w_full]
    return pl.pallas_call(
        functools.partial(dx_kernel, part, bool(dqs), n),
        grid_spec=pltpu.PrefetchScalarGridSpec(
            num_scalar_prefetch=1,
            grid=(n * rows // tile,),
            in_specs=specs,
            out_specs=[
                pl.BlockSpec((tile, width), lambda i, c: (i, 0)),
                pl.BlockSpec((1, width), lambda i, c: (0, 0)),
            ],
            scratch_shapes=[pltpu.VMEM((tile, width), F32), pltpu.VMEM((tile, width), BF)],
        ),
        out_shape=[
            jax.ShapeDtypeStruct((n * rows, width), BF),
            jax.ShapeDtypeStruct((1, width), F32),
        ],
        compiler_params=pltpu.CompilerParams(vmem_limit_bytes=48 << 20),
        cost_estimate=pl.CostEstimate(
            flops=2 * width * n * rows * part * (3 if dqs else 2),
            bytes_accessed=12 << 20,
            transcendentals=0,
        ),
        name="input_gradient",
    )(core, *operands)


class Plan:
    def __init__(self, dp, ctx):
        self.dp, self.ctx = dp, ctx
        self.half = ctx // 2

    def index(self, pair, core, z):
        return (pair * 2 + core) * self.ctx + z

    def perm(self, to):
        out = []
        for d in range(self.dp):
            for z in range(self.ctx):
                got = to(d // 2, d % 2, z)
                if got is not None:
                    out.append((self.index(d // 2, d % 2, z), self.index(*got)))
        return out

    def home(self, core, z):
        return core == z // self.half

    def turned(self, z, k):
        first = z // self.half * self.half
        return first + (z - first + k) % self.half

    def core_swap(self):
        return self.perm(lambda p, c, z: (p, 1 - c, z))

    def pair_swap(self, mask):
        return self.perm(lambda p, c, z: (p ^ mask, c, z))

    def z_turn(self, k):
        return self.perm(lambda p, c, z: (p, c, (z + k) % self.ctx))

    def line_in(self, s):
        last = self.ctx - 1
        to = {s: s + 1, last - s: last - s - 1}
        return self.perm(lambda p, c, z: (p, c, to[z]) if z in to else None)

    def line_out(self, s):
        last = self.ctx - 1
        to = {s + 1: s, last - s - 1: last - s}
        return self.perm(lambda p, c, z: (p, c, to[z]) if z in to else None)

    def line_middle(self):
        to = {self.half - 1: self.half, self.half: self.half - 1}
        return self.perm(lambda p, c, z: (p, c, to[z]) if z in to else None)

    def mirror(self):
        return self.perm(
            lambda p, c, z: (p, c, z) if self.home(c, z) else (p, 1 - c, self.ctx - 1 - z)
        )

    def mirror_or_turn(self, k):
        return self.perm(
            lambda p, c, z: (p, c, self.turned(z, k))
            if self.home(c, z)
            else (p, 1 - c, self.ctx - 1 - z)
        )

    def turn(self, k, away_only):
        return self.perm(
            lambda p, c, z: None
            if away_only and self.home(c, z)
            else (p, c, self.turned(z, k))
        )

    def shard(self, core, z, k, mine):
        chip = self.turned(z, -k)
        at_home = self.home(core, z) if mine else not self.home(core, z)
        return chip if at_home else self.ctx - 1 - chip

    def places(self):
        table = np.zeros((self.dp, self.ctx, 4 * self.ctx), np.int32)
        for d in range(self.dp):
            for z in range(self.ctx):
                slots = [
                    self.shard(d % 2, z, k, mine) for k in range(self.half) for mine in (True, False)
                ]
                stretches = [s for shard in slots for s in (shard, 2 * self.ctx - 1 - shard)]
                for block, stretch in enumerate(stretches):
                    table[d, z, stretch] = block
                    table[d, z, 2 * self.ctx + block] = stretch
        return table.reshape(self.dp * self.ctx, 4 * self.ctx)


def send(value, pairs):
    return lax.ppermute(value, AXES, pairs)


def tie(*values):
    return lax.optimization_barrier(values)


def line_inward(value, plan, kind):
    total = value.astype(F32)
    for s in range(plan.half - 1):
        total = total + send(total.astype(kind), plan.line_in(s)).astype(F32)
    return total.astype(kind)


def line_across(sent, plan, kind):
    return (sent.astype(F32) + send(sent, plan.line_middle()).astype(F32)).astype(kind)


def line_outward(total, plan, z):
    for s in reversed(range(plan.half - 1)):
        back = send(total, plan.line_out(s))
        total = jnp.where((z == s) | (z == plan.ctx - 1 - s), back, total)
    return total


def body(
    tokens_in, block_ids, w_qkv, w_out, w_in, w_down, gain_attn, gain_mlp, bias_in, bias_down,
    query_scale, cotangent,
):
    n = lax.axis_size("ctx")
    plan = Plan(lax.axis_size("dp"), n)
    half = plan.half
    z = lax.axis_index("ctx")
    core = lax.axis_index("dp") % 2
    pair = lax.axis_index("dp") // 2
    pairs = plan.dp // 2
    home = core == z // half
    rows = tokens_in.shape[1]
    width = tokens_in.shape[2]
    hd = query_scale.shape[0]
    heads = width // hd
    part = width // 2
    tile = rows // 2
    wrows = w_qkv.shape[0]
    core_swap = plan.core_swap()

    own = tokens_in[0]
    first = send(own, plan.mirror_or_turn(1))
    token0 = jnp.where(home, own, first)
    second = send(token0, plan.turn(1, True))
    mine = [token0, jnp.where(home, first, second)]
    for k in range(2, half):
        mine.append(send(token0, plan.turn(k, False)))
    theirs = [send(m, core_swap) for m in mine]
    slots = [a for both in zip(mine, theirs) for a in both]

    full_qkv = lax.all_gather(w_qkv, "dp", axis=0, tiled=True)
    at = jnp.stack([pair ^ mask for mask in range(pairs)]).astype(jnp.int32)
    core_at = core.astype(jnp.int32).reshape(1)

    ids = jnp.where(home, block_ids[0], send(block_ids[0], core_swap))
    place = lax.dynamic_index_in_dim(
        jnp.asarray(plan.places()), lax.axis_index("dp") * n + z, 0, False
    )
    col = ids.reshape(-1, 1)

    gain_one = gain_attn.astype(F32)
    gain_two = gain_mlp.astype(F32)
    scale_exp = jnp.exp(query_scale.astype(F32))
    scale_dim = SOFT_FACTOR / math.sqrt(hd) * jnp.log1p(scale_exp)
    scale_vec = jnp.tile(scale_dim, heads // 2)[:, None]
    weights = lax.all_gather(
        jnp.concatenate([w_down, w_in, w_out], 1), "dp", axis=0, tiled=True
    )
    qt, kt, vt, xt = project(
        slots, full_qkv, core_at, gain_one.reshape(1, -1), scale_vec * LOG2E
    )
    grad_low = send(tie(cotangent[0], slots[-1])[0], plan.mirror())
    ot, lse = attention_forward(ids, col, place, qt, kt, vt, hd, tile)
    ot, grad_low = tie(ot, grad_low)
    o_got = send(ot[1], core_swap)

    (
        output, to_keep, to_give, grad_middle, hidden_t, normed_t, grad_pre, grad_mid_low,
        grad_gain_two, grad_bin, grad_bdown,
    ) = mlp(
        ot, o_got, weights, token0, grad_low, core_at, gain_two.reshape(1, -1),
        bias_in.astype(F32).reshape(1, -1), bias_down.astype(F32).reshape(1, -1),
    )
    far = send(to_give, core_swap)
    output = send(output, plan.mirror())
    joined = mlp_weights(ot, o_got, hidden_t, normed_t, grad_low, grad_pre, grad_mid_low, core_at)
    early_qt, joined, far = tie(qt, joined, far)
    scattered = lax.psum_scatter(joined, "dp", scatter_dimension=0, tiled=True)

    def backward(at_group, queries):
        return attention_backward(
            ids, col, place, queries, kt, vt, to_keep, far, ot, lse, scale_vec, hd, tile, at_group
        )

    def to_owners(grads):
        return [send(grads[m], plan.pair_swap(m)) for m in range(1, pairs)]

    def add_up(grads, came):
        total = grads[0].astype(F32)
        for one in came:
            total = total + one.astype(F32)
        return total

    dq_a, dkv_a, gs_a = backward(0, early_qt)
    grads_a = weight_gradient(xt, dq_a, dkv_a, at, pairs)
    later_qt, *grads_a = tie(qt, *grads_a)
    came_a = to_owners(grads_a)
    dq_b, dkv_b, gs_b = backward(1, later_qt)
    dq_b, output, scattered, *came_a = tie(dq_b, output, scattered, *came_a)
    grads_b = weight_gradient(xt, dq_b, dkv_b, at, pairs)
    line_a = line_inward(add_up(grads_a, came_a), plan, BF)
    dkv_b, line_a, *grads_b = tie(dkv_b, line_a, *grads_b)
    came_b = to_owners(grads_b)
    line_a = line_across(line_a, plan, BF)
    others = lax.psum(scattered, "ctx")

    gain_row = gain_one.reshape(1, -1)
    late_dx, gain_late = input_gradient(
        (dkv_a, dkv_b), (), full_qkv, slots[2:], 2, core_at, gain_row
    )
    late_got = [
        send(late_dx[(2 * k + 1) * rows : (2 * k + 2) * rows], core_swap) for k in range(half - 1)
    ]
    dkv_a, late_dx = tie(dkv_a, late_dx)
    dx, gain_early = input_gradient(
        (dkv_a, dkv_b), (dq_a, dq_b), full_qkv, slots[:2], 0, core_at, gain_row
    )
    dx, line_a, *came = tie(dx, line_a, *late_got, *came_b)
    late_got, came_b = came[: half - 1], came[half - 1 :]
    sums = [
        late_dx[2 * k * rows : (2 * k + 1) * rows].astype(F32) + late_got[k].astype(F32)
        for k in range(half - 1)
    ]
    near_sum = sums[0].astype(BF)
    turned = send(near_sum, plan.turn(-1, True))
    got = send(dx[rows:], core_swap)
    others_in = [send(sums[k].astype(BF), plan.turn(-k - 1, False)) for k in range(1, half - 1)]
    line_a = line_outward(line_a, plan, z)
    line_b = line_inward(add_up(grads_b, came_b), plan, BF)
    turned, got, line_a, line_b, others, *others_in = tie(
        turned, got, line_a, line_b, others, *others_in
    )
    total = dx[:rows].astype(F32) + got.astype(F32) + grad_middle
    for one in others_in:
        total = total + one.astype(F32)
    passed = jnp.where(home, near_sum, (total + turned.astype(F32)).astype(BF))
    last = send(passed, plan.mirror_or_turn(-1))
    line_b = line_across(line_b, plan, BF)

    def owned_rows(value):
        keep = lax.dynamic_slice_in_dim(value, core * wrows, wrows, 0)
        give = lax.dynamic_slice_in_dim(value, (1 - core) * wrows, wrows, 0)
        came = send(give, core_swap)
        return jnp.where(core == 0, keep, came), jnp.where(core == 0, came, keep)

    swapped_a = owned_rows(line_a)
    last, line_b = tie(last, line_b)
    grad_tokens = jnp.where(home, total + last.astype(F32), last.astype(F32))
    swapped = (swapped_a, owned_rows(line_outward(line_b, plan, z)))
    size = part // 2
    owned_qkv = jnp.concatenate(
        [
            swapped[g][c][:, which * size : (which + 1) * size]
            for which in (2, 0, 1)
            for c in range(2)
            for g in range(2)
        ],
        1,
    ).astype(F32)
    others = others.astype(F32)

    scale_slope = SOFT_FACTOR / math.sqrt(hd) * scale_exp / (1.0 + scale_exp)
    grad_scale = jnp.sum(jnp.concatenate([gs_a, gs_b], 0).reshape(heads // 2, hd), 0)
    grad_scale = grad_scale * scale_slope / (scale_dim * LOG2E)
    small = jnp.concatenate(
        [
            *(v.reshape(-1) for v in (gain_late + gain_early, grad_gain_two, grad_bin, grad_bdown)),
            grad_scale,
        ]
    )
    small_size = small.shape[0]
    small = jnp.pad(small, (0, -small_size % 1024)).reshape(-1, 128)
    small = small + send(small, core_swap)
    mask = 1
    while mask < pairs:
        small = small + send(small, plan.pair_swap(mask))
        mask *= 2
    small = line_across(line_inward(small, plan, F32), plan, F32)
    small = line_outward(small, plan, z).reshape(-1)
    return (
        output[None],
        grad_tokens[None],
        owned_qkv,
        others[:, 2 * width :],
        others[:, width : 2 * width],
        others[:, :width],
        small[:width],
        small[width : 2 * width],
        small[2 * width : 3 * width],
        small[3 * width : 4 * width],
        small[4 * width : small_size],
    )


def solution(mesh):
    split = P("dp", "ctx", None)
    weight = P("dp", None)
    return jax.shard_map(
        body,
        mesh=mesh,
        in_specs=(split, weight, weight, weight, weight, weight, P(), P(), P(), P(), P(), split),
        out_specs=(split, split, weight, weight, weight, weight, P(), P(), P(), P(), P()),
        check_vma=False,
    )
```

```python
import functools
import math

import jax
import jax.numpy as jnp
import numpy as np
from jax import lax
from jax.experimental import pallas as pl
from jax.experimental.pallas import tpu as pltpu
from jax.sharding import PartitionSpec as P

EPSILON = 1e-06
SOFT_FACTOR = 1.442695041
LOG2E = 1.4426950408889634
MASKED = -1e30
HEADS_AT_ONCE = 4
COST = 1.0
AXES = ("dp", "ctx")
BF = jnp.bfloat16
F32 = jnp.float32


def nn(a, b):
    return lax.dot_general(a, b, (((1,), (0,)), ((), ())), preferred_element_type=F32)


def nt(a, b):
    return lax.dot_general(a, b, (((1,), (1,)), ((), ())), preferred_element_type=F32)


def tile_counts(ids_ref, stretch, tile, tiles):
    low = ids_ref[stretch * tile]
    high = ids_ref[stretch * tile + tile - 1]
    full = jnp.int32(0)
    need = jnp.int32(0)
    for t in range(tiles):
        full += (ids_ref[t * tile + tile - 1] <= low).astype(jnp.int32)
        need += (ids_ref[t * tile] <= high).astype(jnp.int32)
    return full, need


def project_kernel(part, query_slots, n, core_ref, gain_ref, scale_ref, *refs):
    x_refs, w_refs = refs[:n], refs[n : n + 3]
    qt_ref, kt_ref, vt_ref, xt_ref, wt, xs = refs[n + 3 :]
    i = pl.program_id(0)

    @pl.when(i == 0)
    def _():
        for j, ref in enumerate(w_refs):
            wt[j * part : (j + 1) * part, :] = ref[...].T

    for s in range(n):

        @pl.when(i == s)
        def _(s=s):
            xs[...] = x_refs[s][...]

    x = xs[...].astype(F32)
    inverse = lax.rsqrt(jnp.mean(x * x, -1, keepdims=True) + EPSILON)
    xt_ref[...] = (x * inverse * gain_ref[...]).astype(BF).T
    kt_ref[...] = nn(wt[part : 2 * part, :], xt_ref[...]).astype(BF)
    vt_ref[...] = nn(wt[2 * part :, :], xt_ref[...]).astype(BF)

    @pl.when(i < query_slots)
    def _():
        qt_ref[...] = (nn(wt[:part, :], xt_ref[...]) * scale_ref[...]).astype(BF)


def project(slots, w_full, core, gain, scale):
    n = len(slots)
    rows, width = slots[0].shape
    part = width // 2
    query_slots = 2
    once = pl.Buffered(1)
    return pl.pallas_call(
        functools.partial(project_kernel, part, query_slots, n),
        grid_spec=pltpu.PrefetchScalarGridSpec(
            num_scalar_prefetch=1,
            grid=(n,),
            in_specs=[
                pl.BlockSpec((1, width), lambda i, c: (0, 0)),
                pl.BlockSpec((part, 1), lambda i, c: (0, 0)),
                *[pl.BlockSpec((rows, width), lambda i, c: (0, 0), pipeline_mode=once)] * n,
                *[
                    pl.BlockSpec(
                        (width, part), lambda i, c, j=j: (0, 2 * j + c[0]), pipeline_mode=once
                    )
                    for j in range(3)
                ],
            ],
            out_specs=[
                pl.BlockSpec((part, rows), lambda i, c: (0, jnp.minimum(i, query_slots - 1))),
                pl.BlockSpec((part, rows), lambda i, c: (0, i)),
                pl.BlockSpec((part, rows), lambda i, c: (0, i)),
                pl.BlockSpec((width, rows), lambda i, c: (0, i)),
            ],
            scratch_shapes=[pltpu.VMEM((3 * part, width), BF), pltpu.VMEM((rows, width), BF)],
        ),
        out_shape=[
            jax.ShapeDtypeStruct((part, query_slots * rows), BF),
            jax.ShapeDtypeStruct((part, n * rows), BF),
            jax.ShapeDtypeStruct((part, n * rows), BF),
            jax.ShapeDtypeStruct((width, n * rows), BF),
        ],
        compiler_params=pltpu.CompilerParams(vmem_limit_bytes=60 << 20),
        cost_estimate=pl.CostEstimate(
            flops=int(COST * 2 * width * part * rows * (2 * n + query_slots)),
            bytes_accessed=1 << 16,
            transcendentals=0,
        ),
        name="project",
    )(core, gain, scale, *slots, *[w_full] * 3)


def mlp_kernel(
    part, core_ref, near_ref, far_ref, w_ref, x_ref, cot_ref, gain_ref, bin_ref, bdown_ref,
    out_ref, keep_ref, give_ref, gmid_ref, ht_ref, nt_ref, gpre_ref, gml_ref, gain_out, bin_out,
    bdown_out, middle, normed, hidden, slope, g_ref,
):
    width = x_ref.shape[1]
    step = width // 5
    chunks = [slice(c * step, (c + 1) * step) for c in range(5)]
    down, inner = 0, width
    outer = 2 * width
    core = core_ref[0]
    near_rows = pl.ds(pl.multiple_of(core * part, part), part)
    far_rows = pl.ds(pl.multiple_of((1 - core) * part, part), part)

    @pl.when(pl.program_id(0) == 0)
    def _():
        for ref in (gain_out, bin_out, bdown_out):
            ref[...] = jnp.zeros(ref.shape, F32)

    near, far = near_ref[0].T, far_ref[...].T
    for cols in chunks:
        at = slice(outer + cols.start, outer + cols.stop)
        middle[:, cols] = (
            x_ref[:, cols].astype(F32) + nn(near, w_ref[near_rows, at]) + nn(far, w_ref[far_rows, at])
        )
    mid = middle[...]
    inverse = lax.rsqrt(jnp.mean(mid * mid, -1, keepdims=True) + EPSILON)
    normed[...] = (mid * inverse * gain_ref[...]).astype(BF)
    nt_ref[...] = normed[...].T
    for cols in chunks:
        at = slice(inner + cols.start, inner + cols.stop)
        pre = nn(normed[...], w_ref[:, at]) + bin_ref[:, cols]
        sigma = 1.0 / (1.0 + jnp.exp(-pre))
        hidden[:, cols] = (pre * sigma).astype(BF)
        slope[:, cols] = sigma * (1.0 + pre * (1.0 - sigma))
    ht_ref[...] = hidden[...].T
    for cols in chunks:
        at = slice(down + cols.start, down + cols.stop)
        out_ref[:, cols] = (
            middle[:, cols] + nn(hidden[...], w_ref[:, at]) + bdown_ref[:, cols]
        ).astype(BF)
    for cols in chunks:
        gpre_ref[:, cols] = (
            nt(cot_ref[...], w_ref[cols, down : down + width]) * slope[:, cols]
        ).astype(BF)
    for cols in chunks:
        g_ref[:, cols] = nt(gpre_ref[...], w_ref[cols, inner : inner + width])
    bin_out[...] += jnp.sum(gpre_ref[...].astype(F32), 0, keepdims=True)
    cot = cot_ref[...].astype(F32)
    bdown_out[...] += jnp.sum(cot, 0, keepdims=True)
    turned = middle[...] * inverse
    gn = g_ref[...] * turned
    gain_out[...] += jnp.sum(gn, 0, keepdims=True)
    mean = jnp.mean(gn * gain_ref[...], -1, keepdims=True)
    gmid = cot + inverse * (g_ref[...] * gain_ref[...] - turned * mean)
    gmid_ref[...] = gmid
    gml_ref[...] = gmid.astype(BF)
    low = gml_ref[...]
    keep_ref[...] = nt(w_ref[near_rows, outer : outer + width], low).astype(BF)
    give_ref[...] = nt(w_ref[far_rows, outer : outer + width], low).astype(BF)


def mlp(halves, far, weights, x, cot, core, gain, bias_in, bias_down):
    part, rows = far.shape
    width = x.shape[1]
    tile = 256
    once = pl.Buffered(1)
    row = pl.BlockSpec((tile, width), lambda i, c: (i, 0))
    feature = pl.BlockSpec((part, tile), lambda i, c: (0, i))
    wide = pl.BlockSpec((width, tile), lambda i, c: (0, i))
    vector = pl.BlockSpec((1, width), lambda i, c: (0, 0))
    return pl.pallas_call(
        functools.partial(mlp_kernel, part),
        grid_spec=pltpu.PrefetchScalarGridSpec(
            num_scalar_prefetch=1,
            grid=(rows // tile,),
            in_specs=[
                pl.BlockSpec((1, part, tile), lambda i, c: (0, 0, i)),
                feature,
                pl.BlockSpec(weights.shape, lambda i, c: (0, 0), pipeline_mode=once),
                row, row, vector, vector, vector,
            ],
            out_specs=[
                row, feature, feature, row, wide, wide, row, row, vector, vector, vector
            ],
            scratch_shapes=[
                pltpu.VMEM((tile, width), F32),
                pltpu.VMEM((tile, width), BF),
                pltpu.VMEM((tile, width), BF),
                pltpu.VMEM((tile, width), F32),
                pltpu.VMEM((tile, width), F32),
            ],
        ),
        out_shape=[
            jax.ShapeDtypeStruct((rows, width), BF),
            jax.ShapeDtypeStruct((part, rows), BF),
            jax.ShapeDtypeStruct((part, rows), BF),
            jax.ShapeDtypeStruct((rows, width), F32),
            jax.ShapeDtypeStruct((width, rows), BF),
            jax.ShapeDtypeStruct((width, rows), BF),
            jax.ShapeDtypeStruct((rows, width), BF),
            jax.ShapeDtypeStruct((rows, width), BF),
            jax.ShapeDtypeStruct((1, width), F32),
            jax.ShapeDtypeStruct((1, width), F32),
            jax.ShapeDtypeStruct((1, width), F32),
        ],
        compiler_params=pltpu.CompilerParams(vmem_limit_bytes=56 << 20),
        cost_estimate=pl.CostEstimate(
            flops=int(COST * 12 * rows * width * width), bytes_accessed=1 << 16, transcendentals=0
        ),
        name="mlp",
    )(core, halves, far, weights, x, cot, gain, bias_in, bias_down)


def mlp_weight_kernel(part, core_ref, near_ref, far_ref, ht_ref, nt_ref, cot_ref, gpre_ref, gml_ref, out_ref):
    width = ht_ref.shape[0]
    core = core_ref[0]

    def half(i, carry):
        own = pl.ds(pl.multiple_of(i * part, part), part)
        out_ref[own, :width] = nn(ht_ref[own, :], cot_ref[...]).astype(BF)
        out_ref[own, width : 2 * width] = nn(nt_ref[own, :], gpre_ref[...]).astype(BF)
        return carry

    lax.fori_loop(0, 2, half, 0)
    near_rows = pl.ds(pl.multiple_of(core * part, part), part)
    far_rows = pl.ds(pl.multiple_of((1 - core) * part, part), part)
    out_ref[near_rows, 2 * width :] = nn(near_ref[0], gml_ref[...]).astype(BF)
    out_ref[far_rows, 2 * width :] = nn(far_ref[...], gml_ref[...]).astype(BF)


def mlp_weights(halves, far, ht, nrt, cot, gpre, gml, core):
    part, rows = far.shape
    width = cot.shape[1]
    whole = pl.BlockSpec(memory_space=pltpu.VMEM)
    return pl.pallas_call(
        functools.partial(mlp_weight_kernel, part),
        grid=(1,),
        in_specs=[
            pl.BlockSpec(memory_space=pltpu.SMEM),
            pl.BlockSpec((1, part, rows), lambda i: (0, 0, 0)),
            *[whole] * 6,
        ],
        out_specs=whole,
        out_shape=jax.ShapeDtypeStruct((width, 3 * width), BF),
        compiler_params=pltpu.CompilerParams(vmem_limit_bytes=48 << 20),
        cost_estimate=pl.CostEstimate(
            flops=int(COST * 6 * rows * width * width), bytes_accessed=1 << 16, transcendentals=0
        ),
        name="mlp_weights",
    )(core, halves, far, ht, nrt, cot, gpre, gml)


def load_keys(ref, place_ref, hd, tile, group, knat, kt=None):
    tiles = ref.shape[1] // tile
    for b in range(tiles):
        stretch = place_ref[tiles + b]
        piece = ref[:, b * tile : (b + 1) * tile]
        if kt is not None:
            kt[stretch] = piece
        if knat is not None:
            for h in range(group):
                knat[h, stretch] = piece[h * hd : (h + 1) * hd, :].T


def forward_kernel(
    hd, tile, ids_ref, place_ref, row_ref, col_ref, qt_ref, kt_ref, vt_ref, ot_ref, lse_ref,
    knat, vt, acc, m_ref, l_ref,
):
    group = qt_ref.shape[0] // hd
    tiles = vt.shape[0]
    load_keys(kt_ref, place_ref, hd, tile, group, knat)
    load_keys(vt_ref, place_ref, hd, tile, group, None, vt)
    per_half = ot_ref.shape[2] // tile

    def one_tile(qi, carry):
        stretch = place_ref[tiles + qi]
        full, need = tile_counts(ids_ref, stretch, tile, tiles)
        qcol = pl.ds(pl.multiple_of(qi * tile, tile), tile)
        qpos = pl.ds(pl.multiple_of(stretch * tile, tile), tile)
        m_ref[...] = jnp.full(m_ref.shape, MASKED, F32)
        l_ref[...] = jnp.zeros(l_ref.shape, F32)
        acc[...] = jnp.zeros(acc.shape, F32)

        def step(t, masked):
            if masked:
                kpos = pl.ds(pl.multiple_of(t * tile, tile), tile)
                allowed = col_ref[kpos, :] <= row_ref[:, qpos]
            scores = [nn(knat[h, t], qt_ref[h * hd : (h + 1) * hd, qcol]) for h in range(group)]
            for h in range(group):
                s = scores[h]
                if masked:
                    s = jnp.where(allowed, s, MASKED)
                old = m_ref[h]
                new = jnp.maximum(old, jnp.max(s, 0, keepdims=True))
                p = jnp.exp2(s - new)
                alpha = jnp.exp2(old - new)
                l_ref[h] = l_ref[h] * alpha + jnp.sum(p, 0, keepdims=True)
                m_ref[h] = new
                acc[h] = acc[h] * alpha + nn(vt[t, h * hd : (h + 1) * hd, :], p.astype(BF))

        def full_step(t, c):
            step(t, False)
            return c

        def mask_step(t, c):
            step(t, True)
            return c

        lax.fori_loop(0, full, full_step, 0)
        lax.fori_loop(full, need, mask_step, 0)
        for h in range(group):
            inner = pl.ds(pl.multiple_of((qi % per_half) * tile, tile), tile)
            ot_ref[qi // per_half, h * hd : (h + 1) * hd, inner] = (acc[h] / l_ref[h]).astype(BF)
            lse_ref[h, :, qcol] = m_ref[h] + jnp.log2(l_ref[h])
        return carry

    lax.fori_loop(0, qt_ref.shape[1] // tile, one_tile, 0)


def backward_kernel(
    hd, tile, ids_ref, place_ref, row_ref, col_ref, qt_ref, kt_ref, vt_ref, near_ref, far_ref,
    ot_ref, lse_ref, scale_ref, dqt_ref, dkvt_ref, gs_ref, knat, vnat, kt, dq, dk, dv, delta, dot,
):
    group = qt_ref.shape[0] // hd
    tiles = kt.shape[0]
    load_keys(kt_ref, place_ref, hd, tile, group, knat, kt)
    load_keys(vt_ref, place_ref, hd, tile, group, vnat)
    per_half = near_ref.shape[1] // tile
    for half, ref in enumerate((near_ref, far_ref)):
        for b in range(per_half):
            cols = slice(b * tile, (b + 1) * tile)
            dot[half * per_half + b] = ref[:, cols]
            product = ref[:, cols].astype(F32) * ot_ref[half, :, cols].astype(F32)
            for h in range(group):
                delta[half * per_half + b, h] = jnp.sum(
                    product[h * hd : (h + 1) * hd], 0, keepdims=True
                )
    dk[...] = jnp.zeros(dk.shape, F32)
    dv[...] = jnp.zeros(dv.shape, F32)
    gs_ref[...] = jnp.zeros(gs_ref.shape, F32)

    def one_tile(qi, carry):
        stretch = place_ref[tiles + qi]
        full, need = tile_counts(ids_ref, stretch, tile, tiles)
        qcol = pl.ds(pl.multiple_of(qi * tile, tile), tile)
        qpos = pl.ds(pl.multiple_of(stretch * tile, tile), tile)
        dq[...] = jnp.zeros(dq.shape, F32)

        def step(t, masked):
            if masked:
                kpos = pl.ds(pl.multiple_of(t * tile, tile), tile)
                allowed = col_ref[kpos, :] <= row_ref[:, qpos]
            for h in range(group):
                hs = slice(h * hd, (h + 1) * hd)
                qh, doh = qt_ref[hs, qcol], dot[qi, hs, :]
                s = nn(knat[h, t], qh)
                dp = nn(vnat[h, t], doh)
                if masked:
                    s = jnp.where(allowed, s, MASKED)
                p = jnp.exp2(s - lse_ref[h, :, qcol])
                ds = (p * (dp - delta[qi, h])).astype(BF)
                dv[t, hs, :] += nt(doh, p.astype(BF))
                dk[t, hs, :] += nt(qh, ds)
                dq[hs, :] += nn(kt[t, hs, :], ds)

        def full_step(t, c):
            step(t, False)
            return c

        def mask_step(t, c):
            step(t, True)
            return c

        lax.fori_loop(0, full, full_step, 0)
        lax.fori_loop(full, need, mask_step, 0)
        gs_ref[...] += jnp.sum(dq[...] * qt_ref[:, qcol].astype(F32), 1, keepdims=True)
        dqt_ref[:, qcol] = (dq[...] * scale_ref[...]).astype(BF)
        return carry

    lax.fori_loop(0, qt_ref.shape[1] // tile, one_tile, 0)
    for b in range(tiles):
        stretch = place_ref[tiles + b]
        cols = slice(b * tile, (b + 1) * tile)
        dkvt_ref[: group * hd, cols] = (dk[stretch] * (1.0 / LOG2E)).astype(BF)
        dkvt_ref[group * hd :, cols] = dv[stretch].astype(BF)


def attention_specs(nq, nk, hd, group, at):
    size = group * hd
    return (
        [
            pl.BlockSpec(memory_space=pltpu.SMEM),
            pl.BlockSpec(memory_space=pltpu.SMEM),
            pl.BlockSpec((1, nk), lambda i: (0, 0)),
            pl.BlockSpec((nk, 1), lambda i: (0, 0)),
            pl.BlockSpec((size, nq), lambda i: (i + at, 0)),
            pl.BlockSpec((size, nk), lambda i: (i + at, 0)),
            pl.BlockSpec((size, nk), lambda i: (i + at, 0)),
        ],
        pl.BlockSpec((2, size, nq // 2), lambda i: (0, i + at, 0)),
        pl.BlockSpec((group, 1, nq), lambda i: (i + at, 0, 0)),
    )


def attention_forward(ids, col, place, qt, kt, vt, hd, tile):
    heads = qt.shape[0] // hd
    nq, nk = qt.shape[1], kt.shape[1]
    group = HEADS_AT_ONCE
    common, halves, rows = attention_specs(nq, nk, hd, group, 0)
    pairs = heads * nq * nk * 0.6
    return pl.pallas_call(
        functools.partial(forward_kernel, hd, tile),
        grid=(heads // group,),
        in_specs=common,
        out_specs=[halves, rows],
        out_shape=[
            jax.ShapeDtypeStruct((2, heads * hd, nq // 2), BF),
            jax.ShapeDtypeStruct((heads, 1, nq), F32),
        ],
        scratch_shapes=[
            pltpu.VMEM((group, nk // tile, tile, hd), BF),
            pltpu.VMEM((nk // tile, group * hd, tile), BF),
            pltpu.VMEM((group, hd, tile), F32),
            pltpu.VMEM((group, 1, tile), F32),
            pltpu.VMEM((group, 1, tile), F32),
        ],
        compiler_params=pltpu.CompilerParams(vmem_limit_bytes=56 << 20),
        cost_estimate=pl.CostEstimate(
            flops=int(COST * pairs * 1024), bytes_accessed=1 << 16, transcendentals=int(COST * pairs)
        ),
        name="attention_forward",
    )(ids, place, ids.reshape(1, -1), col, qt, kt, vt)


def attention_backward(ids, col, place, qt, kt, vt, near, far, ot, lse, scale_vec, hd, tile, at):
    nq, nk = qt.shape[1], kt.shape[1]
    group = HEADS_AT_ONCE
    size = group * hd
    common, halves, rows = attention_specs(nq, nk, hd, group, at)
    grads = pl.BlockSpec((size, nq // 2), lambda i: (i + at, 0))
    pairs = group * nq * nk * 0.6
    return pl.pallas_call(
        functools.partial(backward_kernel, hd, tile),
        grid=(1,),
        in_specs=[
            *common, grads, grads, halves, rows, pl.BlockSpec((size, 1), lambda i: (i + at, 0))
        ],
        out_specs=[
            pl.BlockSpec((size, nq), lambda i: (0, 0)),
            pl.BlockSpec((2 * size, nk), lambda i: (0, 0)),
            pl.BlockSpec((size, 1), lambda i: (0, 0)),
        ],
        out_shape=[
            jax.ShapeDtypeStruct((size, nq), BF),
            jax.ShapeDtypeStruct((2 * size, nk), BF),
            jax.ShapeDtypeStruct((size, 1), F32),
        ],
        scratch_shapes=[
            pltpu.VMEM((group, nk // tile, tile, hd), BF),
            pltpu.VMEM((group, nk // tile, tile, hd), BF),
            pltpu.VMEM((nk // tile, size, tile), BF),
            pltpu.VMEM((size, tile), F32),
            pltpu.VMEM((nk // tile, size, tile), F32),
            pltpu.VMEM((nk // tile, size, tile), F32),
            pltpu.VMEM((nq // tile, group, 1, tile), F32),
            pltpu.VMEM((nq // tile, size, tile), BF),
        ],
        compiler_params=pltpu.CompilerParams(vmem_limit_bytes=60 << 20),
        cost_estimate=pl.CostEstimate(
            flops=int(COST * pairs * 2560), bytes_accessed=1 << 16, transcendentals=int(COST * pairs)
        ),
        name="attention_backward",
    )(ids, place, ids.reshape(1, -1), col, qt, kt, vt, near, far, ot, lse, scale_vec)


def weight_kernel(size, nq, rows, at_ref, xt_ref, dqt_ref, dkvt_ref, *out_refs):
    for m, ref in enumerate(out_refs):
        own = pl.ds(pl.multiple_of(at_ref[m] * rows, rows), rows)
        x = xt_ref[own, :]
        ref[:, : 2 * size] = nt(x, dkvt_ref[...]).astype(BF)
        ref[:, 2 * size :] = nt(x[:, :nq], dqt_ref[...]).astype(BF)


def weight_gradient(xt, dqt, dkvt, at, pieces):
    width, nk = xt.shape
    size, nq = dqt.shape
    rows = width // pieces
    return pl.pallas_call(
        functools.partial(weight_kernel, size, nq, rows),
        in_specs=[
            pl.BlockSpec(memory_space=pltpu.SMEM),
            *[pl.BlockSpec(memory_space=pltpu.VMEM)] * 3,
        ],
        out_specs=[pl.BlockSpec(memory_space=pltpu.VMEM)] * pieces,
        out_shape=[jax.ShapeDtypeStruct((rows, 3 * size), BF)] * pieces,
        compiler_params=pltpu.CompilerParams(vmem_limit_bytes=40 << 20),
        cost_estimate=pl.CostEstimate(
            flops=int(COST * 2 * width * size * (2 * nk + nq)), bytes_accessed=1 << 16, transcendentals=0
        ),
        name="weight_gradient",
    )(at, xt, dqt, dkvt)


def dx_kernel(part, queries, n, core_ref, *refs):
    dka, dkb, wk_ref, wv_ref, gain_ref = refs[:5]
    x_refs = refs[5 : 5 + n]
    rest = refs[5 + n :]
    if queries:
        dqa, dqb, wq_ref = rest[:3]
        rest = rest[3:]
    dx_ref, gg_ref, g_ref, xs = rest
    i = pl.program_id(0)
    size = part // 2
    width = dx_ref.shape[1]
    tile = dx_ref.shape[0]
    step = width // 5
    dk = jnp.concatenate([dka[:size, :], dkb[:size, :]], 0).T
    dv = jnp.concatenate([dka[size:, :], dkb[size:, :]], 0).T
    if queries:
        dq = jnp.concatenate([dqa[...], dqb[...]], 0).T
    for c in range(5):
        cols = slice(c * step, (c + 1) * step)
        g = nt(dk, wk_ref[cols, :]) + nt(dv, wv_ref[cols, :])
        if queries:
            g = g + nt(dq, wq_ref[cols, :])
        g_ref[:, cols] = g

    @pl.when(i == 0)
    def _():
        gg_ref[...] = jnp.zeros(gg_ref.shape, F32)

    per_slot = x_refs[0].shape[0] // tile
    for s in range(n):

        @pl.when(i // per_slot == s)
        def _(s=s):
            xs[...] = x_refs[s][pl.ds(pl.multiple_of((i % per_slot) * tile, tile), tile), :]

    x = xs[...].astype(F32)
    inverse = lax.rsqrt(jnp.mean(x * x, -1, keepdims=True) + EPSILON)
    normed = x * inverse
    g = g_ref[...]
    gn = g * normed
    gg_ref[...] += jnp.sum(gn, 0, keepdims=True)
    scaled = g * gain_ref[...]
    mean = jnp.mean(gn * gain_ref[...], -1, keepdims=True)
    dx_ref[...] = (inverse * (scaled - normed * mean)).astype(BF)


def input_gradient(dkvs, dqs, w_full, slots, first_slot, core, gain):
    part = dkvs[0].shape[0]
    size = part // 2
    n = len(slots)
    rows, width = slots[0].shape
    tile = 256
    first = first_slot * rows // tile
    once = pl.Buffered(1)
    dkv = pl.BlockSpec((part, tile), lambda i, c: (0, i + first))
    dq = pl.BlockSpec((size, tile), lambda i, c: (0, i))

    def weight(j):
        return pl.BlockSpec(
            (width, part), lambda i, c, j=j: (0, 2 * j + c[0]), pipeline_mode=once
        )

    specs = [
        dkv, dkv, weight(1), weight(2), pl.BlockSpec((1, width), lambda i, c: (0, 0)),
        *[pl.BlockSpec((rows, width), lambda i, c: (0, 0), pipeline_mode=once)] * n,
    ]
    operands = [*dkvs, w_full, w_full, gain, *slots]
    if dqs:
        specs += [dq, dq, weight(0)]
        operands += [*dqs, w_full]
    return pl.pallas_call(
        functools.partial(dx_kernel, part, bool(dqs), n),
        grid_spec=pltpu.PrefetchScalarGridSpec(
            num_scalar_prefetch=1,
            grid=(n * rows // tile,),
            in_specs=specs,
            out_specs=[
                pl.BlockSpec((tile, width), lambda i, c: (i, 0)),
                pl.BlockSpec((1, width), lambda i, c: (0, 0)),
            ],
            scratch_shapes=[pltpu.VMEM((tile, width), F32), pltpu.VMEM((tile, width), BF)],
        ),
        out_shape=[
            jax.ShapeDtypeStruct((n * rows, width), BF),
            jax.ShapeDtypeStruct((1, width), F32),
        ],
        compiler_params=pltpu.CompilerParams(vmem_limit_bytes=48 << 20),
        cost_estimate=pl.CostEstimate(
            flops=int(COST * 2 * width * n * rows * part * (3 if dqs else 2)),
            bytes_accessed=1 << 16,
            transcendentals=0,
        ),
        name="input_gradient",
    )(core, *operands)


class Plan:
    def __init__(self, dp, ctx):
        self.dp, self.ctx = dp, ctx
        self.half = ctx // 2

    def index(self, pair, core, z):
        return (pair * 2 + core) * self.ctx + z

    def perm(self, to):
        out = []
        for d in range(self.dp):
            for z in range(self.ctx):
                got = to(d // 2, d % 2, z)
                if got is not None:
                    out.append((self.index(d // 2, d % 2, z), self.index(*got)))
        return out

    def home(self, core, z):
        return core == z // self.half

    def turned(self, z, k):
        first = z // self.half * self.half
        return first + (z - first + k) % self.half

    def core_swap(self):
        return self.perm(lambda p, c, z: (p, 1 - c, z))

    def pair_swap(self, mask):
        return self.perm(lambda p, c, z: (p ^ mask, c, z))

    def line_swap(self, mask):
        return self.perm(lambda p, c, z: (p, c, z ^ mask))

    def line_in(self, s):
        last = self.ctx - 1
        to = {s: s + 1, last - s: last - s - 1}
        return self.perm(lambda p, c, z: (p, c, to[z]) if z in to else None)

    def line_out(self, s):
        last = self.ctx - 1
        to = {s + 1: s, last - s - 1: last - s}
        return self.perm(lambda p, c, z: (p, c, to[z]) if z in to else None)

    def line_middle(self):
        to = {self.half - 1: self.half, self.half: self.half - 1}
        return self.perm(lambda p, c, z: (p, c, to[z]) if z in to else None)

    def mirror(self):
        return self.perm(
            lambda p, c, z: None if self.home(c, z) else (p, 1 - c, self.ctx - 1 - z)
        )

    def mirror_or_turn(self, k):
        return self.perm(
            lambda p, c, z: (p, c, self.turned(z, k))
            if self.home(c, z)
            else (p, 1 - c, self.ctx - 1 - z)
        )

    def turn(self, k, away_only):
        return self.perm(
            lambda p, c, z: None
            if away_only and self.home(c, z)
            else (p, c, self.turned(z, k))
        )

    def shard(self, core, z, k, mine):
        chip = self.turned(z, -k)
        at_home = self.home(core, z) if mine else not self.home(core, z)
        return chip if at_home else self.ctx - 1 - chip

    def places(self):
        table = np.zeros((self.dp, self.ctx, 4 * self.ctx), np.int32)
        for d in range(self.dp):
            for z in range(self.ctx):
                slots = [
                    self.shard(d % 2, z, k, mine) for k in range(self.half) for mine in (True, False)
                ]
                stretches = [s for shard in slots for s in (shard, 2 * self.ctx - 1 - shard)]
                for block, stretch in enumerate(stretches):
                    table[d, z, stretch] = block
                    table[d, z, 2 * self.ctx + block] = stretch
        return table.reshape(self.dp * self.ctx, 4 * self.ctx)


def send(value, pairs):
    return lax.ppermute(value, AXES, pairs)


def tie(*values):
    return lax.optimization_barrier(values)


def line_inward(value, plan, kind):
    total = value.astype(F32)
    for s in range(plan.half - 2):
        total = total + send(total.astype(kind), plan.line_in(s)).astype(F32)
    if plan.half == 1:
        return total, jnp.zeros_like(total, kind)
    return total, send(total.astype(kind), plan.line_in(plan.half - 2))


def line_across(held, came, plan, kind):
    sent = (held + came.astype(F32)).astype(kind)
    return sent, send(sent, plan.line_middle())


def line_joined(sent, came):
    return (sent.astype(F32) + came.astype(F32)).astype(sent.dtype)


def line_outward(total, plan, z):
    for s in reversed(range(plan.half - 1)):
        back = send(total, plan.line_out(s))
        total = jnp.where((z == s) | (z == plan.ctx - 1 - s), back, total)
    return total


def body(
    tokens_in, block_ids, w_qkv, w_out, w_in, w_down, gain_attn, gain_mlp, bias_in, bias_down,
    query_scale, cotangent,
):
    n = lax.axis_size("ctx")
    plan = Plan(lax.axis_size("dp"), n)
    half = plan.half
    z = lax.axis_index("ctx")
    core = lax.axis_index("dp") % 2
    pair = lax.axis_index("dp") // 2
    pairs = plan.dp // 2
    home = core == z // half
    rows = tokens_in.shape[1]
    width = tokens_in.shape[2]
    hd = query_scale.shape[0]
    heads = width // hd
    part = width // 2
    tile = rows // 2
    wrows = w_qkv.shape[0]
    core_swap = plan.core_swap()

    own = tokens_in[0]
    first = send(own, plan.mirror_or_turn(1))
    token0 = jnp.where(home, own, first)
    second = send(token0, plan.turn(1, True))
    mine = [token0, jnp.where(home, first, second)]
    for k in range(2, half):
        mine.append(send(token0, plan.turn(k, False)))
    theirs = [send(m, core_swap) for m in mine]
    slots = [a for both in zip(mine, theirs) for a in both]

    full_qkv = lax.all_gather(w_qkv, "dp", axis=0, tiled=True)
    at = jnp.stack([pair ^ mask for mask in range(pairs)]).astype(jnp.int32)
    core_at = core.astype(jnp.int32).reshape(1)

    ids = jnp.where(home, block_ids[0], send(block_ids[0], core_swap))
    place = lax.dynamic_index_in_dim(
        jnp.asarray(plan.places()), lax.axis_index("dp") * n + z, 0, False
    )
    col = ids.reshape(-1, 1)

    gain_one = gain_attn.astype(F32)
    gain_two = gain_mlp.astype(F32)
    scale_exp = jnp.exp(query_scale.astype(F32))
    scale_dim = SOFT_FACTOR / math.sqrt(hd) * jnp.log1p(scale_exp)
    scale_vec = jnp.tile(scale_dim, heads // 2)[:, None]
    weights = lax.all_gather(
        jnp.concatenate([w_down, w_in, w_out], 1), "dp", axis=0, tiled=True
    )
    qt, kt, vt, xt = project(
        slots, full_qkv, core_at, gain_one.reshape(1, -1), scale_vec * LOG2E
    )
    grad_low = send(tie(cotangent[0], slots[-1])[0], plan.mirror())
    ot, lse = attention_forward(ids, col, place, qt, kt, vt, hd, tile)
    ot, grad_low = tie(ot, grad_low)
    grad_low = jnp.where(home, cotangent[0], grad_low)
    o_got = send(ot[1], core_swap)

    (
        output, to_keep, to_give, grad_middle, hidden_t, normed_t, grad_pre, grad_mid_low,
        grad_gain_two, grad_bin, grad_bdown,
    ) = mlp(
        ot, o_got, weights, token0, grad_low, core_at, gain_two.reshape(1, -1),
        bias_in.astype(F32).reshape(1, -1), bias_down.astype(F32).reshape(1, -1),
    )
    far = send(to_give, core_swap)
    away_output = send(output, plan.mirror())
    joined = mlp_weights(ot, o_got, hidden_t, normed_t, grad_low, grad_pre, grad_mid_low, core_at)
    early_qt, joined, far = tie(qt, joined, far)
    scattered = lax.psum_scatter(joined, "dp", scatter_dimension=0, tiled=True)

    def backward(at_group, queries):
        return attention_backward(
            ids, col, place, queries, kt, vt, to_keep, far, ot, lse, scale_vec, hd, tile, at_group
        )

    def to_owners(grads):
        return [send(grads[m], plan.pair_swap(m)) for m in range(1, pairs)]

    def add_up(grads, came):
        total = grads[0].astype(F32)
        for one in came:
            total = total + one.astype(F32)
        return total

    dq_a, dkv_a, gs_a = backward(0, early_qt)
    grads_a = weight_gradient(xt, dq_a, dkv_a, at, pairs)
    later_qt, *grads_a = tie(qt, *grads_a)
    came_a = to_owners(grads_a)
    dq_b, dkv_b, gs_b = backward(1, later_qt)
    dq_b, dkv_b, away_output = tie(dq_b, dkv_b, away_output)
    output = jnp.where(home, output, away_output)

    gain_row = gain_one.reshape(1, -1)
    late_dx, gain_late = input_gradient(
        (dkv_a, dkv_b), (), full_qkv, slots[2:], 2, core_at, gain_row
    )
    late_dx, later_dq, scattered, *came_a = tie(late_dx, dq_b, scattered, *came_a)
    held_a, line_a = line_inward(add_up(grads_a, came_a), plan, BF)
    held_o, line_o = line_inward(scattered, plan, BF)
    late_got = [
        send(late_dx[(2 * k + 1) * rows : (2 * k + 2) * rows], core_swap) for k in range(half - 1)
    ]
    grads_b = weight_gradient(xt, later_dq, dkv_b, at, pairs)
    last_dq, line_a, *rest = tie(dq_b, line_a, *late_got, *grads_b)
    late_got, grads_b = rest[: half - 1], rest[half - 1 :]
    came_b = to_owners(grads_b)
    held_a, line_a = line_across(held_a, line_a, plan, BF)
    dx, gain_early = input_gradient(
        (dkv_a, dkv_b), (dq_a, last_dq), full_qkv, slots[:2], 0, core_at, gain_row
    )
    dx, gain_early, line_o, line_a, *rest = tie(
        dx, gain_early, line_o, line_a, *late_got, *came_b
    )
    late_got, came_b = rest[: half - 1], rest[half - 1 :]
    turned = []
    for k in range(half - 1):
        mine = late_dx[2 * k * rows : (2 * k + 1) * rows].astype(F32)
        turned.append(
            send((mine + late_got[k].astype(F32)).astype(BF), plan.turn(-k - 1, False))
        )
    got = send(dx[rows:], core_swap)
    held_b, line_b = line_inward(add_up(grads_b, came_b), plan, BF)
    held_o, line_o = line_across(held_o, line_o, plan, BF)
    line_a = line_outward(line_joined(held_a, line_a), plan, z)

    scale_slope = SOFT_FACTOR / math.sqrt(hd) * scale_exp / (1.0 + scale_exp)
    grad_scale = jnp.sum(jnp.concatenate([gs_a, gs_b], 0).reshape(heads // 2, hd), 0)
    grad_scale = grad_scale * scale_slope / (scale_dim * LOG2E)
    small = jnp.concatenate(
        [
            *(v.reshape(-1) for v in (gain_late + gain_early, grad_gain_two, grad_bin, grad_bdown)),
            grad_scale,
        ]
    )
    small_size = small.shape[0]
    small = jnp.pad(small, (0, -small_size % 1024)).reshape(-1, 128)
    small = small + send(small, core_swap)
    mask = 1
    while mask < pairs:
        small = small + send(small, plan.pair_swap(mask))
        mask *= 2
    got, line_b = tie(got, line_b)
    held_b, line_b = line_across(held_b, line_b, plan, BF)
    total = dx[:rows].astype(F32) + got.astype(F32) + grad_middle
    for one in turned:
        total = total + one.astype(F32)
    last = send(total.astype(BF), plan.mirror())
    line_b, line_a, small = tie(line_b, line_a, small)
    line_b = line_outward(line_joined(held_b, line_b), plan, z)
    others = line_outward(line_joined(held_o, line_o), plan, z).astype(F32)
    mask = 1
    while mask < n:
        small = small + send(small, plan.line_swap(mask))
        mask *= 2
    small = small.reshape(-1)

    def owned_rows(value):
        keep = lax.dynamic_slice_in_dim(value, core * wrows, wrows, 0)
        give = lax.dynamic_slice_in_dim(value, (1 - core) * wrows, wrows, 0)
        came = send(give, core_swap)
        return jnp.where(core == 0, keep, came), jnp.where(core == 0, came, keep)

    swapped_a = owned_rows(line_a)
    last, line_b = tie(last, line_b)
    grad_tokens = jnp.where(home, total, last.astype(F32))
    swapped = (swapped_a, owned_rows(line_b))
    size = part // 2
    owned_qkv = jnp.concatenate(
        [
            swapped[g][c][:, which * size : (which + 1) * size]
            for which in (2, 0, 1)
            for c in range(2)
            for g in range(2)
        ],
        1,
    ).astype(F32)

    return (
        output[None],
        grad_tokens[None],
        owned_qkv,
        others[:, 2 * width :],
        others[:, width : 2 * width],
        others[:, :width],
        small[:width],
        small[width : 2 * width],
        small[2 * width : 3 * width],
        small[3 * width : 4 * width],
        small[4 * width : small_size],
    )


def solution(mesh):
    split = P("dp", "ctx", None)
    weight = P("dp", None)
    return jax.shard_map(
        body,
        mesh=mesh,
        in_specs=(split, weight, weight, weight, weight, weight, P(), P(), P(), P(), P(), split),
        out_specs=(split, split, weight, weight, weight, weight, P(), P(), P(), P(), P()),
        check_vma=False,
    )
```

```python
import functools
import math

import jax
import jax.numpy as jnp
import numpy as np
from jax import lax
from jax.experimental import pallas as pl
from jax.experimental.pallas import tpu as pltpu
from jax.sharding import PartitionSpec as P

EPSILON = 1e-06
SOFT_FACTOR = 1.442695041
LOG2E = 1.4426950408889634
MASKED = -1e30
HEADS_AT_ONCE = 4
COST = 1.0
AXES = ("dp", "ctx")
BF = jnp.bfloat16
F32 = jnp.float32


def nn(a, b):
    return lax.dot_general(a, b, (((1,), (0,)), ((), ())), preferred_element_type=F32)


def nt(a, b):
    return lax.dot_general(a, b, (((1,), (1,)), ((), ())), preferred_element_type=F32)


def tile_counts(ids_ref, stretch, tile, tiles):
    low = ids_ref[stretch * tile]
    high = ids_ref[stretch * tile + tile - 1]
    full = jnp.int32(0)
    need = jnp.int32(0)
    for t in range(tiles):
        full += (ids_ref[t * tile + tile - 1] <= low).astype(jnp.int32)
        need += (ids_ref[t * tile] <= high).astype(jnp.int32)
    return full, need


def project_kernel(part, query_slots, n, core_ref, gain_ref, scale_ref, *refs):
    x_refs, w_refs = refs[:n], refs[n : n + 3]
    qt_ref, kt_ref, vt_ref, xt_ref, wt, xs = refs[n + 3 :]
    i = pl.program_id(0)

    @pl.when(i == 0)
    def _():
        for j, ref in enumerate(w_refs):
            wt[j * part : (j + 1) * part, :] = ref[...].T

    for s in range(n):

        @pl.when(i == s)
        def _(s=s):
            xs[...] = x_refs[s][...]

    x = xs[...].astype(F32)
    inverse = lax.rsqrt(jnp.mean(x * x, -1, keepdims=True) + EPSILON)
    xt_ref[...] = (x * inverse * gain_ref[...]).astype(BF).T
    kt_ref[...] = nn(wt[part : 2 * part, :], xt_ref[...]).astype(BF)
    vt_ref[...] = nn(wt[2 * part :, :], xt_ref[...]).astype(BF)

    @pl.when(i < query_slots)
    def _():
        qt_ref[...] = (nn(wt[:part, :], xt_ref[...]) * scale_ref[...]).astype(BF)


def project(slots, w_full, core, gain, scale):
    n = len(slots)
    rows, width = slots[0].shape
    part = width // 2
    query_slots = 2
    once = pl.Buffered(1)
    return pl.pallas_call(
        functools.partial(project_kernel, part, query_slots, n),
        grid_spec=pltpu.PrefetchScalarGridSpec(
            num_scalar_prefetch=1,
            grid=(n,),
            in_specs=[
                pl.BlockSpec((1, width), lambda i, c: (0, 0)),
                pl.BlockSpec((part, 1), lambda i, c: (0, 0)),
                *[pl.BlockSpec((rows, width), lambda i, c: (0, 0), pipeline_mode=once)] * n,
                *[
                    pl.BlockSpec(
                        (width, part), lambda i, c, j=j: (0, 2 * j + c[0]), pipeline_mode=once
                    )
                    for j in range(3)
                ],
            ],
            out_specs=[
                pl.BlockSpec((part, rows), lambda i, c: (0, jnp.minimum(i, query_slots - 1))),
                pl.BlockSpec((part, rows), lambda i, c: (0, i)),
                pl.BlockSpec((part, rows), lambda i, c: (0, i)),
                pl.BlockSpec((width, rows), lambda i, c: (0, i)),
            ],
            scratch_shapes=[pltpu.VMEM((3 * part, width), BF), pltpu.VMEM((rows, width), BF)],
        ),
        out_shape=[
            jax.ShapeDtypeStruct((part, query_slots * rows), BF),
            jax.ShapeDtypeStruct((part, n * rows), BF),
            jax.ShapeDtypeStruct((part, n * rows), BF),
            jax.ShapeDtypeStruct((width, n * rows), BF),
        ],
        compiler_params=pltpu.CompilerParams(vmem_limit_bytes=60 << 20),
        cost_estimate=pl.CostEstimate(
            flops=int(COST * 2 * width * part * rows * (2 * n + query_slots)),
            bytes_accessed=1 << 16,
            transcendentals=0,
        ),
        name="project",
    )(core, gain, scale, *slots, *[w_full] * 3)


def mlp_kernel(
    part, core_ref, near_ref, far_ref, w_ref, x_ref, cot_ref, gain_ref, bin_ref, bdown_ref, out_ref, keep_ref, give_ref,
    gmid_ref, ht_ref, nt_ref, gpre_ref, gml_ref, gain_out, bin_out, bdown_out, middle, normed,
    hidden, slope, g_ref,
):
    width = x_ref.shape[1]
    step = width // 5
    chunks = [slice(c * step, (c + 1) * step) for c in range(5)]
    down, inner, outer = 0, width, 2 * width
    core = core_ref[0]
    near_rows = pl.ds(pl.multiple_of(core * part, part), part)
    far_rows = pl.ds(pl.multiple_of((1 - core) * part, part), part)

    @pl.when(pl.program_id(0) == 0)
    def _():
        for ref in (gain_out, bin_out, bdown_out):
            ref[...] = jnp.zeros(ref.shape, F32)

    near, far = near_ref[...].T, far_ref[...].T
    for cols in chunks:
        at = slice(outer + cols.start, outer + cols.stop)
        middle[:, cols] = (
            x_ref[:, cols].astype(F32) + nn(near, w_ref[near_rows, at]) + nn(far, w_ref[far_rows, at])
        )
    mid = middle[...]
    inverse = lax.rsqrt(jnp.mean(mid * mid, -1, keepdims=True) + EPSILON)
    normed[...] = (mid * inverse * gain_ref[...]).astype(BF)
    nt_ref[...] = normed[...].T
    for cols in chunks:
        at = slice(inner + cols.start, inner + cols.stop)
        pre = nn(normed[...], w_ref[:, at]) + bin_ref[:, cols]
        sigma = 1.0 / (1.0 + jnp.exp(-pre))
        hidden[:, cols] = (pre * sigma).astype(BF)
        slope[:, cols] = sigma * (1.0 + pre * (1.0 - sigma))
    ht_ref[...] = hidden[...].T
    for cols in chunks:
        at = slice(down + cols.start, down + cols.stop)
        out_ref[:, cols] = (
            middle[:, cols] + nn(hidden[...], w_ref[:, at]) + bdown_ref[:, cols]
        ).astype(BF)
    for cols in chunks:
        gpre_ref[:, cols] = (
            nt(cot_ref[...], w_ref[cols, down : down + width]) * slope[:, cols]
        ).astype(BF)
    for cols in chunks:
        g_ref[:, cols] = nt(gpre_ref[...], w_ref[cols, inner : inner + width])
    bin_out[...] += jnp.sum(gpre_ref[...].astype(F32), 0, keepdims=True)
    cot = cot_ref[...].astype(F32)
    bdown_out[...] += jnp.sum(cot, 0, keepdims=True)
    turned = middle[...] * inverse
    gn = g_ref[...] * turned
    gain_out[...] += jnp.sum(gn, 0, keepdims=True)
    mean = jnp.mean(gn * gain_ref[...], -1, keepdims=True)
    gmid = cot + inverse * (g_ref[...] * gain_ref[...] - turned * mean)
    gmid_ref[...] = gmid
    gml_ref[...] = gmid.astype(BF)
    low = gml_ref[...]
    keep_ref[...] = nt(w_ref[near_rows, outer : outer + width], low).astype(BF)
    give_ref[...] = nt(w_ref[far_rows, outer : outer + width], low).astype(BF)


def mlp(near, far, weights, x, cot, core, gain, bias_in, bias_down):
    part, rows = far.shape
    width = x.shape[1]
    tile = 256
    once = pl.Buffered(1)
    row = pl.BlockSpec((tile, width), lambda i, c: (i, 0))
    feature = pl.BlockSpec((part, tile), lambda i, c: (0, i))
    wide = pl.BlockSpec((width, tile), lambda i, c: (0, i))
    vector = pl.BlockSpec((1, width), lambda i, c: (0, 0))
    return pl.pallas_call(
        functools.partial(mlp_kernel, part),
        grid_spec=pltpu.PrefetchScalarGridSpec(
            num_scalar_prefetch=1,
            grid=(rows // tile,),
            in_specs=[
                feature,
                feature,
                pl.BlockSpec(weights.shape, lambda i, c: (0, 0), pipeline_mode=once),
                row, row, vector, vector, vector,
            ],
            out_specs=[
                row, feature, feature, row, wide, wide, row, row, vector, vector, vector
            ],
            scratch_shapes=[
                pltpu.VMEM((tile, width), F32),
                pltpu.VMEM((tile, width), BF),
                pltpu.VMEM((tile, width), BF),
                pltpu.VMEM((tile, width), F32),
                pltpu.VMEM((tile, width), F32),
            ],
        ),
        out_shape=[
            jax.ShapeDtypeStruct((rows, width), BF),
            jax.ShapeDtypeStruct((part, rows), BF),
            jax.ShapeDtypeStruct((part, rows), BF),
            jax.ShapeDtypeStruct((rows, width), F32),
            jax.ShapeDtypeStruct((width, rows), BF),
            jax.ShapeDtypeStruct((width, rows), BF),
            jax.ShapeDtypeStruct((rows, width), BF),
            jax.ShapeDtypeStruct((rows, width), BF),
            jax.ShapeDtypeStruct((1, width), F32),
            jax.ShapeDtypeStruct((1, width), F32),
            jax.ShapeDtypeStruct((1, width), F32),
        ],
        compiler_params=pltpu.CompilerParams(vmem_limit_bytes=60 << 20),
        cost_estimate=pl.CostEstimate(
            flops=int(COST * 12 * rows * width * width), bytes_accessed=1 << 16, transcendentals=0
        ),
        name="mlp",
    )(core, near, far, weights, x, cot, gain, bias_in, bias_down)


def mlp_weight_kernel(
    core_ref, near_ref, far_ref, ht_ref, nt_ref, cot_ref, gpre_ref, gml_ref, out_ref
):
    which, part_at = pl.program_id(0), pl.program_id(1)

    @pl.when(which == 0)
    def _():
        out_ref[...] = nn(ht_ref[...], cot_ref[...]).astype(BF)

    @pl.when(which == 1)
    def _():
        out_ref[...] = nn(nt_ref[...], gpre_ref[...]).astype(BF)

    @pl.when((which == 2) & (part_at == core_ref[0]))
    def _():
        out_ref[...] = nn(near_ref[...], gml_ref[...]).astype(BF)

    @pl.when((which == 2) & (part_at != core_ref[0]))
    def _():
        out_ref[...] = nn(far_ref[...], gml_ref[...]).astype(BF)


def mlp_weights(near, far, ht, nrt, cot, gpre, gml, core):
    part, rows = far.shape
    width = cot.shape[1]
    once = pl.Buffered(1)

    def whole(shape):
        return pl.BlockSpec(shape, lambda j, r, c: (0,) * len(shape), pipeline_mode=once)

    return pl.pallas_call(
        mlp_weight_kernel,
        grid_spec=pltpu.PrefetchScalarGridSpec(
            num_scalar_prefetch=1,
            grid=(3, 2),
            in_specs=[
                whole((part, rows)),
                whole((part, rows)),
                pl.BlockSpec((part, rows), lambda j, r, c: (jnp.where(j == 0, r, 1), 0)),
                pl.BlockSpec((part, rows), lambda j, r, c: (jnp.where(j == 1, r, j // 2), 0)),
                whole((rows, width)),
                whole((rows, width)),
                whole((rows, width)),
            ],
            out_specs=pl.BlockSpec((part, width), lambda j, r, c: (r, j)),
        ),
        out_shape=jax.ShapeDtypeStruct((width, 3 * width), BF),
        compiler_params=pltpu.CompilerParams(vmem_limit_bytes=60 << 20),
        cost_estimate=pl.CostEstimate(
            flops=6 * rows * width * width, bytes_accessed=20 << 20, transcendentals=0
        ),
        name="mlp_weights",
    )(core, near, far, ht, nrt, cot, gpre, gml)


def load_keys(ref, place_ref, hd, tile, group, knat, kt=None):
    tiles = ref.shape[1] // tile
    for b in range(tiles):
        stretch = place_ref[tiles + b]
        piece = ref[:, b * tile : (b + 1) * tile]
        if kt is not None:
            kt[stretch] = piece
        if knat is not None:
            for h in range(group):
                knat[h, stretch] = piece[h * hd : (h + 1) * hd, :].T


def forward_kernel(
    hd, tile, ids_ref, place_ref, row_ref, col_ref, qt_ref, kt_ref, vt_ref, near_ref, far_ref,
    lse_ref, knat, vt, acc, m_ref, l_ref,
):
    group = qt_ref.shape[0] // hd
    tiles = vt.shape[0]
    load_keys(kt_ref, place_ref, hd, tile, group, knat)
    load_keys(vt_ref, place_ref, hd, tile, group, None, vt)
    per_half = near_ref.shape[1] // tile

    def one_tile(qi, carry):
        stretch = place_ref[tiles + qi]
        full, need = tile_counts(ids_ref, stretch, tile, tiles)
        qcol = pl.ds(pl.multiple_of(qi * tile, tile), tile)
        qpos = pl.ds(pl.multiple_of(stretch * tile, tile), tile)
        m_ref[...] = jnp.full(m_ref.shape, MASKED, F32)
        l_ref[...] = jnp.zeros(l_ref.shape, F32)
        acc[...] = jnp.zeros(acc.shape, F32)

        def step(ts, masked):
            if masked:
                allowed = [
                    col_ref[pl.ds(pl.multiple_of(t * tile, tile), tile), :] <= row_ref[:, qpos]
                    for t in ts
                ]
            scores = [
                [nn(knat[h, t], qt_ref[h * hd : (h + 1) * hd, qcol]) for t in ts]
                for h in range(group)
            ]
            for h in range(group):
                s = scores[h]
                if masked:
                    s = [jnp.where(ok, one, MASKED) for ok, one in zip(allowed, s)]
                old = m_ref[h]
                new = old
                for one in s:
                    new = jnp.maximum(new, jnp.max(one, 0, keepdims=True))
                p = [jnp.exp2(one - new) for one in s]
                alpha = jnp.exp2(old - new)
                total = l_ref[h] * alpha
                for one in p:
                    total = total + jnp.sum(one, 0, keepdims=True)
                l_ref[h] = total
                m_ref[h] = new
                out = acc[h] * alpha
                for t, one in zip(ts, p):
                    out = out + nn(vt[t, h * hd : (h + 1) * hd, :], one.astype(BF))
                acc[h] = out

        def full_step(i, c):
            step([2 * i, 2 * i + 1], False)
            return c

        def mask_step(i, c):
            step([2 * i, 2 * i + 1], True)
            return c

        lax.fori_loop(0, full // 2, full_step, 0)
        lax.fori_loop(full // 2, (need + 1) // 2, mask_step, 0)
        inner = pl.ds(pl.multiple_of((qi % per_half) * tile, tile), tile)
        for half, ref in enumerate((near_ref, far_ref)):

            @pl.when(qi // per_half == half)
            def _(ref=ref):
                for h in range(group):
                    ref[h * hd : (h + 1) * hd, inner] = (acc[h] / l_ref[h]).astype(BF)

        for h in range(group):
            lse_ref[h, :, qcol] = m_ref[h] + jnp.log2(l_ref[h])
        return carry

    lax.fori_loop(0, qt_ref.shape[1] // tile, one_tile, 0)


def backward_kernel(hd, tile, base, count, first, last, *refs):
    ids_ref, place_ref, row_ref, col_ref, qt_ref, kt_ref, vt_ref = refs[:7]
    near_ref, far_ref, onear_ref, ofar_ref, lse_ref = refs[7:12]
    if last:
        before_ref, scale_ref, dqt_ref, dkt_ref, dvt_ref, gs_ref = refs[12:18]
        knat, vnat, kt, dq, dk, dv, delta, dot = refs[18:]
    else:
        dqt_ref, dkt_ref, dvt_ref = refs[12:15]
        knat, vnat, kt, dq, dk, dv, delta, dot = refs[15:]
    tiles = kt_ref.shape[1] // tile
    group = qt_ref.shape[0] // hd

    def block_of(i):
        return pl.multiple_of(place_ref[place_ref[base + i]] * tile, tile)

    for i in range(count):
        cols = pl.ds(block_of(i), tile)
        kt[i] = kt_ref[:, cols]
        for h in range(group):
            hs = slice(h * hd, (h + 1) * hd)
            knat[h, i] = kt_ref[hs, cols].T
            vnat[h, i] = vt_ref[hs, cols].T
    per_half = near_ref.shape[1] // tile
    for half, (ref, o_ref) in enumerate(((near_ref, onear_ref), (far_ref, ofar_ref))):
        for b in range(per_half):
            cols = slice(b * tile, (b + 1) * tile)
            dot[half * per_half + b] = ref[:, cols]
            product = ref[:, cols].astype(F32) * o_ref[:, cols].astype(F32)
            for h in range(group):
                delta[half * per_half + b, h] = jnp.sum(
                    product[h * hd : (h + 1) * hd], 0, keepdims=True
                )
    dk[...] = jnp.zeros(dk.shape, F32)
    dv[...] = jnp.zeros(dv.shape, F32)
    if last:
        gs_ref[...] = jnp.zeros(gs_ref.shape, F32)

    def one_tile(qi, carry):
        stretch = place_ref[tiles + qi]
        low = ids_ref[stretch * tile]
        high = ids_ref[stretch * tile + tile - 1]
        full = jnp.int32(0)
        need = jnp.int32(0)
        for i in range(count):
            t = place_ref[base + i]
            full += (ids_ref[t * tile + tile - 1] <= low).astype(jnp.int32)
            need += (ids_ref[t * tile] <= high).astype(jnp.int32)
        qcol = pl.ds(pl.multiple_of(qi * tile, tile), tile)
        qpos = pl.ds(pl.multiple_of(stretch * tile, tile), tile)
        dq[...] = before_ref[:, qcol] if last else jnp.zeros(dq.shape, F32)

        def step(ts, masked):
            if masked:
                allowed = [
                    col_ref[pl.ds(pl.multiple_of(place_ref[base + t] * tile, tile), tile), :]
                    <= row_ref[:, qpos]
                    for t in ts
                ]

            def scores(h, t):
                hs = slice(h * hd, (h + 1) * hd)
                return nn(knat[h, t], qt_ref[hs, qcol]), nn(vnat[h, t], dot[qi, hs, :])

            order = [(h, i) for h in range(group) for i in range(len(ts))]
            ahead = scores(0, ts[0])
            for j, (h, i) in enumerate(order):
                hs = slice(h * hd, (h + 1) * hd)
                t = ts[i]
                s, dp = ahead
                if j + 1 < len(order):
                    ahead = scores(order[j + 1][0], ts[order[j + 1][1]])
                if masked:
                    s = jnp.where(allowed[i], s, MASKED)
                p = jnp.exp2(s - lse_ref[h, :, qcol])
                ds = (p * (dp - delta[qi, h])).astype(BF)
                dv[t, hs, :] += nt(dot[qi, hs, :], p.astype(BF))
                dk[t, hs, :] += nt(qt_ref[hs, qcol], ds)
                dq[hs, :] += nn(kt[t, hs, :], ds)

        def full_step(i, c):
            step([2 * i, 2 * i + 1], False)
            return c

        def mask_step(i, c):
            step([2 * i, 2 * i + 1], True)
            return c

        lax.fori_loop(0, full // 2, full_step, 0)
        lax.fori_loop(full // 2, (need + 1) // 2, mask_step, 0)
        if last:
            gs_ref[...] += jnp.sum(dq[...] * qt_ref[:, qcol].astype(F32), 1, keepdims=True)
            dqt_ref[:, qcol] = (dq[...] * scale_ref[...]).astype(BF)
        else:
            dqt_ref[:, qcol] = dq[...]
        return carry

    lax.fori_loop(0, qt_ref.shape[1] // tile, one_tile, 0)
    for i in range(count):
        cols = pl.ds(pl.multiple_of(block_of(i) - first * tile, tile), tile)
        dkt_ref[:, cols] = (dk[i] * (1.0 / LOG2E)).astype(BF)
        dvt_ref[:, cols] = dv[i].astype(BF)


def attention_specs(nq, nk, hd, group, at):
    size = group * hd
    return (
        [
            pl.BlockSpec(memory_space=pltpu.SMEM),
            pl.BlockSpec(memory_space=pltpu.SMEM),
            pl.BlockSpec((1, nk), lambda i: (0, 0)),
            pl.BlockSpec((nk, 1), lambda i: (0, 0)),
            pl.BlockSpec((size, nq), lambda i: (i + at, 0)),
            pl.BlockSpec((size, nk), lambda i: (i + at, 0)),
            pl.BlockSpec((size, nk), lambda i: (i + at, 0)),
        ],
        pl.BlockSpec((size, nq // 2), lambda i: (i + at, 0)),
        pl.BlockSpec((group, 1, nq), lambda i: (i + at, 0, 0)),
    )


def attention_forward(ids, col, place, qt, kt, vt, hd, tile):
    heads = qt.shape[0] // hd
    nq, nk = qt.shape[1], kt.shape[1]
    group = HEADS_AT_ONCE
    common, halves, rows = attention_specs(nq, nk, hd, group, 0)
    pairs = heads * nq * nk * 0.6
    return pl.pallas_call(
        functools.partial(forward_kernel, hd, tile),
        grid=(heads // group,),
        in_specs=common,
        out_specs=[halves, halves, rows],
        out_shape=[
            jax.ShapeDtypeStruct((heads * hd, nq // 2), BF),
            jax.ShapeDtypeStruct((heads * hd, nq // 2), BF),
            jax.ShapeDtypeStruct((heads, 1, nq), F32),
        ],
        scratch_shapes=[
            pltpu.VMEM((group, nk // tile, tile, hd), BF),
            pltpu.VMEM((nk // tile, group * hd, tile), BF),
            pltpu.VMEM((group, hd, tile), F32),
            pltpu.VMEM((group, 1, tile), F32),
            pltpu.VMEM((group, 1, tile), F32),
        ],
        compiler_params=pltpu.CompilerParams(vmem_limit_bytes=60 << 20),
        cost_estimate=pl.CostEstimate(
            flops=int(COST * pairs * 1024), bytes_accessed=1 << 16, transcendentals=int(COST * pairs)
        ),
        name="attention_forward",
    )(ids, place, ids.reshape(1, -1), col, qt, kt, vt)


def attention_backward(
    ids, col, place, qt, kt, vt, near, far, onear, ofar, lse, hd, tile, before=None, scale=None
):
    heads = qt.shape[0] // hd
    nq, nk = qt.shape[1], kt.shape[1]
    group = HEADS_AT_ONCE
    size = group * hd
    last = before is not None
    early = nq // tile
    tiles = nk // tile
    count, first = (early, 0) if last else (tiles - early, early)
    base = 2 * tiles + (0 if last else early)
    common, halves, rows = attention_specs(nq, nk, hd, group, 0)
    wide = pl.BlockSpec((size, nq), lambda i: (i, 0))
    keys = pl.BlockSpec((size, count * tile), lambda i: (i, 0))
    one = pl.BlockSpec((size, 1), lambda i: (i, 0))
    pairs = heads * nq * count * tile * 0.6
    return pl.pallas_call(
        functools.partial(backward_kernel, hd, tile, base, count, first, last),
        grid=(heads // group,),
        in_specs=[*common, halves, halves, halves, halves, rows, *([wide, one] if last else [])],
        out_specs=[wide, keys, keys, *([one] if last else [])],
        out_shape=[
            jax.ShapeDtypeStruct((heads * hd, nq), BF if last else F32),
            jax.ShapeDtypeStruct((heads * hd, count * tile), BF),
            jax.ShapeDtypeStruct((heads * hd, count * tile), BF),
            *([jax.ShapeDtypeStruct((heads * hd, 1), F32)] if last else []),
        ],
        scratch_shapes=[
            pltpu.VMEM((group, count, tile, hd), BF),
            pltpu.VMEM((group, count, tile, hd), BF),
            pltpu.VMEM((count, size, tile), BF),
            pltpu.VMEM((size, tile), F32),
            pltpu.VMEM((count, size, tile), F32),
            pltpu.VMEM((count, size, tile), F32),
            pltpu.VMEM((nq // tile, group, 1, tile), F32),
            pltpu.VMEM((nq // tile, size, tile), BF),
        ],
        compiler_params=pltpu.CompilerParams(vmem_limit_bytes=60 << 20),
        cost_estimate=pl.CostEstimate(
            flops=int(pairs * 2560), bytes_accessed=16 << 20, transcendentals=int(pairs)
        ),
        name="attention_backward",
    )(
        ids, place, ids.reshape(1, -1), col, qt, kt, vt, near, far, onear, ofar, lse,
        *([before, scale] if last else []),
    )


def weight_kernel(size, nq, at_ref, xt_ref, dqt_ref, dka_ref, dva_ref, dkb_ref, dvb_ref, *out_refs):
    for m, ref in enumerate(out_refs):

        @pl.when(pl.program_id(0) == m)
        def _(ref=ref):
            early = jnp.concatenate([dka_ref[...], dva_ref[...]], 0)
            late = jnp.concatenate([dkb_ref[...], dvb_ref[...]], 0)
            ref[:, : 2 * size] = (nt(xt_ref[:, :nq], early) + nt(xt_ref[:, nq:], late)).astype(BF)
            ref[:, 2 * size :] = nt(xt_ref[:, :nq], dqt_ref[...]).astype(BF)


def weight_gradient(xt, dqt, early, late, at, pieces, which):
    width, nk = xt.shape
    part, nq = dqt.shape
    size = part // 2
    rows = width // pieces
    once = pl.Buffered(1)

    def heads(cols):
        return pl.BlockSpec((size, cols), lambda i, a: (which, 0), pipeline_mode=once)

    return pl.pallas_call(
        functools.partial(weight_kernel, size, nq),
        grid_spec=pltpu.PrefetchScalarGridSpec(
            num_scalar_prefetch=1,
            grid=(pieces,),
            in_specs=[
                pl.BlockSpec((rows, nk), lambda i, a: (a[i], 0)),
                heads(nq), heads(nq), heads(nq), heads(nk - nq), heads(nk - nq),
            ],
            out_specs=[pl.BlockSpec((rows, 3 * size), lambda i, a: (0, 0))] * pieces,
        ),
        out_shape=[jax.ShapeDtypeStruct((rows, 3 * size), BF)] * pieces,
        compiler_params=pltpu.CompilerParams(vmem_limit_bytes=60 << 20),
        cost_estimate=pl.CostEstimate(
            flops=2 * width * size * (2 * nk + nq), bytes_accessed=12 << 20, transcendentals=0
        ),
        name="weight_gradient",
    )(at, xt, dqt, *early, *late)


def dx_kernel(part, queries, n, core_ref, *refs):
    dk_ref, dv_ref, wk_ref, wv_ref, gain_ref = refs[:5]
    x_refs = refs[5 : 5 + n]
    rest = refs[5 + n :]
    if queries:
        dq_ref, wq_ref = rest[:2]
        rest = rest[2:]
    dx_ref, gg_ref, g_ref, xs = rest
    i = pl.program_id(0)
    width = dx_ref.shape[1]
    tile = dx_ref.shape[0]
    step = width // 5
    dk = dk_ref[...].T
    dv = dv_ref[...].T
    if queries:
        dq = dq_ref[...].T
    for c in range(5):
        cols = slice(c * step, (c + 1) * step)
        g = nt(dk, wk_ref[cols, :]) + nt(dv, wv_ref[cols, :])
        if queries:
            g = g + nt(dq, wq_ref[cols, :])
        g_ref[:, cols] = g

    @pl.when(i == 0)
    def _():
        gg_ref[...] = jnp.zeros(gg_ref.shape, F32)

    per_slot = x_refs[0].shape[0] // tile
    for s in range(n):

        @pl.when(i // per_slot == s)
        def _(s=s):
            xs[...] = x_refs[s][pl.ds(pl.multiple_of((i % per_slot) * tile, tile), tile), :]

    x = xs[...].astype(F32)
    inverse = lax.rsqrt(jnp.mean(x * x, -1, keepdims=True) + EPSILON)
    normed = x * inverse
    g = g_ref[...]
    gn = g * normed
    gg_ref[...] += jnp.sum(gn, 0, keepdims=True)
    scaled = g * gain_ref[...]
    mean = jnp.mean(gn * gain_ref[...], -1, keepdims=True)
    dx_ref[...] = (inverse * (scaled - normed * mean)).astype(BF)


def input_gradient(dkvs, dqs, w_full, slots, core, gain):
    part = dkvs[0].shape[0]
    n = len(slots)
    rows, width = slots[0].shape
    tile = 256
    once = pl.Buffered(1)
    dkv = pl.BlockSpec((part, tile), lambda i, c: (0, i))

    def weight(j):
        return pl.BlockSpec(
            (width, part), lambda i, c, j=j: (0, 2 * j + c[0]), pipeline_mode=once
        )

    specs = [
        dkv, dkv, weight(1), weight(2), pl.BlockSpec((1, width), lambda i, c: (0, 0)),
        *[pl.BlockSpec((rows, width), lambda i, c: (0, 0), pipeline_mode=once)] * n,
    ]
    operands = [*dkvs, w_full, w_full, gain, *slots]
    if dqs:
        specs += [dkv, weight(0)]
        operands += [*dqs, w_full]
    return pl.pallas_call(
        functools.partial(dx_kernel, part, bool(dqs), n),
        grid_spec=pltpu.PrefetchScalarGridSpec(
            num_scalar_prefetch=1,
            grid=(n * rows // tile,),
            in_specs=specs,
            out_specs=[
                pl.BlockSpec((tile, width), lambda i, c: (i, 0)),
                pl.BlockSpec((1, width), lambda i, c: (0, 0)),
            ],
            scratch_shapes=[pltpu.VMEM((tile, width), F32), pltpu.VMEM((tile, width), BF)],
        ),
        out_shape=[
            jax.ShapeDtypeStruct((n * rows, width), BF),
            jax.ShapeDtypeStruct((1, width), F32),
        ],
        compiler_params=pltpu.CompilerParams(vmem_limit_bytes=60 << 20),
        cost_estimate=pl.CostEstimate(
            flops=int(COST * 2 * width * n * rows * part * (3 if dqs else 2)),
            bytes_accessed=1 << 16,
            transcendentals=0,
        ),
        name="input_gradient",
    )(core, *operands)


class Plan:
    def __init__(self, dp, ctx):
        self.dp, self.ctx = dp, ctx
        self.half = ctx // 2

    def index(self, pair, core, z):
        return (pair * 2 + core) * self.ctx + z

    def perm(self, to):
        out = []
        for d in range(self.dp):
            for z in range(self.ctx):
                got = to(d // 2, d % 2, z)
                if got is not None:
                    out.append((self.index(d // 2, d % 2, z), self.index(*got)))
        return out

    def home(self, core, z):
        return core == z // self.half

    def turned(self, z, k):
        first = z // self.half * self.half
        return first + (z - first + k) % self.half

    def core_swap(self):
        return self.perm(lambda p, c, z: (p, 1 - c, z))

    def pair_swap(self, mask):
        return self.perm(lambda p, c, z: (p ^ mask, c, z))

    def line_swap(self, mask):
        return self.perm(lambda p, c, z: (p, c, z ^ mask))

    def line_in(self, s):
        last = self.ctx - 1
        to = {s: s + 1, last - s: last - s - 1}
        return self.perm(lambda p, c, z: (p, c, to[z]) if z in to else None)

    def line_out(self, s):
        last = self.ctx - 1
        to = {s + 1: s, last - s - 1: last - s}
        return self.perm(lambda p, c, z: (p, c, to[z]) if z in to else None)

    def line_middle(self):
        to = {self.half - 1: self.half, self.half: self.half - 1}
        return self.perm(lambda p, c, z: (p, c, to[z]) if z in to else None)

    def mirror(self):
        return self.perm(
            lambda p, c, z: None if self.home(c, z) else (p, 1 - c, self.ctx - 1 - z)
        )

    def mirror_or_turn(self, k):
        return self.perm(
            lambda p, c, z: (p, c, self.turned(z, k))
            if self.home(c, z)
            else (p, 1 - c, self.ctx - 1 - z)
        )

    def turn(self, k, away_only):
        return self.perm(
            lambda p, c, z: None
            if away_only and self.home(c, z)
            else (p, c, self.turned(z, k))
        )

    def shard(self, core, z, k, mine):
        chip = self.turned(z, -k)
        at_home = self.home(core, z) if mine else not self.home(core, z)
        return chip if at_home else self.ctx - 1 - chip

    def places(self):
        table = np.zeros((self.dp, self.ctx, 6 * self.ctx), np.int32)
        for d in range(self.dp):
            for z in range(self.ctx):
                slots = [
                    self.shard(d % 2, z, k, mine) for k in range(self.half) for mine in (True, False)
                ]
                stretches = [s for shard in slots for s in (shard, 2 * self.ctx - 1 - shard)]
                for block, stretch in enumerate(stretches):
                    table[d, z, stretch] = block
                    table[d, z, 2 * self.ctx + block] = stretch
                table[d, z, 4 * self.ctx :] = sorted(stretches[:4]) + sorted(stretches[4:])
        return table.reshape(self.dp * self.ctx, 6 * self.ctx)


def send(value, pairs):
    return lax.ppermute(value, AXES, pairs)


def tie(*values):
    return lax.optimization_barrier(values)


def line_inward(value, plan, kind):
    total = value.astype(F32)
    for s in range(plan.half - 2):
        total = total + send(total.astype(kind), plan.line_in(s)).astype(F32)
    if plan.half == 1:
        return total, jnp.zeros_like(total, kind)
    return total, send(total.astype(kind), plan.line_in(plan.half - 2))


def line_across(held, came, plan, kind):
    sent = (held + came.astype(F32)).astype(kind)
    return sent, send(sent, plan.line_middle())


def line_joined(sent, came):
    return (sent.astype(F32) + came.astype(F32)).astype(sent.dtype)


def line_outward(total, plan, z):
    for s in reversed(range(plan.half - 1)):
        back = send(total, plan.line_out(s))
        total = jnp.where((z == s) | (z == plan.ctx - 1 - s), back, total)
    return total


def body(
    tokens_in, block_ids, w_qkv, w_out, w_in, w_down, gain_attn, gain_mlp, bias_in, bias_down,
    query_scale, cotangent,
):
    n = lax.axis_size("ctx")
    plan = Plan(lax.axis_size("dp"), n)
    half = plan.half
    z = lax.axis_index("ctx")
    core = lax.axis_index("dp") % 2
    pair = lax.axis_index("dp") // 2
    pairs = plan.dp // 2
    home = core == z // half
    rows = tokens_in.shape[1]
    width = tokens_in.shape[2]
    hd = query_scale.shape[0]
    heads = width // hd
    part = width // 2
    tile = rows // 2
    wrows = w_qkv.shape[0]
    core_swap = plan.core_swap()

    own = tokens_in[0]
    first = send(own, plan.mirror_or_turn(1))
    token0 = jnp.where(home, own, first)
    second = send(token0, plan.turn(1, True))
    mine = [token0, jnp.where(home, first, second)]
    for k in range(2, half):
        mine.append(send(token0, plan.turn(k, False)))
    theirs = [send(m, core_swap) for m in mine]
    slots = [a for both in zip(mine, theirs) for a in both]

    full_qkv = lax.all_gather(w_qkv, "dp", axis=0, tiled=True)
    at = jnp.stack([pair ^ mask for mask in range(pairs)]).astype(jnp.int32)
    core_at = core.astype(jnp.int32).reshape(1)

    ids = jnp.where(home, block_ids[0], send(block_ids[0], core_swap))
    place = lax.dynamic_index_in_dim(
        jnp.asarray(plan.places()), lax.axis_index("dp") * n + z, 0, False
    )
    col = ids.reshape(-1, 1)

    gain_one = gain_attn.astype(F32)
    gain_two = gain_mlp.astype(F32)
    scale_exp = jnp.exp(query_scale.astype(F32))
    scale_dim = SOFT_FACTOR / math.sqrt(hd) * jnp.log1p(scale_exp)
    scale_vec = jnp.tile(scale_dim, heads // 2)[:, None]
    weights = lax.all_gather(
        jnp.concatenate([w_down, w_in, w_out], 1), "dp", axis=0, tiled=True
    )
    qt, kt, vt, xt = project(
        slots, full_qkv, core_at, gain_one.reshape(1, -1), scale_vec * LOG2E
    )
    grad_low = send(tie(cotangent[0], slots[-1])[0], plan.mirror())
    onear, ofar, lse = attention_forward(ids, col, place, qt, kt, vt, hd, tile)
    onear, ofar, grad_low = tie(onear, ofar, grad_low)
    grad_low = jnp.where(home, cotangent[0], grad_low)
    o_got = send(ofar, core_swap)

    (
        output, to_keep, to_give, grad_middle, hidden_t, normed_t, grad_pre, grad_mid_low,
        grad_gain_two, grad_bin, grad_bdown,
    ) = mlp(
        onear, o_got, weights, token0, grad_low, core_at, gain_two.reshape(1, -1),
        bias_in.astype(F32).reshape(1, -1), bias_down.astype(F32).reshape(1, -1),
    )
    far = send(to_give, core_swap)
    away_output = send(output, plan.mirror())
    joined = mlp_weights(onear, o_got, hidden_t, normed_t, grad_low, grad_pre, grad_mid_low, core_at)
    early_qt, joined, far = tie(qt, joined, far)
    scattered = lax.psum_scatter(joined, "dp", scatter_dimension=0, tiled=True)

    def backward(queries, **rest):
        return attention_backward(
            ids, col, place, queries, kt, vt, to_keep, far, onear, ofar, lse, hd, tile, **rest
        )

    def to_owners(grads):
        return [send(grads[m], plan.pair_swap(m)) for m in range(1, pairs)]

    def add_up(grads, came):
        total = grads[0].astype(F32)
        for one in came:
            total = total + one.astype(F32)
        return total

    gain_row = gain_one.reshape(1, -1)
    dq_part, *late_kv = backward(early_qt)
    late_dx, gain_late = input_gradient(late_kv, (), full_qkv, slots[2:], core_at, gain_row)
    late_dx, dq_part, away_output = tie(late_dx, dq_part, away_output)
    output = jnp.where(home, output, away_output)
    late_got = [
        send(late_dx[(2 * k + 1) * rows : (2 * k + 2) * rows], core_swap) for k in range(half - 1)
    ]
    dq_part, *late_got = tie(dq_part, *late_got)
    turned = []
    for k in range(half - 1):
        mine = late_dx[2 * k * rows : (2 * k + 1) * rows].astype(F32)
        turned.append(
            send((mine + late_got[k].astype(F32)).astype(BF), plan.turn(-k - 1, False))
        )
    dqt, dk_early, dv_early, gs = backward(qt, before=dq_part, scale=scale_vec)
    dqt, dk_early, dv_early, scattered, *turned = tie(
        dqt, dk_early, dv_early, scattered, *turned
    )
    held_o, line_o = line_inward(scattered, plan, BF)
    early_kv = (dk_early, dv_early)
    grads_a = weight_gradient(xt, dqt, early_kv, late_kv, at, pairs, 0)
    later_dq, *grads_a = tie(dqt, *grads_a)
    came_a = to_owners(grads_a)
    grads_b = weight_gradient(xt, later_dq, early_kv, late_kv, at, pairs, 1)
    last_dq, line_o, *rest = tie(dqt, line_o, *came_a, *grads_b)
    came_a, grads_b = rest[: pairs - 1], rest[pairs - 1 :]
    held_o, line_o = line_across(held_o, line_o, plan, BF)
    came_b = to_owners(grads_b)
    held_a, line_a = line_inward(add_up(grads_a, came_a), plan, BF)
    dx, gain_early = input_gradient(
        early_kv, (last_dq,), full_qkv, slots[:2], core_at, gain_row
    )
    dx, gain_early, line_o, line_a, *came_b = tie(dx, gain_early, line_o, line_a, *came_b)
    got = send(dx[rows:], core_swap)
    others = line_outward(line_joined(held_o, line_o), plan, z)
    held_b, line_b = line_inward(add_up(grads_b, came_b), plan, BF)
    held_a, line_a = line_across(held_a, line_a, plan, BF)
    total = dx[:rows].astype(F32) + got.astype(F32) + grad_middle
    for one in turned:
        total = total + one.astype(F32)
    last = send(total.astype(BF), plan.mirror())

    scale_slope = SOFT_FACTOR / math.sqrt(hd) * scale_exp / (1.0 + scale_exp)
    grad_scale = jnp.sum(gs.reshape(heads // 2, hd), 0)
    grad_scale = grad_scale * scale_slope / (scale_dim * LOG2E)
    small = jnp.concatenate(
        [
            *(v.reshape(-1) for v in (gain_late + gain_early, grad_gain_two, grad_bin, grad_bdown)),
            grad_scale,
        ]
    )
    small_size = small.shape[0]
    small = jnp.pad(small, (0, -small_size % 1024)).reshape(-1, 128)
    small = small + send(small, core_swap)
    mask = 1
    while mask < pairs:
        small = small + send(small, plan.pair_swap(mask))
        mask *= 2
    line_b, line_a, small = tie(line_b, line_a, small)
    held_b, line_b = line_across(held_b, line_b, plan, BF)
    line_a = line_outward(line_joined(held_a, line_a), plan, z)

    def owned_rows(value):
        keep = lax.dynamic_slice_in_dim(value, core * wrows, wrows, 0)
        give = lax.dynamic_slice_in_dim(value, (1 - core) * wrows, wrows, 0)
        came = send(give, core_swap)
        return jnp.where(core == 0, keep, came), jnp.where(core == 0, came, keep)

    line_b, line_a, last = tie(line_b, line_a, last)
    swapped_a = owned_rows(line_a)
    line_b = line_outward(line_joined(held_b, line_b), plan, z)
    last, line_b, others, small = tie(last, line_b, others, small)
    mask = 1
    while mask < n:
        small = small + send(small, plan.line_swap(mask))
        mask *= 2
    small = small.reshape(-1)
    grad_tokens = jnp.where(home, total, last.astype(F32))
    others = others.astype(F32)
    swapped = (swapped_a, owned_rows(line_b))
    size = part // 2
    owned_qkv = jnp.concatenate(
        [
            swapped[g][c][:, which * size : (which + 1) * size]
            for which in (2, 0, 1)
            for c in range(2)
            for g in range(2)
        ],
        1,
    ).astype(F32)

    return (
        output[None],
        grad_tokens[None],
        owned_qkv,
        others[:, 2 * width :],
        others[:, width : 2 * width],
        others[:, :width],
        small[:width],
        small[width : 2 * width],
        small[2 * width : 3 * width],
        small[3 * width : 4 * width],
        small[4 * width : small_size],
    )


def solution(mesh):
    split = P("dp", "ctx", None)
    weight = P("dp", None)
    return jax.shard_map(
        body,
        mesh=mesh,
        in_specs=(split, weight, weight, weight, weight, weight, P(), P(), P(), P(), P(), split),
        out_specs=(split, split, weight, weight, weight, weight, P(), P(), P(), P(), P()),
        check_vma=False,
    )
```

```python
import functools
import math

import jax
import jax.numpy as jnp
import numpy as np
from jax import lax
from jax.experimental import pallas as pl
from jax.experimental.pallas import tpu as pltpu
from jax.sharding import PartitionSpec as P

EPSILON = 1e-06
SOFT_FACTOR = 1.442695041
LOG2E = 1.4426950408889634
MASKED = -1e30
HEADS_AT_ONCE = 4
COST = 1.0
AXES = ("dp", "ctx")
BF = jnp.bfloat16
F32 = jnp.float32


def nn(a, b):
    return lax.dot_general(a, b, (((1,), (0,)), ((), ())), preferred_element_type=F32)


def nt(a, b):
    return lax.dot_general(a, b, (((1,), (1,)), ((), ())), preferred_element_type=F32)


def tile_counts(ids_ref, stretch, tile, tiles):
    low = ids_ref[stretch * tile]
    high = ids_ref[stretch * tile + tile - 1]
    full = jnp.int32(0)
    need = jnp.int32(0)
    for t in range(tiles):
        full += (ids_ref[t * tile + tile - 1] <= low).astype(jnp.int32)
        need += (ids_ref[t * tile] <= high).astype(jnp.int32)
    return full, need


def project_kernel(part, query_slots, n, core_ref, gain_ref, scale_ref, *refs):
    x_refs, w_refs = refs[:n], refs[n : n + 3]
    qt_ref, kt_ref, vt_ref, xt_ref, wt, xs = refs[n + 3 :]
    i = pl.program_id(0)

    @pl.when(i == 0)
    def _():
        for j, ref in enumerate(w_refs):
            wt[j * part : (j + 1) * part, :] = ref[...].T

    for s in range(n):

        @pl.when(i == s)
        def _(s=s):
            xs[...] = x_refs[s][...]

    x = xs[...].astype(F32)
    inverse = lax.rsqrt(jnp.mean(x * x, -1, keepdims=True) + EPSILON)
    xt_ref[...] = (x * inverse * gain_ref[...]).astype(BF).T
    kt_ref[...] = nn(wt[part : 2 * part, :], xt_ref[...]).astype(BF)
    vt_ref[...] = nn(wt[2 * part :, :], xt_ref[...]).astype(BF)

    @pl.when(i < query_slots)
    def _():
        qt_ref[...] = (nn(wt[:part, :], xt_ref[...]) * scale_ref[...]).astype(BF)


def project(slots, w_full, core, gain, scale):
    n = len(slots)
    rows, width = slots[0].shape
    part = width // 2
    query_slots = 2
    once = pl.Buffered(1)
    return pl.pallas_call(
        functools.partial(project_kernel, part, query_slots, n),
        grid_spec=pltpu.PrefetchScalarGridSpec(
            num_scalar_prefetch=1,
            grid=(n,),
            in_specs=[
                pl.BlockSpec((1, width), lambda i, c: (0, 0)),
                pl.BlockSpec((part, 1), lambda i, c: (0, 0)),
                *[pl.BlockSpec((rows, width), lambda i, c: (0, 0), pipeline_mode=once)] * n,
                *[
                    pl.BlockSpec(
                        (width, part), lambda i, c, j=j: (0, 2 * j + c[0]), pipeline_mode=once
                    )
                    for j in range(3)
                ],
            ],
            out_specs=[
                pl.BlockSpec((part, rows), lambda i, c: (0, jnp.minimum(i, query_slots - 1))),
                pl.BlockSpec((part, rows), lambda i, c: (0, i)),
                pl.BlockSpec((part, rows), lambda i, c: (0, i)),
                pl.BlockSpec((width, rows), lambda i, c: (0, i)),
            ],
            scratch_shapes=[pltpu.VMEM((3 * part, width), BF), pltpu.VMEM((rows, width), BF)],
        ),
        out_shape=[
            jax.ShapeDtypeStruct((part, query_slots * rows), BF),
            jax.ShapeDtypeStruct((part, n * rows), BF),
            jax.ShapeDtypeStruct((part, n * rows), BF),
            jax.ShapeDtypeStruct((width, n * rows), BF),
        ],
        compiler_params=pltpu.CompilerParams(vmem_limit_bytes=60 << 20),
        cost_estimate=pl.CostEstimate(
            flops=int(COST * 2 * width * part * rows * (2 * n + query_slots)),
            bytes_accessed=1 << 16,
            transcendentals=0,
        ),
        name="project",
    )(core, gain, scale, *slots, *[w_full] * 3)


def mlp_kernel(
    part, core_ref, near_ref, far_ref, w_ref, x_ref, cot_ref, gain_ref, bin_ref, bdown_ref, out_ref, keep_ref, give_ref,
    gmid_ref, ht_ref, nt_ref, gpre_ref, gml_ref, gain_out, bin_out, bdown_out, middle, normed,
    hidden, slope, g_ref,
):
    width = x_ref.shape[1]
    step = width // 5
    chunks = [slice(c * step, (c + 1) * step) for c in range(5)]
    down, inner, outer = 0, width, 2 * width
    core = core_ref[0]
    near_rows = pl.ds(pl.multiple_of(core * part, part), part)
    far_rows = pl.ds(pl.multiple_of((1 - core) * part, part), part)

    @pl.when(pl.program_id(0) == 0)
    def _():
        for ref in (gain_out, bin_out, bdown_out):
            ref[...] = jnp.zeros(ref.shape, F32)

    near, far = near_ref[...].T, far_ref[...].T
    for cols in chunks:
        at = slice(outer + cols.start, outer + cols.stop)
        middle[:, cols] = (
            x_ref[:, cols].astype(F32) + nn(near, w_ref[near_rows, at]) + nn(far, w_ref[far_rows, at])
        )
    mid = middle[...]
    inverse = lax.rsqrt(jnp.mean(mid * mid, -1, keepdims=True) + EPSILON)
    normed[...] = (mid * inverse * gain_ref[...]).astype(BF)
    nt_ref[...] = normed[...].T
    for cols in chunks:
        at = slice(inner + cols.start, inner + cols.stop)
        pre = nn(normed[...], w_ref[:, at]) + bin_ref[:, cols]
        sigma = 1.0 / (1.0 + jnp.exp(-pre))
        hidden[:, cols] = (pre * sigma).astype(BF)
        slope[:, cols] = sigma * (1.0 + pre * (1.0 - sigma))
    ht_ref[...] = hidden[...].T
    for cols in chunks:
        at = slice(down + cols.start, down + cols.stop)
        out_ref[:, cols] = (
            middle[:, cols] + nn(hidden[...], w_ref[:, at]) + bdown_ref[:, cols]
        ).astype(BF)
    for cols in chunks:
        gpre_ref[:, cols] = (
            nt(cot_ref[...], w_ref[cols, down : down + width]) * slope[:, cols]
        ).astype(BF)
    for cols in chunks:
        g_ref[:, cols] = nt(gpre_ref[...], w_ref[cols, inner : inner + width])
    bin_out[...] += jnp.sum(gpre_ref[...].astype(F32), 0, keepdims=True)
    cot = cot_ref[...].astype(F32)
    bdown_out[...] += jnp.sum(cot, 0, keepdims=True)
    turned = middle[...] * inverse
    gn = g_ref[...] * turned
    gain_out[...] += jnp.sum(gn, 0, keepdims=True)
    mean = jnp.mean(gn * gain_ref[...], -1, keepdims=True)
    gmid = cot + inverse * (g_ref[...] * gain_ref[...] - turned * mean)
    gmid_ref[...] = gmid
    gml_ref[...] = gmid.astype(BF)
    low = gml_ref[...]
    keep_ref[...] = nt(w_ref[near_rows, outer : outer + width], low).astype(BF)
    give_ref[...] = nt(w_ref[far_rows, outer : outer + width], low).astype(BF)


def mlp(near, far, weights, x, cot, core, gain, bias_in, bias_down):
    part, rows = far.shape
    width = x.shape[1]
    tile = 256
    once = pl.Buffered(1)
    row = pl.BlockSpec((tile, width), lambda i, c: (i, 0))
    feature = pl.BlockSpec((part, tile), lambda i, c: (0, i))
    wide = pl.BlockSpec((width, tile), lambda i, c: (0, i))
    vector = pl.BlockSpec((1, width), lambda i, c: (0, 0))
    return pl.pallas_call(
        functools.partial(mlp_kernel, part),
        grid_spec=pltpu.PrefetchScalarGridSpec(
            num_scalar_prefetch=1,
            grid=(rows // tile,),
            in_specs=[
                feature,
                feature,
                pl.BlockSpec(weights.shape, lambda i, c: (0, 0), pipeline_mode=once),
                row, row, vector, vector, vector,
            ],
            out_specs=[
                row, feature, feature, row, wide, wide, row, row, vector, vector, vector
            ],
            scratch_shapes=[
                pltpu.VMEM((tile, width), F32),
                pltpu.VMEM((tile, width), BF),
                pltpu.VMEM((tile, width), BF),
                pltpu.VMEM((tile, width), F32),
                pltpu.VMEM((tile, width), F32),
            ],
        ),
        out_shape=[
            jax.ShapeDtypeStruct((rows, width), BF),
            jax.ShapeDtypeStruct((part, rows), BF),
            jax.ShapeDtypeStruct((part, rows), BF),
            jax.ShapeDtypeStruct((rows, width), F32),
            jax.ShapeDtypeStruct((width, rows), BF),
            jax.ShapeDtypeStruct((width, rows), BF),
            jax.ShapeDtypeStruct((rows, width), BF),
            jax.ShapeDtypeStruct((rows, width), BF),
            jax.ShapeDtypeStruct((1, width), F32),
            jax.ShapeDtypeStruct((1, width), F32),
            jax.ShapeDtypeStruct((1, width), F32),
        ],
        compiler_params=pltpu.CompilerParams(vmem_limit_bytes=60 << 20),
        cost_estimate=pl.CostEstimate(
            flops=int(COST * 12 * rows * width * width), bytes_accessed=1 << 16, transcendentals=0
        ),
        name="mlp",
    )(core, near, far, weights, x, cot, gain, bias_in, bias_down)


def mlp_weight_kernel(
    core_ref, near_ref, far_ref, ht_ref, nt_ref, cot_ref, gpre_ref, gml_ref, out_ref
):
    which, part_at = pl.program_id(0), pl.program_id(1)

    @pl.when(which == 0)
    def _():
        out_ref[...] = nn(ht_ref[...], cot_ref[...]).astype(BF)

    @pl.when(which == 1)
    def _():
        out_ref[...] = nn(nt_ref[...], gpre_ref[...]).astype(BF)

    @pl.when((which == 2) & (part_at == core_ref[0]))
    def _():
        out_ref[...] = nn(near_ref[...], gml_ref[...]).astype(BF)

    @pl.when((which == 2) & (part_at != core_ref[0]))
    def _():
        out_ref[...] = nn(far_ref[...], gml_ref[...]).astype(BF)


def mlp_weights(near, far, ht, nrt, cot, gpre, gml, core):
    part, rows = far.shape
    width = cot.shape[1]
    once = pl.Buffered(1)

    def whole(shape):
        return pl.BlockSpec(shape, lambda j, r, c: (0,) * len(shape), pipeline_mode=once)

    return pl.pallas_call(
        mlp_weight_kernel,
        grid_spec=pltpu.PrefetchScalarGridSpec(
            num_scalar_prefetch=1,
            grid=(3, 2),
            in_specs=[
                whole((part, rows)),
                whole((part, rows)),
                pl.BlockSpec((part, rows), lambda j, r, c: (jnp.where(j == 0, r, 1), 0)),
                pl.BlockSpec((part, rows), lambda j, r, c: (jnp.where(j == 1, r, j // 2), 0)),
                whole((rows, width)),
                whole((rows, width)),
                whole((rows, width)),
            ],
            out_specs=pl.BlockSpec((part, width), lambda j, r, c: (r, j)),
        ),
        out_shape=jax.ShapeDtypeStruct((width, 3 * width), BF),
        compiler_params=pltpu.CompilerParams(vmem_limit_bytes=60 << 20),
        cost_estimate=pl.CostEstimate(
            flops=6 * rows * width * width, bytes_accessed=20 << 20, transcendentals=0
        ),
        name="mlp_weights",
    )(core, near, far, ht, nrt, cot, gpre, gml)


def load_keys(ref, place_ref, hd, tile, group, knat, kt=None):
    tiles = ref.shape[1] // tile
    for b in range(tiles):
        stretch = place_ref[tiles + b]
        piece = ref[:, b * tile : (b + 1) * tile]
        if kt is not None:
            kt[stretch] = piece
        if knat is not None:
            for h in range(group):
                knat[h, stretch] = piece[h * hd : (h + 1) * hd, :].T


def forward_kernel(
    hd, tile, ids_ref, place_ref, row_ref, col_ref, qt_ref, kt_ref, vt_ref, near_ref, far_ref,
    lse_ref, knat, vt, acc, m_ref, l_ref,
):
    group = qt_ref.shape[0] // hd
    tiles = vt.shape[0]
    load_keys(kt_ref, place_ref, hd, tile, group, knat)
    load_keys(vt_ref, place_ref, hd, tile, group, None, vt)
    per_half = near_ref.shape[1] // tile

    def one_tile(qi, carry):
        stretch = place_ref[tiles + qi]
        full, need = tile_counts(ids_ref, stretch, tile, tiles)
        qcol = pl.ds(pl.multiple_of(qi * tile, tile), tile)
        qpos = pl.ds(pl.multiple_of(stretch * tile, tile), tile)
        m_ref[...] = jnp.full(m_ref.shape, MASKED, F32)
        l_ref[...] = jnp.zeros(l_ref.shape, F32)
        acc[...] = jnp.zeros(acc.shape, F32)

        def step(ts, masked):
            if masked:
                allowed = [
                    col_ref[pl.ds(pl.multiple_of(t * tile, tile), tile), :] <= row_ref[:, qpos]
                    for t in ts
                ]
            scores = [
                [nn(knat[h, t], qt_ref[h * hd : (h + 1) * hd, qcol]) for t in ts]
                for h in range(group)
            ]
            for h in range(group):
                s = scores[h]
                if masked:
                    s = [jnp.where(ok, one, MASKED) for ok, one in zip(allowed, s)]
                old = m_ref[h]
                new = old
                for one in s:
                    new = jnp.maximum(new, jnp.max(one, 0, keepdims=True))
                p = [jnp.exp2(one - new) for one in s]
                alpha = jnp.exp2(old - new)
                total = l_ref[h] * alpha
                for one in p:
                    total = total + jnp.sum(one, 0, keepdims=True)
                l_ref[h] = total
                m_ref[h] = new
                out = acc[h] * alpha
                for t, one in zip(ts, p):
                    out = out + nn(vt[t, h * hd : (h + 1) * hd, :], one.astype(BF))
                acc[h] = out

        def full_step(i, c):
            step([2 * i, 2 * i + 1], False)
            return c

        def mask_step(i, c):
            step([2 * i, 2 * i + 1], True)
            return c

        lax.fori_loop(0, full // 2, full_step, 0)
        lax.fori_loop(full // 2, (need + 1) // 2, mask_step, 0)
        inner = pl.ds(pl.multiple_of((qi % per_half) * tile, tile), tile)
        for half, ref in enumerate((near_ref, far_ref)):

            @pl.when(qi // per_half == half)
            def _(ref=ref):
                for h in range(group):
                    ref[h * hd : (h + 1) * hd, inner] = (acc[h] / l_ref[h]).astype(BF)

        for h in range(group):
            lse_ref[h, :, qcol] = m_ref[h] + jnp.log2(l_ref[h])
        return carry

    lax.fori_loop(0, qt_ref.shape[1] // tile, one_tile, 0)


def backward_kernel(hd, tile, base, count, first, last, *refs):
    ids_ref, place_ref, row_ref, col_ref, qt_ref, kt_ref, vt_ref = refs[:7]
    near_ref, far_ref, onear_ref, ofar_ref, lse_ref = refs[7:12]
    if last:
        before_ref, scale_ref, dqt_ref, dkt_ref, dvt_ref, gs_ref = refs[12:18]
        knat, vnat, kt, dq, dk, dv, delta, dot = refs[18:]
    else:
        dqt_ref, dkt_ref, dvt_ref = refs[12:15]
        knat, vnat, kt, dq, dk, dv, delta, dot = refs[15:]
    tiles = kt_ref.shape[1] // tile
    group = qt_ref.shape[0] // hd

    def block_of(i):
        return pl.multiple_of(place_ref[place_ref[base + i]] * tile, tile)

    for i in range(count):
        cols = pl.ds(block_of(i), tile)
        kt[i] = kt_ref[:, cols]
        for h in range(group):
            hs = slice(h * hd, (h + 1) * hd)
            knat[h, i] = kt_ref[hs, cols].T
            vnat[h, i] = vt_ref[hs, cols].T
    per_half = near_ref.shape[1] // tile
    for half, (ref, o_ref) in enumerate(((near_ref, onear_ref), (far_ref, ofar_ref))):
        for b in range(per_half):
            cols = slice(b * tile, (b + 1) * tile)
            dot[half * per_half + b] = ref[:, cols]
            product = ref[:, cols].astype(F32) * o_ref[:, cols].astype(F32)
            for h in range(group):
                delta[half * per_half + b, h] = jnp.sum(
                    product[h * hd : (h + 1) * hd], 0, keepdims=True
                )
    dk[...] = jnp.zeros(dk.shape, F32)
    dv[...] = jnp.zeros(dv.shape, F32)
    if last:
        gs_ref[...] = jnp.zeros(gs_ref.shape, F32)

    def one_tile(qi, carry):
        stretch = place_ref[tiles + qi]
        low = ids_ref[stretch * tile]
        high = ids_ref[stretch * tile + tile - 1]
        full = jnp.int32(0)
        need = jnp.int32(0)
        for i in range(count):
            t = place_ref[base + i]
            full += (ids_ref[t * tile + tile - 1] <= low).astype(jnp.int32)
            need += (ids_ref[t * tile] <= high).astype(jnp.int32)
        qcol = pl.ds(pl.multiple_of(qi * tile, tile), tile)
        qpos = pl.ds(pl.multiple_of(stretch * tile, tile), tile)
        dq[...] = before_ref[:, qcol] if last else jnp.zeros(dq.shape, F32)

        def step(ts, masked):
            if masked:
                allowed = [
                    col_ref[pl.ds(pl.multiple_of(place_ref[base + t] * tile, tile), tile), :]
                    <= row_ref[:, qpos]
                    for t in ts
                ]

            def scores(h, t):
                hs = slice(h * hd, (h + 1) * hd)
                return nn(knat[h, t], qt_ref[hs, qcol]), nn(vnat[h, t], dot[qi, hs, :])

            order = [(h, i) for h in range(group) for i in range(len(ts))]
            ahead = scores(0, ts[0])
            for j, (h, i) in enumerate(order):
                hs = slice(h * hd, (h + 1) * hd)
                t = ts[i]
                s, dp = ahead
                if j + 1 < len(order):
                    ahead = scores(order[j + 1][0], ts[order[j + 1][1]])
                if masked:
                    s = jnp.where(allowed[i], s, MASKED)
                p = jnp.exp2(s - lse_ref[h, :, qcol])
                ds = (p * (dp - delta[qi, h])).astype(BF)
                dv[t, hs, :] += nt(dot[qi, hs, :], p.astype(BF))
                dk[t, hs, :] += nt(qt_ref[hs, qcol], ds)
                dq[hs, :] += nn(kt[t, hs, :], ds)

        def full_step(i, c):
            step([2 * i, 2 * i + 1], False)
            return c

        def mask_step(i, c):
            step([2 * i, 2 * i + 1], True)
            return c

        lax.fori_loop(0, full // 2, full_step, 0)
        lax.fori_loop(full // 2, (need + 1) // 2, mask_step, 0)
        if last:
            gs_ref[...] += jnp.sum(dq[...] * qt_ref[:, qcol].astype(F32), 1, keepdims=True)
            dqt_ref[:, qcol] = (dq[...] * scale_ref[...]).astype(BF)
        else:
            dqt_ref[:, qcol] = dq[...]
        return carry

    lax.fori_loop(0, qt_ref.shape[1] // tile, one_tile, 0)
    for i in range(count):
        cols = pl.ds(pl.multiple_of(block_of(i) - first * tile, tile), tile)
        dkt_ref[:, cols] = (dk[i] * (1.0 / LOG2E)).astype(BF)
        dvt_ref[:, cols] = dv[i].astype(BF)


def attention_specs(nq, nk, hd, group, at):
    size = group * hd
    return (
        [
            pl.BlockSpec(memory_space=pltpu.SMEM),
            pl.BlockSpec(memory_space=pltpu.SMEM),
            pl.BlockSpec((1, nk), lambda i: (0, 0)),
            pl.BlockSpec((nk, 1), lambda i: (0, 0)),
            pl.BlockSpec((size, nq), lambda i: (i + at, 0)),
            pl.BlockSpec((size, nk), lambda i: (i + at, 0)),
            pl.BlockSpec((size, nk), lambda i: (i + at, 0)),
        ],
        pl.BlockSpec((size, nq // 2), lambda i: (i + at, 0)),
        pl.BlockSpec((group, 1, nq), lambda i: (i + at, 0, 0)),
    )


def attention_forward(ids, col, place, qt, kt, vt, hd, tile):
    heads = qt.shape[0] // hd
    nq, nk = qt.shape[1], kt.shape[1]
    group = HEADS_AT_ONCE
    common, halves, rows = attention_specs(nq, nk, hd, group, 0)
    pairs = heads * nq * nk * 0.6
    return pl.pallas_call(
        functools.partial(forward_kernel, hd, tile),
        grid=(heads // group,),
        in_specs=common,
        out_specs=[halves, halves, rows],
        out_shape=[
            jax.ShapeDtypeStruct((heads * hd, nq // 2), BF),
            jax.ShapeDtypeStruct((heads * hd, nq // 2), BF),
            jax.ShapeDtypeStruct((heads, 1, nq), F32),
        ],
        scratch_shapes=[
            pltpu.VMEM((group, nk // tile, tile, hd), BF),
            pltpu.VMEM((nk // tile, group * hd, tile), BF),
            pltpu.VMEM((group, hd, tile), F32),
            pltpu.VMEM((group, 1, tile), F32),
            pltpu.VMEM((group, 1, tile), F32),
        ],
        compiler_params=pltpu.CompilerParams(vmem_limit_bytes=60 << 20),
        cost_estimate=pl.CostEstimate(
            flops=int(COST * pairs * 1024), bytes_accessed=1 << 16, transcendentals=int(COST * pairs)
        ),
        name="attention_forward",
    )(ids, place, ids.reshape(1, -1), col, qt, kt, vt)


def attention_backward(
    ids, col, place, qt, kt, vt, near, far, onear, ofar, lse, hd, tile, before=None, scale=None
):
    heads = qt.shape[0] // hd
    nq, nk = qt.shape[1], kt.shape[1]
    group = HEADS_AT_ONCE
    size = group * hd
    last = before is not None
    early = nq // tile
    tiles = nk // tile
    count, first = (early, 0) if last else (tiles - early, early)
    base = 2 * tiles + (0 if last else early)
    common, halves, rows = attention_specs(nq, nk, hd, group, 0)
    wide = pl.BlockSpec((size, nq), lambda i: (i, 0))
    keys = pl.BlockSpec((size, count * tile), lambda i: (i, 0))
    one = pl.BlockSpec((size, 1), lambda i: (i, 0))
    pairs = heads * nq * count * tile * 0.6
    return pl.pallas_call(
        functools.partial(backward_kernel, hd, tile, base, count, first, last),
        grid=(heads // group,),
        in_specs=[*common, halves, halves, halves, halves, rows, *([wide, one] if last else [])],
        out_specs=[wide, keys, keys, *([one] if last else [])],
        out_shape=[
            jax.ShapeDtypeStruct((heads * hd, nq), BF if last else F32),
            jax.ShapeDtypeStruct((heads * hd, count * tile), BF),
            jax.ShapeDtypeStruct((heads * hd, count * tile), BF),
            *([jax.ShapeDtypeStruct((heads * hd, 1), F32)] if last else []),
        ],
        scratch_shapes=[
            pltpu.VMEM((group, count, tile, hd), BF),
            pltpu.VMEM((group, count, tile, hd), BF),
            pltpu.VMEM((count, size, tile), BF),
            pltpu.VMEM((size, tile), F32),
            pltpu.VMEM((count, size, tile), F32),
            pltpu.VMEM((count, size, tile), F32),
            pltpu.VMEM((nq // tile, group, 1, tile), F32),
            pltpu.VMEM((nq // tile, size, tile), BF),
        ],
        compiler_params=pltpu.CompilerParams(vmem_limit_bytes=60 << 20),
        cost_estimate=pl.CostEstimate(
            flops=int(pairs * 2560), bytes_accessed=16 << 20, transcendentals=int(pairs)
        ),
        name="attention_backward",
    )(
        ids, place, ids.reshape(1, -1), col, qt, kt, vt, near, far, onear, ofar, lse,
        *([before, scale] if last else []),
    )


def weight_kernel(size, nq, at_ref, xt_ref, dqt_ref, dka_ref, dva_ref, dkb_ref, dvb_ref, *out_refs):
    for m, ref in enumerate(out_refs):

        @pl.when(pl.program_id(0) == m)
        def _(ref=ref):
            early = jnp.concatenate([dka_ref[...], dva_ref[...]], 0)
            late = jnp.concatenate([dkb_ref[...], dvb_ref[...]], 0)
            ref[:, : 2 * size] = (nt(xt_ref[:, :nq], early) + nt(xt_ref[:, nq:], late)).astype(BF)
            ref[:, 2 * size :] = nt(xt_ref[:, :nq], dqt_ref[...]).astype(BF)


def weight_gradient(xt, dqt, early, late, at, pieces, which):
    width, nk = xt.shape
    part, nq = dqt.shape
    size = part // 2
    rows = width // pieces
    once = pl.Buffered(1)

    def heads(cols):
        return pl.BlockSpec((size, cols), lambda i, a: (which, 0), pipeline_mode=once)

    return pl.pallas_call(
        functools.partial(weight_kernel, size, nq),
        grid_spec=pltpu.PrefetchScalarGridSpec(
            num_scalar_prefetch=1,
            grid=(pieces,),
            in_specs=[
                pl.BlockSpec((rows, nk), lambda i, a: (a[i], 0)),
                heads(nq), heads(nq), heads(nq), heads(nk - nq), heads(nk - nq),
            ],
            out_specs=[pl.BlockSpec((rows, 3 * size), lambda i, a: (0, 0))] * pieces,
        ),
        out_shape=[jax.ShapeDtypeStruct((rows, 3 * size), BF)] * pieces,
        compiler_params=pltpu.CompilerParams(vmem_limit_bytes=60 << 20),
        cost_estimate=pl.CostEstimate(
            flops=2 * width * size * (2 * nk + nq), bytes_accessed=12 << 20, transcendentals=0
        ),
        name="weight_gradient",
    )(at, xt, dqt, *early, *late)


def dx_kernel(part, queries, n, core_ref, *refs):
    dk_ref, dv_ref, wk_ref, wv_ref, gain_ref = refs[:5]
    x_refs = refs[5 : 5 + n]
    rest = refs[5 + n :]
    if queries:
        dq_ref, wq_ref = rest[:2]
        rest = rest[2:]
    dx_refs, (gg_ref, g_ref, xs) = rest[:n], rest[n:]
    i = pl.program_id(0)
    tile, width = xs.shape
    step = width // 5
    dk = dk_ref[...].T
    dv = dv_ref[...].T
    if queries:
        dq = dq_ref[...].T
    for c in range(5):
        cols = slice(c * step, (c + 1) * step)
        g = nt(dk, wk_ref[cols, :]) + nt(dv, wv_ref[cols, :])
        if queries:
            g = g + nt(dq, wq_ref[cols, :])
        g_ref[:, cols] = g

    @pl.when(i == 0)
    def _():
        gg_ref[...] = jnp.zeros(gg_ref.shape, F32)

    per_slot = x_refs[0].shape[0] // tile
    for s in range(n):

        @pl.when(i // per_slot == s)
        def _(s=s):
            xs[...] = x_refs[s][pl.ds(pl.multiple_of((i % per_slot) * tile, tile), tile), :]

    x = xs[...].astype(F32)
    inverse = lax.rsqrt(jnp.mean(x * x, -1, keepdims=True) + EPSILON)
    normed = x * inverse
    g = g_ref[...]
    gn = g * normed
    gg_ref[...] += jnp.sum(gn, 0, keepdims=True)
    scaled = g * gain_ref[...]
    mean = jnp.mean(gn * gain_ref[...], -1, keepdims=True)
    out = (inverse * (scaled - normed * mean)).astype(BF)
    for s in range(n):

        @pl.when(i // per_slot == s)
        def _(s=s):
            dx_refs[s][...] = out


def input_gradient(dkvs, dqs, w_full, slots, core, gain):
    part = dkvs[0].shape[0]
    n = len(slots)
    rows, width = slots[0].shape
    tile = 256
    per_slot = rows // tile
    once = pl.Buffered(1)
    dkv = pl.BlockSpec((part, tile), lambda i, c: (0, i))

    def weight(j):
        return pl.BlockSpec(
            (width, part), lambda i, c, j=j: (0, 2 * j + c[0]), pipeline_mode=once
        )

    specs = [
        dkv, dkv, weight(1), weight(2), pl.BlockSpec((1, width), lambda i, c: (0, 0)),
        *[pl.BlockSpec((rows, width), lambda i, c: (0, 0), pipeline_mode=once)] * n,
    ]
    operands = [*dkvs, w_full, w_full, gain, *slots]
    if dqs:
        specs += [dkv, weight(0)]
        operands += [*dqs, w_full]
    return pl.pallas_call(
        functools.partial(dx_kernel, part, bool(dqs), n),
        grid_spec=pltpu.PrefetchScalarGridSpec(
            num_scalar_prefetch=1,
            grid=(n * rows // tile,),
            in_specs=specs,
            out_specs=[
                *[
                    pl.BlockSpec(
                        (tile, width),
                        lambda i, c, s=s: (jnp.clip(i - s * per_slot, 0, per_slot - 1), 0),
                    )
                    for s in range(n)
                ],
                pl.BlockSpec((1, width), lambda i, c: (0, 0)),
            ],
            scratch_shapes=[pltpu.VMEM((tile, width), F32), pltpu.VMEM((tile, width), BF)],
        ),
        out_shape=[
            *[jax.ShapeDtypeStruct((rows, width), BF)] * n,
            jax.ShapeDtypeStruct((1, width), F32),
        ],
        compiler_params=pltpu.CompilerParams(vmem_limit_bytes=60 << 20),
        cost_estimate=pl.CostEstimate(
            flops=int(COST * 2 * width * n * rows * part * (3 if dqs else 2)),
            bytes_accessed=1 << 16,
            transcendentals=0,
        ),
        name="input_gradient",
    )(core, *operands)


class Plan:
    def __init__(self, dp, ctx):
        self.dp, self.ctx = dp, ctx
        self.half = ctx // 2

    def index(self, pair, core, z):
        return (pair * 2 + core) * self.ctx + z

    def perm(self, to):
        out = []
        for d in range(self.dp):
            for z in range(self.ctx):
                got = to(d // 2, d % 2, z)
                if got is not None:
                    out.append((self.index(d // 2, d % 2, z), self.index(*got)))
        return out

    def home(self, core, z):
        return core == z // self.half

    def turned(self, z, k):
        first = z // self.half * self.half
        return first + (z - first + k) % self.half

    def core_swap(self):
        return self.perm(lambda p, c, z: (p, 1 - c, z))

    def pair_swap(self, mask):
        return self.perm(lambda p, c, z: (p ^ mask, c, z))

    def line_swap(self, mask):
        return self.perm(lambda p, c, z: (p, c, z ^ mask))

    def line_in(self, s):
        last = self.ctx - 1
        to = {s: s + 1, last - s: last - s - 1}
        return self.perm(lambda p, c, z: (p, c, to[z]) if z in to else None)

    def line_out(self, s):
        last = self.ctx - 1
        to = {s + 1: s, last - s - 1: last - s}
        return self.perm(lambda p, c, z: (p, c, to[z]) if z in to else None)

    def line_middle(self):
        to = {self.half - 1: self.half, self.half: self.half - 1}
        return self.perm(lambda p, c, z: (p, c, to[z]) if z in to else None)

    def mirror(self):
        return self.perm(
            lambda p, c, z: None if self.home(c, z) else (p, 1 - c, self.ctx - 1 - z)
        )

    def mirror_or_turn(self, k):
        return self.perm(
            lambda p, c, z: (p, c, self.turned(z, k))
            if self.home(c, z)
            else (p, 1 - c, self.ctx - 1 - z)
        )

    def turn(self, k, away_only):
        return self.perm(
            lambda p, c, z: None
            if away_only and self.home(c, z)
            else (p, c, self.turned(z, k))
        )

    def shard(self, core, z, k, mine):
        chip = self.turned(z, -k)
        at_home = self.home(core, z) if mine else not self.home(core, z)
        return chip if at_home else self.ctx - 1 - chip

    def places(self):
        table = np.zeros((self.dp, self.ctx, 6 * self.ctx), np.int32)
        for d in range(self.dp):
            for z in range(self.ctx):
                slots = [
                    self.shard(d % 2, z, k, mine) for k in range(self.half) for mine in (True, False)
                ]
                stretches = [s for shard in slots for s in (shard, 2 * self.ctx - 1 - shard)]
                for block, stretch in enumerate(stretches):
                    table[d, z, stretch] = block
                    table[d, z, 2 * self.ctx + block] = stretch
                table[d, z, 4 * self.ctx :] = sorted(stretches[:4]) + sorted(stretches[4:])
        return table.reshape(self.dp * self.ctx, 6 * self.ctx)


def send(value, pairs):
    return lax.ppermute(value, AXES, pairs)


def tie(*values):
    return lax.optimization_barrier(values)


def line_inward(value, plan, kind):
    total = value.astype(F32)
    for s in range(plan.half - 2):
        total = total + send(total.astype(kind), plan.line_in(s)).astype(F32)
    if plan.half == 1:
        return total, jnp.zeros_like(total, kind)
    return total, send(total.astype(kind), plan.line_in(plan.half - 2))


def line_across(held, came, plan, kind):
    sent = (held + came.astype(F32)).astype(kind)
    return sent, send(sent, plan.line_middle())


def line_joined(sent, came):
    return (sent.astype(F32) + came.astype(F32)).astype(sent.dtype)


def line_outward(total, plan, z):
    for s in reversed(range(plan.half - 1)):
        back = send(total, plan.line_out(s))
        total = jnp.where((z == s) | (z == plan.ctx - 1 - s), back, total)
    return total


def body(
    tokens_in, block_ids, w_qkv, w_out, w_in, w_down, gain_attn, gain_mlp, bias_in, bias_down,
    query_scale, cotangent,
):
    n = lax.axis_size("ctx")
    plan = Plan(lax.axis_size("dp"), n)
    half = plan.half
    z = lax.axis_index("ctx")
    core = lax.axis_index("dp") % 2
    pair = lax.axis_index("dp") // 2
    pairs = plan.dp // 2
    home = core == z // half
    rows = tokens_in.shape[1]
    width = tokens_in.shape[2]
    hd = query_scale.shape[0]
    heads = width // hd
    part = width // 2
    tile = rows // 2
    wrows = w_qkv.shape[0]
    core_swap = plan.core_swap()

    own = tokens_in[0]
    first = send(own, plan.mirror_or_turn(1))
    token0 = jnp.where(home, own, first)
    second = send(token0, plan.turn(1, True))
    mine = [token0, jnp.where(home, first, second)]
    for k in range(2, half):
        mine.append(send(token0, plan.turn(k, False)))
    theirs = [send(m, core_swap) for m in mine]
    slots = [a for both in zip(mine, theirs) for a in both]

    full_qkv = lax.all_gather(w_qkv, "dp", axis=0, tiled=True)
    at = jnp.stack([pair ^ mask for mask in range(pairs)]).astype(jnp.int32)
    core_at = core.astype(jnp.int32).reshape(1)

    ids = jnp.where(home, block_ids[0], send(block_ids[0], core_swap))
    place = lax.dynamic_index_in_dim(
        jnp.asarray(plan.places()), lax.axis_index("dp") * n + z, 0, False
    )
    col = ids.reshape(-1, 1)

    gain_one = gain_attn.astype(F32)
    gain_two = gain_mlp.astype(F32)
    scale_exp = jnp.exp(query_scale.astype(F32))
    scale_dim = SOFT_FACTOR / math.sqrt(hd) * jnp.log1p(scale_exp)
    scale_vec = jnp.tile(scale_dim, heads // 2)[:, None]
    weights = lax.all_gather(
        jnp.concatenate([w_down, w_in, w_out], 1), "dp", axis=0, tiled=True
    )
    qt, kt, vt, xt = project(
        slots, full_qkv, core_at, gain_one.reshape(1, -1), scale_vec * LOG2E
    )
    grad_low = send(tie(cotangent[0], slots[-1])[0], plan.mirror())
    onear, ofar, lse = attention_forward(ids, col, place, qt, kt, vt, hd, tile)
    onear, ofar, grad_low = tie(onear, ofar, grad_low)
    grad_low = jnp.where(home, cotangent[0], grad_low)
    o_got = send(ofar, core_swap)

    (
        output, to_keep, to_give, grad_middle, hidden_t, normed_t, grad_pre, grad_mid_low,
        grad_gain_two, grad_bin, grad_bdown,
    ) = mlp(
        onear, o_got, weights, token0, grad_low, core_at, gain_two.reshape(1, -1),
        bias_in.astype(F32).reshape(1, -1), bias_down.astype(F32).reshape(1, -1),
    )
    far = send(to_give, core_swap)
    away_output = send(output, plan.mirror())
    joined = mlp_weights(onear, o_got, hidden_t, normed_t, grad_low, grad_pre, grad_mid_low, core_at)
    early_qt, joined, far = tie(qt, joined, far)
    scattered = lax.psum_scatter(joined, "dp", scatter_dimension=0, tiled=True)

    def backward(queries, **rest):
        return attention_backward(
            ids, col, place, queries, kt, vt, to_keep, far, onear, ofar, lse, hd, tile, **rest
        )

    def to_owners(grads):
        return [send(grads[m], plan.pair_swap(m)) for m in range(1, pairs)]

    def add_up(grads, came):
        total = grads[0].astype(F32)
        for one in came:
            total = total + one.astype(F32)
        return total

    gain_row = gain_one.reshape(1, -1)
    dq_part, *late_kv = backward(early_qt)
    *late_dx, gain_late = input_gradient(late_kv, (), full_qkv, slots[2:], core_at, gain_row)
    dq_part, away_output, *late_dx = tie(dq_part, away_output, *late_dx)
    output = jnp.where(home, output, away_output)
    late_got = [
        send(late_dx[2 * k + 1], core_swap) for k in range(half - 1)
    ]
    dq_part, *late_got = tie(dq_part, *late_got)
    turned = []
    for k in range(half - 1):
        mine = late_dx[2 * k].astype(F32)
        turned.append(
            send((mine + late_got[k].astype(F32)).astype(BF), plan.turn(-k - 1, False))
        )
    dqt, dk_early, dv_early, gs = backward(qt, before=dq_part, scale=scale_vec)
    dqt, dk_early, dv_early, scattered, *turned = tie(
        dqt, dk_early, dv_early, scattered, *turned
    )
    held_o, line_o = line_inward(scattered, plan, BF)
    early_kv = (dk_early, dv_early)
    grads_a = weight_gradient(xt, dqt, early_kv, late_kv, at, pairs, 0)
    later_dq, *grads_a = tie(dqt, *grads_a)
    came_a = to_owners(grads_a)
    near_dx, far_dx, gain_early = input_gradient(
        early_kv, (later_dq,), full_qkv, slots[:2], core_at, gain_row
    )
    near_dx, far_dx, gain_early, last_dq, line_o, *came_a = tie(
        near_dx, far_dx, gain_early, dqt, line_o, *came_a
    )
    got = send(far_dx, core_swap)
    held_a, line_a = line_inward(add_up(grads_a, came_a), plan, BF)
    held_o, line_o = line_across(held_o, line_o, plan, BF)
    grads_b = weight_gradient(xt, last_dq, early_kv, late_kv, at, pairs, 1)
    got, line_a, *grads_b = tie(got, line_a, *grads_b)
    came_b = to_owners(grads_b)
    total = near_dx.astype(F32) + got.astype(F32) + grad_middle
    for one in turned:
        total = total + one.astype(F32)
    last = send(total.astype(BF), plan.mirror())
    held_a, line_a = line_across(held_a, line_a, plan, BF)
    gain_early, line_a, line_o, *came_b = tie(gain_early, line_a, line_o, *came_b)
    held_b, line_b = line_inward(add_up(grads_b, came_b), plan, BF)
    line_a = line_outward(line_joined(held_a, line_a), plan, z)
    others = line_outward(line_joined(held_o, line_o), plan, z)

    scale_slope = SOFT_FACTOR / math.sqrt(hd) * scale_exp / (1.0 + scale_exp)
    grad_scale = jnp.sum(gs.reshape(heads // 2, hd), 0)
    grad_scale = grad_scale * scale_slope / (scale_dim * LOG2E)
    small = jnp.concatenate(
        [
            *(v.reshape(-1) for v in (gain_late + gain_early, grad_gain_two, grad_bin, grad_bdown)),
            grad_scale,
        ]
    )
    small_size = small.shape[0]
    small = jnp.pad(small, (0, -small_size % 1024)).reshape(-1, 128)
    small = small + send(small, core_swap)
    mask = 1
    while mask < pairs:
        small = small + send(small, plan.pair_swap(mask))
        mask *= 2
    line_b, line_a, small = tie(line_b, line_a, small)
    held_b, line_b = line_across(held_b, line_b, plan, BF)

    def owned_rows(value):
        keep = lax.dynamic_slice_in_dim(value, core * wrows, wrows, 0)
        give = lax.dynamic_slice_in_dim(value, (1 - core) * wrows, wrows, 0)
        came = send(give, core_swap)
        return jnp.where(core == 0, keep, came), jnp.where(core == 0, came, keep)

    line_b, line_a, last = tie(line_b, line_a, last)
    swapped_a = owned_rows(line_a)
    line_b = line_outward(line_joined(held_b, line_b), plan, z)
    line_b, others, small = tie(line_b, others, small)
    mask = 1
    while mask < n:
        small = small + send(small, plan.line_swap(mask))
        mask *= 2
    small = small.reshape(-1)
    grad_tokens = jnp.where(home, total, last.astype(F32))
    others = others.astype(F32)
    swapped = (swapped_a, owned_rows(line_b))
    size = part // 2
    owned_qkv = jnp.concatenate(
        [
            swapped[g][c][:, which * size : (which + 1) * size]
            for which in (2, 0, 1)
            for c in range(2)
            for g in range(2)
        ],
        1,
    ).astype(F32)

    return (
        output[None],
        grad_tokens[None],
        owned_qkv,
        others[:, 2 * width :],
        others[:, width : 2 * width],
        others[:, :width],
        small[:width],
        small[width : 2 * width],
        small[2 * width : 3 * width],
        small[3 * width : 4 * width],
        small[4 * width : small_size],
    )


def solution(mesh):
    split = P("dp", "ctx", None)
    weight = P("dp", None)
    return jax.shard_map(
        body,
        mesh=mesh,
        in_specs=(split, weight, weight, weight, weight, weight, P(), P(), P(), P(), P(), split),
        out_specs=(split, split, weight, weight, weight, weight, P(), P(), P(), P(), P()),
        check_vma=False,
    )
```

```python
import functools
import math

import jax
import jax.numpy as jnp
import numpy as np
from jax import lax
from jax.experimental import pallas as pl
from jax.experimental.pallas import tpu as pltpu
from jax.sharding import PartitionSpec as P

EPSILON = 1e-06
SOFT_FACTOR = 1.442695041
LOG2E = 1.4426950408889634
MASKED = -1e30
HEADS_AT_ONCE = 4
COST = 1.0
AXES = ("dp", "ctx")
BF = jnp.bfloat16
F32 = jnp.float32


def nn(a, b):
    return lax.dot_general(a, b, (((1,), (0,)), ((), ())), preferred_element_type=F32)


def nt(a, b):
    return lax.dot_general(a, b, (((1,), (1,)), ((), ())), preferred_element_type=F32)


def tile_counts(ids_ref, stretch, tile, tiles):
    low = ids_ref[stretch * tile]
    high = ids_ref[stretch * tile + tile - 1]
    full = jnp.int32(0)
    need = jnp.int32(0)
    for t in range(tiles):
        full += (ids_ref[t * tile + tile - 1] <= low).astype(jnp.int32)
        need += (ids_ref[t * tile] <= high).astype(jnp.int32)
    return full, need


def project_kernel(part, query_slots, n, core_ref, gain_ref, scale_ref, *refs):
    x_refs, w_refs = refs[:n], refs[n : n + 3]
    qt_ref, kt_ref, vt_ref, xt_ref, wt, xs = refs[n + 3 :]
    i = pl.program_id(0)

    @pl.when(i == 0)
    def _():
        for j, ref in enumerate(w_refs):
            wt[j * part : (j + 1) * part, :] = ref[...].T

    for s in range(n):

        @pl.when(i == s)
        def _(s=s):
            xs[...] = x_refs[s][...]

    x = xs[...].astype(F32)
    inverse = lax.rsqrt(jnp.mean(x * x, -1, keepdims=True) + EPSILON)
    xt_ref[...] = (x * inverse * gain_ref[...]).astype(BF).T
    kt_ref[...] = nn(wt[part : 2 * part, :], xt_ref[...]).astype(BF)
    vt_ref[...] = nn(wt[2 * part :, :], xt_ref[...]).astype(BF)

    @pl.when(i < query_slots)
    def _():
        qt_ref[...] = (nn(wt[:part, :], xt_ref[...]) * scale_ref[...]).astype(BF)


def project(slots, w_full, core, gain, scale):
    n = len(slots)
    rows, width = slots[0].shape
    part = width // 2
    query_slots = 2
    once = pl.Buffered(1)
    return pl.pallas_call(
        functools.partial(project_kernel, part, query_slots, n),
        grid_spec=pltpu.PrefetchScalarGridSpec(
            num_scalar_prefetch=1,
            grid=(n,),
            in_specs=[
                pl.BlockSpec((1, width), lambda i, c: (0, 0)),
                pl.BlockSpec((part, 1), lambda i, c: (0, 0)),
                *[pl.BlockSpec((rows, width), lambda i, c: (0, 0), pipeline_mode=once)] * n,
                *[
                    pl.BlockSpec(
                        (width, part), lambda i, c, j=j: (0, 2 * j + c[0]), pipeline_mode=once
                    )
                    for j in range(3)
                ],
            ],
            out_specs=[
                pl.BlockSpec((part, rows), lambda i, c: (0, jnp.minimum(i, query_slots - 1))),
                pl.BlockSpec((part, rows), lambda i, c: (0, i)),
                pl.BlockSpec((part, rows), lambda i, c: (0, i)),
                pl.BlockSpec((width, rows), lambda i, c: (0, i)),
            ],
            scratch_shapes=[pltpu.VMEM((3 * part, width), BF), pltpu.VMEM((rows, width), BF)],
        ),
        out_shape=[
            jax.ShapeDtypeStruct((part, query_slots * rows), BF),
            jax.ShapeDtypeStruct((part, n * rows), BF),
            jax.ShapeDtypeStruct((part, n * rows), BF),
            jax.ShapeDtypeStruct((width, n * rows), BF),
        ],
        compiler_params=pltpu.CompilerParams(vmem_limit_bytes=60 << 20),
        cost_estimate=pl.CostEstimate(
            flops=int(COST * 2 * width * part * rows * (2 * n + query_slots)),
            bytes_accessed=1 << 16,
            transcendentals=0,
        ),
        name="project",
    )(core, gain, scale, *slots, *[w_full] * 3)


def mlp_kernel(
    part, core_ref, near_ref, far_ref, w_ref, x_ref, cot_ref, gain_ref, bin_ref, bdown_ref, out_ref, keep_ref, give_ref,
    gmid_ref, ht_ref, nt_ref, gpre_ref, gml_ref, gain_out, bin_out, bdown_out, middle, normed,
    hidden, slope, g_ref,
):
    width = x_ref.shape[1]
    step = width // 5
    chunks = [slice(c * step, (c + 1) * step) for c in range(5)]
    down, inner, outer = 0, width, 2 * width
    core = core_ref[0]
    near_rows = pl.ds(pl.multiple_of(core * part, part), part)
    far_rows = pl.ds(pl.multiple_of((1 - core) * part, part), part)

    @pl.when(pl.program_id(0) == 0)
    def _():
        for ref in (gain_out, bin_out, bdown_out):
            ref[...] = jnp.zeros(ref.shape, F32)

    near, far = near_ref[...].T, far_ref[...].T
    for cols in chunks:
        at = slice(outer + cols.start, outer + cols.stop)
        middle[:, cols] = (
            x_ref[:, cols].astype(F32) + nn(near, w_ref[near_rows, at]) + nn(far, w_ref[far_rows, at])
        )
    mid = middle[...]
    inverse = lax.rsqrt(jnp.mean(mid * mid, -1, keepdims=True) + EPSILON)
    normed[...] = (mid * inverse * gain_ref[...]).astype(BF)
    nt_ref[...] = normed[...].T
    for cols in chunks:
        at = slice(inner + cols.start, inner + cols.stop)
        pre = nn(normed[...], w_ref[:, at]) + bin_ref[:, cols]
        sigma = 1.0 / (1.0 + jnp.exp(-pre))
        hidden[:, cols] = (pre * sigma).astype(BF)
        slope[:, cols] = sigma * (1.0 + pre * (1.0 - sigma))
    ht_ref[...] = hidden[...].T
    for cols in chunks:
        at = slice(down + cols.start, down + cols.stop)
        out_ref[:, cols] = (
            middle[:, cols] + nn(hidden[...], w_ref[:, at]) + bdown_ref[:, cols]
        ).astype(BF)
    for cols in chunks:
        gpre_ref[:, cols] = (
            nt(cot_ref[...], w_ref[cols, down : down + width]) * slope[:, cols]
        ).astype(BF)
    for cols in chunks:
        g_ref[:, cols] = nt(gpre_ref[...], w_ref[cols, inner : inner + width])
    bin_out[...] += jnp.sum(gpre_ref[...].astype(F32), 0, keepdims=True)
    cot = cot_ref[...].astype(F32)
    bdown_out[...] += jnp.sum(cot, 0, keepdims=True)
    turned = middle[...] * inverse
    gn = g_ref[...] * turned
    gain_out[...] += jnp.sum(gn, 0, keepdims=True)
    mean = jnp.mean(gn * gain_ref[...], -1, keepdims=True)
    gmid = cot + inverse * (g_ref[...] * gain_ref[...] - turned * mean)
    gmid_ref[...] = gmid
    gml_ref[...] = gmid.astype(BF)
    low = gml_ref[...]
    keep_ref[...] = nt(w_ref[near_rows, outer : outer + width], low).astype(BF)
    give_ref[...] = nt(w_ref[far_rows, outer : outer + width], low).astype(BF)


def mlp(near, far, weights, x, cot, core, gain, bias_in, bias_down):
    part, rows = far.shape
    width = x.shape[1]
    tile = 256
    once = pl.Buffered(1)
    row = pl.BlockSpec((tile, width), lambda i, c: (i, 0))
    feature = pl.BlockSpec((part, tile), lambda i, c: (0, i))
    wide = pl.BlockSpec((width, tile), lambda i, c: (0, i))
    vector = pl.BlockSpec((1, width), lambda i, c: (0, 0))
    return pl.pallas_call(
        functools.partial(mlp_kernel, part),
        grid_spec=pltpu.PrefetchScalarGridSpec(
            num_scalar_prefetch=1,
            grid=(rows // tile,),
            in_specs=[
                feature,
                feature,
                pl.BlockSpec(weights.shape, lambda i, c: (0, 0), pipeline_mode=once),
                row, row, vector, vector, vector,
            ],
            out_specs=[
                row, feature, feature, row, wide, wide, row, row, vector, vector, vector
            ],
            scratch_shapes=[
                pltpu.VMEM((tile, width), F32),
                pltpu.VMEM((tile, width), BF),
                pltpu.VMEM((tile, width), BF),
                pltpu.VMEM((tile, width), F32),
                pltpu.VMEM((tile, width), F32),
            ],
        ),
        out_shape=[
            jax.ShapeDtypeStruct((rows, width), BF),
            jax.ShapeDtypeStruct((part, rows), BF),
            jax.ShapeDtypeStruct((part, rows), BF),
            jax.ShapeDtypeStruct((rows, width), F32),
            jax.ShapeDtypeStruct((width, rows), BF),
            jax.ShapeDtypeStruct((width, rows), BF),
            jax.ShapeDtypeStruct((rows, width), BF),
            jax.ShapeDtypeStruct((rows, width), BF),
            jax.ShapeDtypeStruct((1, width), F32),
            jax.ShapeDtypeStruct((1, width), F32),
            jax.ShapeDtypeStruct((1, width), F32),
        ],
        compiler_params=pltpu.CompilerParams(vmem_limit_bytes=60 << 20),
        cost_estimate=pl.CostEstimate(
            flops=int(COST * 12 * rows * width * width), bytes_accessed=1 << 16, transcendentals=0
        ),
        name="mlp",
    )(core, near, far, weights, x, cot, gain, bias_in, bias_down)


def mlp_weight_kernel(
    core_ref, near_ref, far_ref, ht_ref, nt_ref, cot_ref, gpre_ref, gml_ref, out_ref
):
    which, part_at = pl.program_id(0), pl.program_id(1)

    @pl.when(which == 0)
    def _():
        out_ref[...] = nn(ht_ref[...], cot_ref[...]).astype(BF)

    @pl.when(which == 1)
    def _():
        out_ref[...] = nn(nt_ref[...], gpre_ref[...]).astype(BF)

    @pl.when((which == 2) & (part_at == core_ref[0]))
    def _():
        out_ref[...] = nn(near_ref[...], gml_ref[...]).astype(BF)

    @pl.when((which == 2) & (part_at != core_ref[0]))
    def _():
        out_ref[...] = nn(far_ref[...], gml_ref[...]).astype(BF)


def mlp_weights(near, far, ht, nrt, cot, gpre, gml, core):
    part, rows = far.shape
    width = cot.shape[1]
    once = pl.Buffered(1)

    def whole(shape):
        return pl.BlockSpec(shape, lambda j, r, c: (0,) * len(shape), pipeline_mode=once)

    return pl.pallas_call(
        mlp_weight_kernel,
        grid_spec=pltpu.PrefetchScalarGridSpec(
            num_scalar_prefetch=1,
            grid=(3, 2),
            in_specs=[
                whole((part, rows)),
                whole((part, rows)),
                pl.BlockSpec((part, rows), lambda j, r, c: (jnp.where(j == 0, r, 1), 0)),
                pl.BlockSpec((part, rows), lambda j, r, c: (jnp.where(j == 1, r, j // 2), 0)),
                whole((rows, width)),
                whole((rows, width)),
                whole((rows, width)),
            ],
            out_specs=pl.BlockSpec((part, width), lambda j, r, c: (r, j)),
        ),
        out_shape=jax.ShapeDtypeStruct((width, 3 * width), BF),
        compiler_params=pltpu.CompilerParams(vmem_limit_bytes=60 << 20),
        cost_estimate=pl.CostEstimate(
            flops=6 * rows * width * width, bytes_accessed=20 << 20, transcendentals=0
        ),
        name="mlp_weights",
    )(core, near, far, ht, nrt, cot, gpre, gml)


def load_keys(ref, place_ref, hd, tile, group, knat, kt=None):
    tiles = ref.shape[1] // tile
    for b in range(tiles):
        stretch = place_ref[tiles + b]
        piece = ref[:, b * tile : (b + 1) * tile]
        if kt is not None:
            kt[stretch] = piece
        if knat is not None:
            for h in range(group):
                knat[h, stretch] = piece[h * hd : (h + 1) * hd, :].T


def forward_kernel(
    hd, tile, ids_ref, place_ref, row_ref, col_ref, qt_ref, kt_ref, vt_ref, near_ref, far_ref,
    lse_ref, knat, vt, acc, m_ref, l_ref,
):
    group = qt_ref.shape[0] // hd
    tiles = vt.shape[0]
    load_keys(kt_ref, place_ref, hd, tile, group, knat)
    load_keys(vt_ref, place_ref, hd, tile, group, None, vt)
    per_half = near_ref.shape[1] // tile

    def one_tile(qi, carry):
        stretch = place_ref[tiles + qi]
        full, need = tile_counts(ids_ref, stretch, tile, tiles)
        qcol = pl.ds(pl.multiple_of(qi * tile, tile), tile)
        qpos = pl.ds(pl.multiple_of(stretch * tile, tile), tile)
        m_ref[...] = jnp.full(m_ref.shape, MASKED, F32)
        l_ref[...] = jnp.zeros(l_ref.shape, F32)
        acc[...] = jnp.zeros(acc.shape, F32)

        def step(ts, masked):
            if masked:
                allowed = [
                    col_ref[pl.ds(pl.multiple_of(t * tile, tile), tile), :] <= row_ref[:, qpos]
                    for t in ts
                ]
            scores = [
                [nn(knat[h, t], qt_ref[h * hd : (h + 1) * hd, qcol]) for t in ts]
                for h in range(group)
            ]
            for h in range(group):
                s = scores[h]
                if masked:
                    s = [jnp.where(ok, one, MASKED) for ok, one in zip(allowed, s)]
                old = m_ref[h]
                new = old
                for one in s:
                    new = jnp.maximum(new, jnp.max(one, 0, keepdims=True))
                p = [jnp.exp2(one - new) for one in s]
                alpha = jnp.exp2(old - new)
                total = l_ref[h] * alpha
                for one in p:
                    total = total + jnp.sum(one, 0, keepdims=True)
                l_ref[h] = total
                m_ref[h] = new
                out = acc[h] * alpha
                for t, one in zip(ts, p):
                    out = out + nn(vt[t, h * hd : (h + 1) * hd, :], one.astype(BF))
                acc[h] = out

        def full_step(i, c):
            step([2 * i, 2 * i + 1], False)
            return c

        def mask_step(i, c):
            step([2 * i, 2 * i + 1], True)
            return c

        lax.fori_loop(0, full // 2, full_step, 0)
        lax.fori_loop(full // 2, (need + 1) // 2, mask_step, 0)
        inner = pl.ds(pl.multiple_of((qi % per_half) * tile, tile), tile)
        for half, ref in enumerate((near_ref, far_ref)):

            @pl.when(qi // per_half == half)
            def _(ref=ref):
                for h in range(group):
                    ref[h * hd : (h + 1) * hd, inner] = (acc[h] / l_ref[h]).astype(BF)

        for h in range(group):
            lse_ref[h, :, qcol] = m_ref[h] + jnp.log2(l_ref[h])
        return carry

    lax.fori_loop(0, qt_ref.shape[1] // tile, one_tile, 0)


def backward_kernel(hd, tile, base, count, first, last, *refs):
    ids_ref, place_ref, row_ref, col_ref, qt_ref, kt_ref, vt_ref = refs[:7]
    near_ref, far_ref, onear_ref, ofar_ref, lse_ref = refs[7:12]
    if last:
        before_ref, scale_ref, dqt_ref, dkt_ref, dvt_ref, gs_ref = refs[12:18]
        knat, vnat, kt, dq, dk, dv, delta, dot = refs[18:]
    else:
        dqt_ref, dkt_ref, dvt_ref = refs[12:15]
        knat, vnat, kt, dq, dk, dv, delta, dot = refs[15:]
    tiles = kt_ref.shape[1] // tile
    group = qt_ref.shape[0] // hd

    def block_of(i):
        return pl.multiple_of(place_ref[place_ref[base + i]] * tile, tile)

    for i in range(count):
        cols = pl.ds(block_of(i), tile)
        kt[i] = kt_ref[:, cols]
        for h in range(group):
            hs = slice(h * hd, (h + 1) * hd)
            knat[h, i] = kt_ref[hs, cols].T
            vnat[h, i] = vt_ref[hs, cols].T
    per_half = near_ref.shape[1] // tile
    for half, (ref, o_ref) in enumerate(((near_ref, onear_ref), (far_ref, ofar_ref))):
        for b in range(per_half):
            cols = slice(b * tile, (b + 1) * tile)
            dot[half * per_half + b] = ref[:, cols]
            product = ref[:, cols].astype(F32) * o_ref[:, cols].astype(F32)
            for h in range(group):
                delta[half * per_half + b, h] = jnp.sum(
                    product[h * hd : (h + 1) * hd], 0, keepdims=True
                )
    dk[...] = jnp.zeros(dk.shape, F32)
    dv[...] = jnp.zeros(dv.shape, F32)
    if last:
        gs_ref[...] = jnp.zeros(gs_ref.shape, F32)

    def one_tile(qi, carry):
        stretch = place_ref[tiles + qi]
        low = ids_ref[stretch * tile]
        high = ids_ref[stretch * tile + tile - 1]
        full = jnp.int32(0)
        need = jnp.int32(0)
        for i in range(count):
            t = place_ref[base + i]
            full += (ids_ref[t * tile + tile - 1] <= low).astype(jnp.int32)
            need += (ids_ref[t * tile] <= high).astype(jnp.int32)
        qcol = pl.ds(pl.multiple_of(qi * tile, tile), tile)
        qpos = pl.ds(pl.multiple_of(stretch * tile, tile), tile)
        dq[...] = before_ref[:, qcol] if last else jnp.zeros(dq.shape, F32)

        def step(ts, masked):
            if masked:
                allowed = [
                    col_ref[pl.ds(pl.multiple_of(place_ref[base + t] * tile, tile), tile), :]
                    <= row_ref[:, qpos]
                    for t in ts
                ]

            def scores(h, t):
                hs = slice(h * hd, (h + 1) * hd)
                return nn(knat[h, t], qt_ref[hs, qcol]), nn(vnat[h, t], dot[qi, hs, :])

            order = [(h, i) for h in range(group) for i in range(len(ts))]
            ahead = scores(0, ts[0])
            for j, (h, i) in enumerate(order):
                hs = slice(h * hd, (h + 1) * hd)
                t = ts[i]
                s, dp = ahead
                if j + 1 < len(order):
                    ahead = scores(order[j + 1][0], ts[order[j + 1][1]])
                if masked:
                    s = jnp.where(allowed[i], s, MASKED)
                p = jnp.exp2(s - lse_ref[h, :, qcol])
                ds = (p * (dp - delta[qi, h])).astype(BF)
                dv[t, hs, :] += nt(dot[qi, hs, :], p.astype(BF))
                dk[t, hs, :] += nt(qt_ref[hs, qcol], ds)
                dq[hs, :] += nn(kt[t, hs, :], ds)

        def full_step(i, c):
            step([2 * i, 2 * i + 1], False)
            return c

        def mask_step(i, c):
            step([2 * i, 2 * i + 1], True)
            return c

        lax.fori_loop(0, full // 2, full_step, 0)
        lax.fori_loop(full // 2, (need + 1) // 2, mask_step, 0)
        if last:
            gs_ref[...] += jnp.sum(dq[...] * qt_ref[:, qcol].astype(F32), 1, keepdims=True)
            dqt_ref[:, qcol] = (dq[...] * scale_ref[...]).astype(BF)
        else:
            dqt_ref[:, qcol] = dq[...]
        return carry

    lax.fori_loop(0, qt_ref.shape[1] // tile, one_tile, 0)
    for i in range(count):
        cols = pl.ds(pl.multiple_of(block_of(i) - first * tile, tile), tile)
        dkt_ref[:, cols] = (dk[i] * (1.0 / LOG2E)).astype(BF)
        dvt_ref[:, cols] = dv[i].astype(BF)


def attention_specs(nq, nk, hd, group, at):
    size = group * hd
    return (
        [
            pl.BlockSpec(memory_space=pltpu.SMEM),
            pl.BlockSpec(memory_space=pltpu.SMEM),
            pl.BlockSpec((1, nk), lambda i: (0, 0)),
            pl.BlockSpec((nk, 1), lambda i: (0, 0)),
            pl.BlockSpec((size, nq), lambda i: (i + at, 0)),
            pl.BlockSpec((size, nk), lambda i: (i + at, 0)),
            pl.BlockSpec((size, nk), lambda i: (i + at, 0)),
        ],
        pl.BlockSpec((size, nq // 2), lambda i: (i + at, 0)),
        pl.BlockSpec((group, 1, nq), lambda i: (i + at, 0, 0)),
    )


def attention_forward(ids, col, place, qt, kt, vt, hd, tile):
    heads = qt.shape[0] // hd
    nq, nk = qt.shape[1], kt.shape[1]
    group = HEADS_AT_ONCE
    common, halves, rows = attention_specs(nq, nk, hd, group, 0)
    pairs = heads * nq * nk * 0.6
    return pl.pallas_call(
        functools.partial(forward_kernel, hd, tile),
        grid=(heads // group,),
        in_specs=common,
        out_specs=[halves, halves, rows],
        out_shape=[
            jax.ShapeDtypeStruct((heads * hd, nq // 2), BF),
            jax.ShapeDtypeStruct((heads * hd, nq // 2), BF),
            jax.ShapeDtypeStruct((heads, 1, nq), F32),
        ],
        scratch_shapes=[
            pltpu.VMEM((group, nk // tile, tile, hd), BF),
            pltpu.VMEM((nk // tile, group * hd, tile), BF),
            pltpu.VMEM((group, hd, tile), F32),
            pltpu.VMEM((group, 1, tile), F32),
            pltpu.VMEM((group, 1, tile), F32),
        ],
        compiler_params=pltpu.CompilerParams(vmem_limit_bytes=60 << 20),
        cost_estimate=pl.CostEstimate(
            flops=int(COST * pairs * 1024), bytes_accessed=1 << 16, transcendentals=int(COST * pairs)
        ),
        name="attention_forward",
    )(ids, place, ids.reshape(1, -1), col, qt, kt, vt)


def attention_backward(
    ids, col, place, qt, kt, vt, near, far, onear, ofar, lse, hd, tile, before=None, scale=None
):
    heads = qt.shape[0] // hd
    nq, nk = qt.shape[1], kt.shape[1]
    group = HEADS_AT_ONCE
    size = group * hd
    last = before is not None
    early = nq // tile
    tiles = nk // tile
    count, first = (early, 0) if last else (tiles - early, early)
    base = 2 * tiles + (0 if last else early)
    common, halves, rows = attention_specs(nq, nk, hd, group, 0)
    wide = pl.BlockSpec((size, nq), lambda i: (i, 0))
    keys = pl.BlockSpec((size, count * tile), lambda i: (i, 0))
    one = pl.BlockSpec((size, 1), lambda i: (i, 0))
    pairs = heads * nq * count * tile * 0.6
    return pl.pallas_call(
        functools.partial(backward_kernel, hd, tile, base, count, first, last),
        grid=(heads // group,),
        in_specs=[*common, halves, halves, halves, halves, rows, *([wide, one] if last else [])],
        out_specs=[wide, keys, keys, *([one] if last else [])],
        out_shape=[
            jax.ShapeDtypeStruct((heads * hd, nq), BF if last else F32),
            jax.ShapeDtypeStruct((heads * hd, count * tile), BF),
            jax.ShapeDtypeStruct((heads * hd, count * tile), BF),
            *([jax.ShapeDtypeStruct((heads * hd, 1), F32)] if last else []),
        ],
        scratch_shapes=[
            pltpu.VMEM((group, count, tile, hd), BF),
            pltpu.VMEM((group, count, tile, hd), BF),
            pltpu.VMEM((count, size, tile), BF),
            pltpu.VMEM((size, tile), F32),
            pltpu.VMEM((count, size, tile), F32),
            pltpu.VMEM((count, size, tile), F32),
            pltpu.VMEM((nq // tile, group, 1, tile), F32),
            pltpu.VMEM((nq // tile, size, tile), BF),
        ],
        compiler_params=pltpu.CompilerParams(vmem_limit_bytes=60 << 20),
        cost_estimate=pl.CostEstimate(
            flops=int(pairs * 2560), bytes_accessed=16 << 20, transcendentals=int(pairs)
        ),
        name="attention_backward",
    )(
        ids, place, ids.reshape(1, -1), col, qt, kt, vt, near, far, onear, ofar, lse,
        *([before, scale] if last else []),
    )


def weight_kernel(size, nq, at_ref, xt_ref, dqt_ref, dka_ref, dva_ref, dkb_ref, dvb_ref, *out_refs):
    for m, ref in enumerate(out_refs):

        @pl.when(pl.program_id(0) == m)
        def _(ref=ref):
            early = jnp.concatenate([dka_ref[...], dva_ref[...]], 0)
            late = jnp.concatenate([dkb_ref[...], dvb_ref[...]], 0)
            ref[:, : 2 * size] = (nt(xt_ref[:, :nq], early) + nt(xt_ref[:, nq:], late)).astype(BF)
            ref[:, 2 * size :] = nt(xt_ref[:, :nq], dqt_ref[...]).astype(BF)


def weight_gradient(xt, dqt, early, late, at, pieces, which):
    width, nk = xt.shape
    part, nq = dqt.shape
    size = part // 2
    rows = width // pieces
    once = pl.Buffered(1)

    def heads(cols):
        return pl.BlockSpec((size, cols), lambda i, a: (which, 0), pipeline_mode=once)

    return pl.pallas_call(
        functools.partial(weight_kernel, size, nq),
        grid_spec=pltpu.PrefetchScalarGridSpec(
            num_scalar_prefetch=1,
            grid=(pieces,),
            in_specs=[
                pl.BlockSpec((rows, nk), lambda i, a: (a[i], 0)),
                heads(nq), heads(nq), heads(nq), heads(nk - nq), heads(nk - nq),
            ],
            out_specs=[pl.BlockSpec((rows, 3 * size), lambda i, a: (0, 0))] * pieces,
        ),
        out_shape=[jax.ShapeDtypeStruct((rows, 3 * size), BF)] * pieces,
        compiler_params=pltpu.CompilerParams(vmem_limit_bytes=60 << 20),
        cost_estimate=pl.CostEstimate(
            flops=2 * width * size * (2 * nk + nq), bytes_accessed=12 << 20, transcendentals=0
        ),
        name="weight_gradient",
    )(at, xt, dqt, *early, *late)


def dx_kernel(part, queries, n, core_ref, *refs):
    dk_ref, dv_ref, wk_ref, wv_ref, gain_ref = refs[:5]
    x_refs = refs[5 : 5 + n]
    rest = refs[5 + n :]
    if queries:
        dq_ref, wq_ref = rest[:2]
        rest = rest[2:]
    dx_refs, (gg_ref, g_ref, xs) = rest[:n], rest[n:]
    i = pl.program_id(0)
    tile, width = xs.shape
    step = width // 5
    dk = dk_ref[...].T
    dv = dv_ref[...].T
    if queries:
        dq = dq_ref[...].T
    for c in range(5):
        cols = slice(c * step, (c + 1) * step)
        g = nt(dk, wk_ref[cols, :]) + nt(dv, wv_ref[cols, :])
        if queries:
            g = g + nt(dq, wq_ref[cols, :])
        g_ref[:, cols] = g

    @pl.when(i == 0)
    def _():
        gg_ref[...] = jnp.zeros(gg_ref.shape, F32)

    per_slot = x_refs[0].shape[0] // tile
    for s in range(n):

        @pl.when(i // per_slot == s)
        def _(s=s):
            xs[...] = x_refs[s][pl.ds(pl.multiple_of((i % per_slot) * tile, tile), tile), :]

    x = xs[...].astype(F32)
    inverse = lax.rsqrt(jnp.mean(x * x, -1, keepdims=True) + EPSILON)
    normed = x * inverse
    g = g_ref[...]
    gn = g * normed
    gg_ref[...] += jnp.sum(gn, 0, keepdims=True)
    scaled = g * gain_ref[...]
    mean = jnp.mean(gn * gain_ref[...], -1, keepdims=True)
    out = (inverse * (scaled - normed * mean)).astype(BF)
    for s in range(n):

        @pl.when(i // per_slot == s)
        def _(s=s):
            dx_refs[s][...] = out


def input_gradient(dkvs, dqs, w_full, slots, core, gain):
    part = dkvs[0].shape[0]
    n = len(slots)
    rows, width = slots[0].shape
    tile = 256
    per_slot = rows // tile
    once = pl.Buffered(1)
    dkv = pl.BlockSpec((part, tile), lambda i, c: (0, i))

    def weight(j):
        return pl.BlockSpec(
            (width, part), lambda i, c, j=j: (0, 2 * j + c[0]), pipeline_mode=once
        )

    specs = [
        dkv, dkv, weight(1), weight(2), pl.BlockSpec((1, width), lambda i, c: (0, 0)),
        *[pl.BlockSpec((rows, width), lambda i, c: (0, 0), pipeline_mode=once)] * n,
    ]
    operands = [*dkvs, w_full, w_full, gain, *slots]
    if dqs:
        specs += [dkv, weight(0)]
        operands += [*dqs, w_full]
    return pl.pallas_call(
        functools.partial(dx_kernel, part, bool(dqs), n),
        grid_spec=pltpu.PrefetchScalarGridSpec(
            num_scalar_prefetch=1,
            grid=(n * rows // tile,),
            in_specs=specs,
            out_specs=[
                *[
                    pl.BlockSpec(
                        (tile, width),
                        lambda i, c, s=s: (jnp.clip(i - s * per_slot, 0, per_slot - 1), 0),
                    )
                    for s in range(n)
                ],
                pl.BlockSpec((1, width), lambda i, c: (0, 0)),
            ],
            scratch_shapes=[pltpu.VMEM((tile, width), F32), pltpu.VMEM((tile, width), BF)],
        ),
        out_shape=[
            *[jax.ShapeDtypeStruct((rows, width), BF)] * n,
            jax.ShapeDtypeStruct((1, width), F32),
        ],
        compiler_params=pltpu.CompilerParams(vmem_limit_bytes=60 << 20),
        cost_estimate=pl.CostEstimate(
            flops=int(COST * 2 * width * n * rows * part * (3 if dqs else 2)),
            bytes_accessed=1 << 16,
            transcendentals=0,
        ),
        name="input_gradient",
    )(core, *operands)


class Plan:
    def __init__(self, dp, ctx):
        self.dp, self.ctx = dp, ctx
        self.half = ctx // 2

    def index(self, pair, core, z):
        return (pair * 2 + core) * self.ctx + z

    def perm(self, to):
        out = []
        for d in range(self.dp):
            for z in range(self.ctx):
                got = to(d // 2, d % 2, z)
                if got is not None:
                    out.append((self.index(d // 2, d % 2, z), self.index(*got)))
        return out

    def home(self, core, z):
        return core == z // self.half

    def turned(self, z, k):
        first = z // self.half * self.half
        return first + (z - first + k) % self.half

    def core_swap(self):
        return self.perm(lambda p, c, z: (p, 1 - c, z))

    def pair_swap(self, mask):
        return self.perm(lambda p, c, z: (p ^ mask, c, z))

    def line_swap(self, mask):
        return self.perm(lambda p, c, z: (p, c, z ^ mask))

    def line_in(self, s):
        last = self.ctx - 1
        to = {s: s + 1, last - s: last - s - 1}
        return self.perm(lambda p, c, z: (p, c, to[z]) if z in to else None)

    def line_out(self, s):
        last = self.ctx - 1
        to = {s + 1: s, last - s - 1: last - s}
        return self.perm(lambda p, c, z: (p, c, to[z]) if z in to else None)

    def line_middle(self):
        to = {self.half - 1: self.half, self.half: self.half - 1}
        return self.perm(lambda p, c, z: (p, c, to[z]) if z in to else None)

    def mirror(self):
        return self.perm(
            lambda p, c, z: None if self.home(c, z) else (p, 1 - c, self.ctx - 1 - z)
        )

    def mirror_or_turn(self, k):
        return self.perm(
            lambda p, c, z: (p, c, self.turned(z, k))
            if self.home(c, z)
            else (p, 1 - c, self.ctx - 1 - z)
        )

    def turn(self, k, away_only):
        return self.perm(
            lambda p, c, z: None
            if away_only and self.home(c, z)
            else (p, c, self.turned(z, k))
        )

    def shard(self, core, z, k, mine):
        chip = self.turned(z, -k)
        at_home = self.home(core, z) if mine else not self.home(core, z)
        return chip if at_home else self.ctx - 1 - chip

    def places(self):
        table = np.zeros((self.dp, self.ctx, 6 * self.ctx), np.int32)
        for d in range(self.dp):
            for z in range(self.ctx):
                slots = [
                    self.shard(d % 2, z, k, mine) for k in range(self.half) for mine in (True, False)
                ]
                stretches = [s for shard in slots for s in (shard, 2 * self.ctx - 1 - shard)]
                for block, stretch in enumerate(stretches):
                    table[d, z, stretch] = block
                    table[d, z, 2 * self.ctx + block] = stretch
                table[d, z, 4 * self.ctx :] = sorted(stretches[:4]) + sorted(stretches[4:])
        return table.reshape(self.dp * self.ctx, 6 * self.ctx)


def send(value, pairs):
    return lax.ppermute(value, AXES, pairs)


def tie(*values):
    return lax.optimization_barrier(values)


def line_inward(value, plan, kind):
    total = value.astype(F32)
    for s in range(plan.half - 2):
        total = total + send(total.astype(kind), plan.line_in(s)).astype(F32)
    if plan.half == 1:
        return total, jnp.zeros_like(total, kind)
    return total, send(total.astype(kind), plan.line_in(plan.half - 2))


def line_across(held, came, plan, kind):
    sent = (held + came.astype(F32)).astype(kind)
    return sent, send(sent, plan.line_middle())


def line_joined(sent, came):
    return (sent.astype(F32) + came.astype(F32)).astype(sent.dtype)


def line_outward(total, plan, z):
    for s in reversed(range(plan.half - 1)):
        back = send(total, plan.line_out(s))
        total = jnp.where((z == s) | (z == plan.ctx - 1 - s), back, total)
    return total


def body(
    tokens_in, block_ids, w_qkv, w_out, w_in, w_down, gain_attn, gain_mlp, bias_in, bias_down,
    query_scale, cotangent,
):
    n = lax.axis_size("ctx")
    plan = Plan(lax.axis_size("dp"), n)
    half = plan.half
    z = lax.axis_index("ctx")
    core = lax.axis_index("dp") % 2
    pair = lax.axis_index("dp") // 2
    pairs = plan.dp // 2
    home = core == z // half
    rows = tokens_in.shape[1]
    width = tokens_in.shape[2]
    hd = query_scale.shape[0]
    heads = width // hd
    part = width // 2
    tile = rows // 2
    wrows = w_qkv.shape[0]
    core_swap = plan.core_swap()

    own = tokens_in[0]
    first = send(own, plan.mirror_or_turn(1))
    token0 = jnp.where(home, own, first)
    second = send(token0, plan.turn(1, True))
    mine = [token0, jnp.where(home, first, second)]
    for k in range(2, half):
        mine.append(send(token0, plan.turn(k, False)))
    theirs = [send(m, core_swap) for m in mine]
    slots = [a for both in zip(mine, theirs) for a in both]

    full_qkv = lax.all_gather(w_qkv, "dp", axis=0, tiled=True)
    at = jnp.stack([pair ^ mask for mask in range(pairs)]).astype(jnp.int32)
    core_at = core.astype(jnp.int32).reshape(1)

    ids = jnp.where(home, block_ids[0], send(block_ids[0], core_swap))
    place = lax.dynamic_index_in_dim(
        jnp.asarray(plan.places()), lax.axis_index("dp") * n + z, 0, False
    )
    col = ids.reshape(-1, 1)

    gain_one = gain_attn.astype(F32)
    gain_two = gain_mlp.astype(F32)
    scale_exp = jnp.exp(query_scale.astype(F32))
    scale_dim = SOFT_FACTOR / math.sqrt(hd) * jnp.log1p(scale_exp)
    scale_vec = jnp.tile(scale_dim, heads // 2)[:, None]
    weights = lax.all_gather(
        jnp.concatenate([w_down, w_in, w_out], 1), "dp", axis=0, tiled=True
    )
    qt, kt, vt, xt = project(
        slots, full_qkv, core_at, gain_one.reshape(1, -1), scale_vec * LOG2E
    )
    grad_low = send(tie(cotangent[0], slots[-1])[0], plan.mirror())
    onear, ofar, lse = attention_forward(ids, col, place, qt, kt, vt, hd, tile)
    onear, ofar, grad_low = tie(onear, ofar, grad_low)
    grad_low = jnp.where(home, cotangent[0], grad_low)
    o_got = send(ofar, core_swap)

    (
        output, to_keep, to_give, grad_middle, hidden_t, normed_t, grad_pre, grad_mid_low,
        grad_gain_two, grad_bin, grad_bdown,
    ) = mlp(
        onear, o_got, weights, token0, grad_low, core_at, gain_two.reshape(1, -1),
        bias_in.astype(F32).reshape(1, -1), bias_down.astype(F32).reshape(1, -1),
    )
    far = send(to_give, core_swap)
    away_output = send(output, plan.mirror())
    joined = mlp_weights(onear, o_got, hidden_t, normed_t, grad_low, grad_pre, grad_mid_low, core_at)
    early_qt, joined, far = tie(qt, joined, far)
    scattered = lax.psum_scatter(joined, "dp", scatter_dimension=0, tiled=True)

    def backward(queries, **rest):
        return attention_backward(
            ids, col, place, queries, kt, vt, to_keep, far, onear, ofar, lse, hd, tile, **rest
        )

    def to_owners(grads):
        return [send(grads[m], plan.pair_swap(m)) for m in range(1, pairs)]

    def add_up(grads, came):
        total = grads[0].astype(F32)
        for one in came:
            total = total + one.astype(F32)
        return total

    gain_row = gain_one.reshape(1, -1)
    dq_part, *late_kv = backward(early_qt)
    *late_dx, gain_late = input_gradient(late_kv, (), full_qkv, slots[2:], core_at, gain_row)
    dq_part, away_output, *late_dx = tie(dq_part, away_output, *late_dx)
    output = jnp.where(home, output, away_output)
    late_got = [
        send(late_dx[2 * k + 1], core_swap) for k in range(half - 1)
    ]
    dq_part, *late_got = tie(dq_part, *late_got)
    turned = []
    for k in range(half - 1):
        mine = late_dx[2 * k].astype(F32)
        turned.append(
            send((mine + late_got[k].astype(F32)).astype(BF), plan.turn(-k - 1, False))
        )
    dqt, dk_early, dv_early, gs = backward(qt, before=dq_part, scale=scale_vec)
    dqt, dk_early, dv_early, scattered, *turned = tie(
        dqt, dk_early, dv_early, scattered, *turned
    )
    held_o, line_o = line_inward(scattered, plan, BF)
    early_kv = (dk_early, dv_early)
    grads_a = weight_gradient(xt, dqt, early_kv, late_kv, at, pairs, 0)
    later_dq, *grads_a = tie(dqt, *grads_a)
    came_a = to_owners(grads_a)
    near_dx, far_dx, gain_early = input_gradient(
        early_kv, (later_dq,), full_qkv, slots[:2], core_at, gain_row
    )
    near_dx, far_dx, gain_early, last_dq, line_o, *came_a = tie(
        near_dx, far_dx, gain_early, dqt, line_o, *came_a
    )
    got = send(far_dx, core_swap)
    held_a, line_a = line_inward(add_up(grads_a, came_a), plan, BF)
    held_o, line_o = line_across(held_o, line_o, plan, BF)
    grads_b = weight_gradient(xt, last_dq, early_kv, late_kv, at, pairs, 1)
    scale_slope = SOFT_FACTOR / math.sqrt(hd) * scale_exp / (1.0 + scale_exp)
    grad_scale = jnp.sum(gs.reshape(heads // 2, hd), 0)
    grad_scale = grad_scale * scale_slope / (scale_dim * LOG2E)
    small = jnp.concatenate(
        [
            *(v.reshape(-1) for v in (gain_late + gain_early, grad_gain_two, grad_bin, grad_bdown)),
            grad_scale,
        ]
    )
    small_size = small.shape[0]
    small = jnp.pad(small, (0, -small_size % 1024)).reshape(-1, 128)
    small = small + send(small, core_swap)
    mask = 1
    while mask < pairs:
        small = small + send(small, plan.pair_swap(mask))
        mask *= 2
    got, line_a, small, *grads_b = tie(got, line_a, small, *grads_b)
    came_b = to_owners(grads_b)
    total = near_dx.astype(F32) + got.astype(F32) + grad_middle
    for one in turned:
        total = total + one.astype(F32)
    last = send(total.astype(BF), plan.mirror())
    held_a, line_a = line_across(held_a, line_a, plan, BF)
    line_a, line_o, *came_b = tie(line_a, line_o, *came_b)
    held_b, line_b = line_inward(add_up(grads_b, came_b), plan, BF)
    line_a = line_outward(line_joined(held_a, line_a), plan, z)
    others = line_outward(line_joined(held_o, line_o), plan, z)

    line_b, line_a = tie(line_b, line_a)
    held_b, line_b = line_across(held_b, line_b, plan, BF)

    def owned_rows(value):
        keep = lax.dynamic_slice_in_dim(value, core * wrows, wrows, 0)
        give = lax.dynamic_slice_in_dim(value, (1 - core) * wrows, wrows, 0)
        came = send(give, core_swap)
        return jnp.where(core == 0, keep, came), jnp.where(core == 0, came, keep)

    line_b, line_a, last, small = tie(line_b, line_a, last, small)
    swapped_a = owned_rows(line_a)
    line_b = line_outward(line_joined(held_b, line_b), plan, z)
    came = send(small, plan.line_swap(1))
    line_b, others, came = tie(line_b, others, came)
    small = small + came
    mask = 2
    while mask < n:
        small = small + send(small, plan.line_swap(mask))
        mask *= 2
    small = small.reshape(-1)
    grad_tokens = jnp.where(home, total, last.astype(F32))
    others = others.astype(F32)
    swapped = (swapped_a, owned_rows(line_b))
    size = part // 2
    owned_qkv = jnp.concatenate(
        [
            swapped[g][c][:, which * size : (which + 1) * size]
            for which in (2, 0, 1)
            for c in range(2)
            for g in range(2)
        ],
        1,
    ).astype(F32)

    return (
        output[None],
        grad_tokens[None],
        owned_qkv,
        others[:, 2 * width :],
        others[:, width : 2 * width],
        others[:, :width],
        small[:width],
        small[width : 2 * width],
        small[2 * width : 3 * width],
        small[3 * width : 4 * width],
        small[4 * width : small_size],
    )


def solution(mesh):
    split = P("dp", "ctx", None)
    weight = P("dp", None)
    return jax.shard_map(
        body,
        mesh=mesh,
        in_specs=(split, weight, weight, weight, weight, weight, P(), P(), P(), P(), P(), split),
        out_specs=(split, split, weight, weight, weight, weight, P(), P(), P(), P(), P()),
        check_vma=False,
    )
```

```python
import functools
import math

import jax
import jax.numpy as jnp
import numpy as np
from jax import lax
from jax.experimental import pallas as pl
from jax.experimental.pallas import tpu as pltpu
from jax.sharding import PartitionSpec as P

EPSILON = 1e-06
SOFT_FACTOR = 1.442695041
LOG2E = 1.4426950408889634
MASKED = -1e30
HEADS_AT_ONCE = 4
COST = 1.0
AXES = ("dp", "ctx")
BF = jnp.bfloat16
F32 = jnp.float32


def nn(a, b):
    return lax.dot_general(a, b, (((1,), (0,)), ((), ())), preferred_element_type=F32)


def nt(a, b):
    return lax.dot_general(a, b, (((1,), (1,)), ((), ())), preferred_element_type=F32)


def tile_counts(ids_ref, stretch, tile, tiles):
    low = ids_ref[stretch * tile]
    high = ids_ref[stretch * tile + tile - 1]
    full = jnp.int32(0)
    need = jnp.int32(0)
    for t in range(tiles):
        full += (ids_ref[t * tile + tile - 1] <= low).astype(jnp.int32)
        need += (ids_ref[t * tile] <= high).astype(jnp.int32)
    return full, need


def project_kernel(part, query_slots, n, core_ref, gain_ref, scale_ref, *refs):
    x_refs, w_refs = refs[:n], refs[n : n + 3]
    qt_ref, kt_ref, vt_ref, xt_ref, wt, xs = refs[n + 3 :]
    i = pl.program_id(0)

    @pl.when(i == 0)
    def _():
        for j, ref in enumerate(w_refs):
            wt[j * part : (j + 1) * part, :] = ref[...].T

    for s in range(n):

        @pl.when(i == s)
        def _(s=s):
            xs[...] = x_refs[s][...]

    x = xs[...].astype(F32)
    inverse = lax.rsqrt(jnp.mean(x * x, -1, keepdims=True) + EPSILON)
    xt_ref[...] = (x * inverse * gain_ref[...]).astype(BF).T
    kt_ref[...] = nn(wt[part : 2 * part, :], xt_ref[...]).astype(BF)
    vt_ref[...] = nn(wt[2 * part :, :], xt_ref[...]).astype(BF)

    @pl.when(i < query_slots)
    def _():
        qt_ref[...] = (nn(wt[:part, :], xt_ref[...]) * scale_ref[...]).astype(BF)


def project(slots, w_full, core, gain, scale):
    n = len(slots)
    rows, width = slots[0].shape
    part = width // 2
    query_slots = 2
    once = pl.Buffered(1)
    return pl.pallas_call(
        functools.partial(project_kernel, part, query_slots, n),
        grid_spec=pltpu.PrefetchScalarGridSpec(
            num_scalar_prefetch=1,
            grid=(n,),
            in_specs=[
                pl.BlockSpec((1, width), lambda i, c: (0, 0)),
                pl.BlockSpec((part, 1), lambda i, c: (0, 0)),
                *[pl.BlockSpec((rows, width), lambda i, c: (0, 0), pipeline_mode=once)] * n,
                *[
                    pl.BlockSpec(
                        (width, part), lambda i, c, j=j: (0, 2 * j + c[0]), pipeline_mode=once
                    )
                    for j in range(3)
                ],
            ],
            out_specs=[
                pl.BlockSpec((part, rows), lambda i, c: (0, jnp.minimum(i, query_slots - 1))),
                pl.BlockSpec((part, rows), lambda i, c: (0, i)),
                pl.BlockSpec((part, rows), lambda i, c: (0, i)),
                pl.BlockSpec((width, rows), lambda i, c: (0, i)),
            ],
            scratch_shapes=[pltpu.VMEM((3 * part, width), BF), pltpu.VMEM((rows, width), BF)],
        ),
        out_shape=[
            jax.ShapeDtypeStruct((part, query_slots * rows), BF),
            jax.ShapeDtypeStruct((part, n * rows), BF),
            jax.ShapeDtypeStruct((part, n * rows), BF),
            jax.ShapeDtypeStruct((width, n * rows), BF),
        ],
        compiler_params=pltpu.CompilerParams(vmem_limit_bytes=60 << 20),
        cost_estimate=pl.CostEstimate(
            flops=int(COST * 2 * width * part * rows * (2 * n + query_slots)),
            bytes_accessed=1 << 16,
            transcendentals=0,
        ),
        name="project",
    )(core, gain, scale, *slots, *[w_full] * 3)


def mlp_kernel(
    part, core_ref, near_ref, far_ref, w_ref, x_ref, cot_ref, gain_ref, bin_ref, bdown_ref, out_ref, keep_ref, give_ref,
    gmid_ref, ht_ref, nt_ref, gpre_ref, gml_ref, gain_out, bin_out, bdown_out, middle, normed,
    hidden, slope, g_ref,
):
    width = x_ref.shape[1]
    step = width // 5
    chunks = [slice(c * step, (c + 1) * step) for c in range(5)]
    down, inner, outer = 0, width, 2 * width
    core = core_ref[0]
    near_rows = pl.ds(pl.multiple_of(core * part, part), part)
    far_rows = pl.ds(pl.multiple_of((1 - core) * part, part), part)

    @pl.when(pl.program_id(0) == 0)
    def _():
        for ref in (gain_out, bin_out, bdown_out):
            ref[...] = jnp.zeros(ref.shape, F32)

    near, far = near_ref[...].T, far_ref[...].T
    for cols in chunks:
        at = slice(outer + cols.start, outer + cols.stop)
        middle[:, cols] = (
            x_ref[:, cols].astype(F32) + nn(near, w_ref[near_rows, at]) + nn(far, w_ref[far_rows, at])
        )
    mid = middle[...]
    inverse = lax.rsqrt(jnp.mean(mid * mid, -1, keepdims=True) + EPSILON)
    normed[...] = (mid * inverse * gain_ref[...]).astype(BF)
    nt_ref[...] = normed[...].T
    for cols in chunks:
        at = slice(inner + cols.start, inner + cols.stop)
        pre = nn(normed[...], w_ref[:, at]) + bin_ref[:, cols]
        sigma = 1.0 / (1.0 + jnp.exp(-pre))
        hidden[:, cols] = (pre * sigma).astype(BF)
        slope[:, cols] = sigma * (1.0 + pre * (1.0 - sigma))
    ht_ref[...] = hidden[...].T
    for cols in chunks:
        at = slice(down + cols.start, down + cols.stop)
        out_ref[:, cols] = (
            middle[:, cols] + nn(hidden[...], w_ref[:, at]) + bdown_ref[:, cols]
        ).astype(BF)
    for cols in chunks:
        gpre_ref[:, cols] = (
            nt(cot_ref[...], w_ref[cols, down : down + width]) * slope[:, cols]
        ).astype(BF)
    for cols in chunks:
        g_ref[:, cols] = nt(gpre_ref[...], w_ref[cols, inner : inner + width])
    bin_out[...] += jnp.sum(gpre_ref[...].astype(F32), 0, keepdims=True)
    cot = cot_ref[...].astype(F32)
    bdown_out[...] += jnp.sum(cot, 0, keepdims=True)
    turned = middle[...] * inverse
    gn = g_ref[...] * turned
    gain_out[...] += jnp.sum(gn, 0, keepdims=True)
    mean = jnp.mean(gn * gain_ref[...], -1, keepdims=True)
    gmid = cot + inverse * (g_ref[...] * gain_ref[...] - turned * mean)
    gmid_ref[...] = gmid
    gml_ref[...] = gmid.astype(BF)
    low = gml_ref[...]
    keep_ref[...] = nt(w_ref[near_rows, outer : outer + width], low).astype(BF)
    give_ref[...] = nt(w_ref[far_rows, outer : outer + width], low).astype(BF)


def mlp(near, far, weights, x, cot, core, gain, bias_in, bias_down):
    part, rows = far.shape
    width = x.shape[1]
    tile = 256
    once = pl.Buffered(1)
    row = pl.BlockSpec((tile, width), lambda i, c: (i, 0))
    feature = pl.BlockSpec((part, tile), lambda i, c: (0, i))
    wide = pl.BlockSpec((width, tile), lambda i, c: (0, i))
    vector = pl.BlockSpec((1, width), lambda i, c: (0, 0))
    return pl.pallas_call(
        functools.partial(mlp_kernel, part),
        grid_spec=pltpu.PrefetchScalarGridSpec(
            num_scalar_prefetch=1,
            grid=(rows // tile,),
            in_specs=[
                feature,
                feature,
                pl.BlockSpec(weights.shape, lambda i, c: (0, 0), pipeline_mode=once),
                row, row, vector, vector, vector,
            ],
            out_specs=[
                row, feature, feature, row, wide, wide, row, row, vector, vector, vector
            ],
            scratch_shapes=[
                pltpu.VMEM((tile, width), F32),
                pltpu.VMEM((tile, width), BF),
                pltpu.VMEM((tile, width), BF),
                pltpu.VMEM((tile, width), F32),
                pltpu.VMEM((tile, width), F32),
            ],
        ),
        out_shape=[
            jax.ShapeDtypeStruct((rows, width), BF),
            jax.ShapeDtypeStruct((part, rows), BF),
            jax.ShapeDtypeStruct((part, rows), BF),
            jax.ShapeDtypeStruct((rows, width), F32),
            jax.ShapeDtypeStruct((width, rows), BF),
            jax.ShapeDtypeStruct((width, rows), BF),
            jax.ShapeDtypeStruct((rows, width), BF),
            jax.ShapeDtypeStruct((rows, width), BF),
            jax.ShapeDtypeStruct((1, width), F32),
            jax.ShapeDtypeStruct((1, width), F32),
            jax.ShapeDtypeStruct((1, width), F32),
        ],
        compiler_params=pltpu.CompilerParams(vmem_limit_bytes=60 << 20),
        cost_estimate=pl.CostEstimate(
            flops=int(COST * 12 * rows * width * width), bytes_accessed=1 << 16, transcendentals=0
        ),
        name="mlp",
    )(core, near, far, weights, x, cot, gain, bias_in, bias_down)


def mlp_weight_kernel(
    core_ref, near_ref, far_ref, ht_ref, nt_ref, cot_ref, gpre_ref, gml_ref, out_ref
):
    which, part_at = pl.program_id(0), pl.program_id(1)

    @pl.when(which == 0)
    def _():
        out_ref[...] = nn(ht_ref[...], cot_ref[...]).astype(BF)

    @pl.when(which == 1)
    def _():
        out_ref[...] = nn(nt_ref[...], gpre_ref[...]).astype(BF)

    @pl.when((which == 2) & (part_at == core_ref[0]))
    def _():
        out_ref[...] = nn(near_ref[...], gml_ref[...]).astype(BF)

    @pl.when((which == 2) & (part_at != core_ref[0]))
    def _():
        out_ref[...] = nn(far_ref[...], gml_ref[...]).astype(BF)


def mlp_weights(near, far, ht, nrt, cot, gpre, gml, core):
    part, rows = far.shape
    width = cot.shape[1]
    once = pl.Buffered(1)

    def whole(shape):
        return pl.BlockSpec(shape, lambda j, r, c: (0,) * len(shape), pipeline_mode=once)

    return pl.pallas_call(
        mlp_weight_kernel,
        grid_spec=pltpu.PrefetchScalarGridSpec(
            num_scalar_prefetch=1,
            grid=(3, 2),
            in_specs=[
                whole((part, rows)),
                whole((part, rows)),
                pl.BlockSpec((part, rows), lambda j, r, c: (jnp.where(j == 0, r, 1), 0)),
                pl.BlockSpec((part, rows), lambda j, r, c: (jnp.where(j == 1, r, j // 2), 0)),
                whole((rows, width)),
                whole((rows, width)),
                whole((rows, width)),
            ],
            out_specs=pl.BlockSpec((part, width), lambda j, r, c: (r, j)),
        ),
        out_shape=jax.ShapeDtypeStruct((width, 3 * width), BF),
        compiler_params=pltpu.CompilerParams(vmem_limit_bytes=60 << 20),
        cost_estimate=pl.CostEstimate(
            flops=6 * rows * width * width, bytes_accessed=20 << 20, transcendentals=0
        ),
        name="mlp_weights",
    )(core, near, far, ht, nrt, cot, gpre, gml)


def load_keys(ref, place_ref, hd, tile, group, knat, kt=None):
    tiles = ref.shape[1] // tile
    for b in range(tiles):
        stretch = place_ref[tiles + b]
        piece = ref[:, b * tile : (b + 1) * tile]
        if kt is not None:
            kt[stretch] = piece
        if knat is not None:
            for h in range(group):
                knat[h, stretch] = piece[h * hd : (h + 1) * hd, :].T


def forward_kernel(
    hd, tile, ids_ref, place_ref, row_ref, col_ref, qt_ref, kt_ref, vt_ref, near_ref, far_ref,
    lse_ref, knat, vt, acc, m_ref, l_ref,
):
    group = qt_ref.shape[0] // hd
    tiles = vt.shape[0]
    load_keys(kt_ref, place_ref, hd, tile, group, knat)
    load_keys(vt_ref, place_ref, hd, tile, group, None, vt)
    per_half = near_ref.shape[1] // tile

    def one_tile(qi, carry):
        stretch = place_ref[tiles + qi]
        full, need = tile_counts(ids_ref, stretch, tile, tiles)
        qcol = pl.ds(pl.multiple_of(qi * tile, tile), tile)
        qpos = pl.ds(pl.multiple_of(stretch * tile, tile), tile)
        m_ref[...] = jnp.full(m_ref.shape, MASKED, F32)
        l_ref[...] = jnp.zeros(l_ref.shape, F32)
        acc[...] = jnp.zeros(acc.shape, F32)

        def step(ts, masked):
            if masked:
                allowed = [
                    col_ref[pl.ds(pl.multiple_of(t * tile, tile), tile), :] <= row_ref[:, qpos]
                    for t in ts
                ]
            scores = [
                [nn(knat[h, t], qt_ref[h * hd : (h + 1) * hd, qcol]) for t in ts]
                for h in range(group)
            ]
            for h in range(group):
                s = scores[h]
                if masked:
                    s = [jnp.where(ok, one, MASKED) for ok, one in zip(allowed, s)]
                old = m_ref[h]
                new = old
                for one in s:
                    new = jnp.maximum(new, jnp.max(one, 0, keepdims=True))
                p = [jnp.exp2(one - new) for one in s]
                alpha = jnp.exp2(old - new)
                total = l_ref[h] * alpha
                for one in p:
                    total = total + jnp.sum(one, 0, keepdims=True)
                l_ref[h] = total
                m_ref[h] = new
                out = acc[h] * alpha
                for t, one in zip(ts, p):
                    out = out + nn(vt[t, h * hd : (h + 1) * hd, :], one.astype(BF))
                acc[h] = out

        def full_step(i, c):
            step([2 * i, 2 * i + 1], False)
            return c

        def mask_step(i, c):
            step([2 * i, 2 * i + 1], True)
            return c

        lax.fori_loop(0, full // 2, full_step, 0)
        lax.fori_loop(full // 2, (need + 1) // 2, mask_step, 0)
        inner = pl.ds(pl.multiple_of((qi % per_half) * tile, tile), tile)
        for half, ref in enumerate((near_ref, far_ref)):

            @pl.when(qi // per_half == half)
            def _(ref=ref):
                for h in range(group):
                    ref[h * hd : (h + 1) * hd, inner] = (acc[h] / l_ref[h]).astype(BF)

        for h in range(group):
            lse_ref[h, :, qcol] = m_ref[h] + jnp.log2(l_ref[h])
        return carry

    lax.fori_loop(0, qt_ref.shape[1] // tile, one_tile, 0)


def backward_kernel(hd, tile, base, count, first, last, *refs):
    ids_ref, place_ref, row_ref, col_ref, qt_ref, kt_ref, vt_ref = refs[:7]
    near_ref, far_ref, onear_ref, ofar_ref, lse_ref = refs[7:12]
    if last:
        before_ref, scale_ref, dqt_ref, dkt_ref, dvt_ref, gs_ref = refs[12:18]
        knat, vnat, kt, dq, dk, dv, delta, dot = refs[18:]
    else:
        dqt_ref, dkt_ref, dvt_ref = refs[12:15]
        knat, vnat, kt, dq, dk, dv, delta, dot = refs[15:]
    tiles = kt_ref.shape[1] // tile
    group = qt_ref.shape[0] // hd

    def block_of(i):
        return pl.multiple_of(place_ref[place_ref[base + i]] * tile, tile)

    for i in range(count):
        cols = pl.ds(block_of(i), tile)
        kt[i] = kt_ref[:, cols]
        for h in range(group):
            hs = slice(h * hd, (h + 1) * hd)
            knat[h, i] = kt_ref[hs, cols].T
            vnat[h, i] = vt_ref[hs, cols].T
    per_half = near_ref.shape[1] // tile
    for half, (ref, o_ref) in enumerate(((near_ref, onear_ref), (far_ref, ofar_ref))):
        for b in range(per_half):
            cols = slice(b * tile, (b + 1) * tile)
            dot[half * per_half + b] = ref[:, cols]
            product = ref[:, cols].astype(F32) * o_ref[:, cols].astype(F32)
            for h in range(group):
                delta[half * per_half + b, h] = jnp.sum(
                    product[h * hd : (h + 1) * hd], 0, keepdims=True
                )
    dk[...] = jnp.zeros(dk.shape, F32)
    dv[...] = jnp.zeros(dv.shape, F32)
    if last:
        gs_ref[...] = jnp.zeros(gs_ref.shape, F32)

    def one_tile(qi, carry):
        stretch = place_ref[tiles + qi]
        low = ids_ref[stretch * tile]
        high = ids_ref[stretch * tile + tile - 1]
        full = jnp.int32(0)
        need = jnp.int32(0)
        for i in range(count):
            t = place_ref[base + i]
            full += (ids_ref[t * tile + tile - 1] <= low).astype(jnp.int32)
            need += (ids_ref[t * tile] <= high).astype(jnp.int32)
        qcol = pl.ds(pl.multiple_of(qi * tile, tile), tile)
        qpos = pl.ds(pl.multiple_of(stretch * tile, tile), tile)
        dq[...] = before_ref[:, qcol] if last else jnp.zeros(dq.shape, F32)

        def step(ts, masked):
            if masked:
                allowed = [
                    col_ref[pl.ds(pl.multiple_of(place_ref[base + t] * tile, tile), tile), :]
                    <= row_ref[:, qpos]
                    for t in ts
                ]

            def scores(h, t):
                hs = slice(h * hd, (h + 1) * hd)
                return nn(knat[h, t], qt_ref[hs, qcol]), nn(vnat[h, t], dot[qi, hs, :])

            order = [(h, i) for h in range(group) for i in range(len(ts))]
            ahead = scores(0, ts[0])
            for j, (h, i) in enumerate(order):
                hs = slice(h * hd, (h + 1) * hd)
                t = ts[i]
                s, dp = ahead
                if j + 1 < len(order):
                    ahead = scores(order[j + 1][0], ts[order[j + 1][1]])
                if masked:
                    s = jnp.where(allowed[i], s, MASKED)
                p = jnp.exp2(s - lse_ref[h, :, qcol])
                ds = (p * (dp - delta[qi, h])).astype(BF)
                dv[t, hs, :] += nt(dot[qi, hs, :], p.astype(BF))
                dk[t, hs, :] += nt(qt_ref[hs, qcol], ds)
                dq[hs, :] += nn(kt[t, hs, :], ds)

        def full_step(i, c):
            step([2 * i, 2 * i + 1], False)
            return c

        def mask_step(i, c):
            step([2 * i, 2 * i + 1], True)
            return c

        lax.fori_loop(0, full // 2, full_step, 0)
        lax.fori_loop(full // 2, (need + 1) // 2, mask_step, 0)
        if last:
            gs_ref[...] += jnp.sum(dq[...] * qt_ref[:, qcol].astype(F32), 1, keepdims=True)
            dqt_ref[:, qcol] = (dq[...] * scale_ref[...]).astype(BF)
        else:
            dqt_ref[:, qcol] = dq[...]
        return carry

    lax.fori_loop(0, qt_ref.shape[1] // tile, one_tile, 0)
    for i in range(count):
        cols = pl.ds(pl.multiple_of(block_of(i) - first * tile, tile), tile)
        dkt_ref[:, cols] = (dk[i] * (1.0 / LOG2E)).astype(BF)
        dvt_ref[:, cols] = dv[i].astype(BF)


def attention_specs(nq, nk, hd, group, at):
    size = group * hd
    return (
        [
            pl.BlockSpec(memory_space=pltpu.SMEM),
            pl.BlockSpec(memory_space=pltpu.SMEM),
            pl.BlockSpec((1, nk), lambda i: (0, 0)),
            pl.BlockSpec((nk, 1), lambda i: (0, 0)),
            pl.BlockSpec((size, nq), lambda i: (i + at, 0)),
            pl.BlockSpec((size, nk), lambda i: (i + at, 0)),
            pl.BlockSpec((size, nk), lambda i: (i + at, 0)),
        ],
        pl.BlockSpec((size, nq // 2), lambda i: (i + at, 0)),
        pl.BlockSpec((group, 1, nq), lambda i: (i + at, 0, 0)),
    )


def attention_forward(ids, col, place, qt, kt, vt, hd, tile):
    heads = qt.shape[0] // hd
    nq, nk = qt.shape[1], kt.shape[1]
    group = HEADS_AT_ONCE
    common, halves, rows = attention_specs(nq, nk, hd, group, 0)
    pairs = heads * nq * nk * 0.6
    return pl.pallas_call(
        functools.partial(forward_kernel, hd, tile),
        grid=(heads // group,),
        in_specs=common,
        out_specs=[halves, halves, rows],
        out_shape=[
            jax.ShapeDtypeStruct((heads * hd, nq // 2), BF),
            jax.ShapeDtypeStruct((heads * hd, nq // 2), BF),
            jax.ShapeDtypeStruct((heads, 1, nq), F32),
        ],
        scratch_shapes=[
            pltpu.VMEM((group, nk // tile, tile, hd), BF),
            pltpu.VMEM((nk // tile, group * hd, tile), BF),
            pltpu.VMEM((group, hd, tile), F32),
            pltpu.VMEM((group, 1, tile), F32),
            pltpu.VMEM((group, 1, tile), F32),
        ],
        compiler_params=pltpu.CompilerParams(vmem_limit_bytes=60 << 20),
        cost_estimate=pl.CostEstimate(
            flops=int(COST * pairs * 1024), bytes_accessed=1 << 16, transcendentals=int(COST * pairs)
        ),
        name="attention_forward",
    )(ids, place, ids.reshape(1, -1), col, qt, kt, vt)


def attention_backward(
    ids, col, place, qt, kt, vt, near, far, onear, ofar, lse, hd, tile, before=None, scale=None
):
    heads = qt.shape[0] // hd
    nq, nk = qt.shape[1], kt.shape[1]
    group = HEADS_AT_ONCE
    size = group * hd
    last = before is not None
    early = nq // tile
    tiles = nk // tile
    count, first = (early, 0) if last else (tiles - early, early)
    base = 2 * tiles + (0 if last else early)
    common, halves, rows = attention_specs(nq, nk, hd, group, 0)
    wide = pl.BlockSpec((size, nq), lambda i: (i, 0))
    keys = pl.BlockSpec((size, count * tile), lambda i: (i, 0))
    one = pl.BlockSpec((size, 1), lambda i: (i, 0))
    pairs = heads * nq * count * tile * 0.6
    return pl.pallas_call(
        functools.partial(backward_kernel, hd, tile, base, count, first, last),
        grid=(heads // group,),
        in_specs=[*common, halves, halves, halves, halves, rows, *([wide, one] if last else [])],
        out_specs=[wide, keys, keys, *([one] if last else [])],
        out_shape=[
            jax.ShapeDtypeStruct((heads * hd, nq), BF if last else F32),
            jax.ShapeDtypeStruct((heads * hd, count * tile), BF),
            jax.ShapeDtypeStruct((heads * hd, count * tile), BF),
            *([jax.ShapeDtypeStruct((heads * hd, 1), F32)] if last else []),
        ],
        scratch_shapes=[
            pltpu.VMEM((group, count, tile, hd), BF),
            pltpu.VMEM((group, count, tile, hd), BF),
            pltpu.VMEM((count, size, tile), BF),
            pltpu.VMEM((size, tile), F32),
            pltpu.VMEM((count, size, tile), F32),
            pltpu.VMEM((count, size, tile), F32),
            pltpu.VMEM((nq // tile, group, 1, tile), F32),
            pltpu.VMEM((nq // tile, size, tile), BF),
        ],
        compiler_params=pltpu.CompilerParams(vmem_limit_bytes=60 << 20),
        cost_estimate=pl.CostEstimate(
            flops=int(pairs * 2560), bytes_accessed=16 << 20, transcendentals=int(pairs)
        ),
        name="attention_backward",
    )(
        ids, place, ids.reshape(1, -1), col, qt, kt, vt, near, far, onear, ofar, lse,
        *([before, scale] if last else []),
    )


def weight_kernel(size, nq, at_ref, xt_ref, dqt_ref, dka_ref, dva_ref, dkb_ref, dvb_ref, *out_refs):
    for m, ref in enumerate(out_refs):

        @pl.when(pl.program_id(0) == m)
        def _(ref=ref):
            early = jnp.concatenate([dka_ref[...], dva_ref[...]], 0)
            late = jnp.concatenate([dkb_ref[...], dvb_ref[...]], 0)
            ref[:, : 2 * size] = (nt(xt_ref[:, :nq], early) + nt(xt_ref[:, nq:], late)).astype(BF)
            ref[:, 2 * size :] = nt(xt_ref[:, :nq], dqt_ref[...]).astype(BF)


def weight_gradient(xt, dqt, early, late, at, pieces, which):
    width, nk = xt.shape
    part, nq = dqt.shape
    size = part // 2
    rows = width // pieces
    once = pl.Buffered(1)

    def heads(cols):
        return pl.BlockSpec((size, cols), lambda i, a: (which, 0), pipeline_mode=once)

    return pl.pallas_call(
        functools.partial(weight_kernel, size, nq),
        grid_spec=pltpu.PrefetchScalarGridSpec(
            num_scalar_prefetch=1,
            grid=(pieces,),
            in_specs=[
                pl.BlockSpec((rows, nk), lambda i, a: (a[i], 0)),
                heads(nq), heads(nq), heads(nq), heads(nk - nq), heads(nk - nq),
            ],
            out_specs=[pl.BlockSpec((rows, 3 * size), lambda i, a: (0, 0))] * pieces,
        ),
        out_shape=[jax.ShapeDtypeStruct((rows, 3 * size), BF)] * pieces,
        compiler_params=pltpu.CompilerParams(vmem_limit_bytes=60 << 20),
        cost_estimate=pl.CostEstimate(
            flops=2 * width * size * (2 * nk + nq), bytes_accessed=12 << 20, transcendentals=0
        ),
        name="weight_gradient",
    )(at, xt, dqt, *early, *late)


def dx_kernel(part, queries, n, core_ref, *refs):
    dk_ref, dv_ref, wk_ref, wv_ref, gain_ref = refs[:5]
    x_refs = refs[5 : 5 + n]
    rest = refs[5 + n :]
    if queries:
        dq_ref, wq_ref = rest[:2]
        rest = rest[2:]
    dx_refs, (gg_ref, g_ref, xs) = rest[:n], rest[n:]
    i = pl.program_id(0)
    tile, width = xs.shape
    step = width // 5
    dk = dk_ref[...].T
    dv = dv_ref[...].T
    if queries:
        dq = dq_ref[...].T
    for c in range(5):
        cols = slice(c * step, (c + 1) * step)
        g = nt(dk, wk_ref[cols, :]) + nt(dv, wv_ref[cols, :])
        if queries:
            g = g + nt(dq, wq_ref[cols, :])
        g_ref[:, cols] = g

    @pl.when(i == 0)
    def _():
        gg_ref[...] = jnp.zeros(gg_ref.shape, F32)

    per_slot = x_refs[0].shape[0] // tile
    for s in range(n):

        @pl.when(i // per_slot == s)
        def _(s=s):
            xs[...] = x_refs[s][pl.ds(pl.multiple_of((i % per_slot) * tile, tile), tile), :]

    x = xs[...].astype(F32)
    inverse = lax.rsqrt(jnp.mean(x * x, -1, keepdims=True) + EPSILON)
    normed = x * inverse
    g = g_ref[...]
    gn = g * normed
    gg_ref[...] += jnp.sum(gn, 0, keepdims=True)
    scaled = g * gain_ref[...]
    mean = jnp.mean(gn * gain_ref[...], -1, keepdims=True)
    out = (inverse * (scaled - normed * mean)).astype(BF)
    for s in range(n):

        @pl.when(i // per_slot == s)
        def _(s=s):
            dx_refs[s][...] = out


def input_gradient(dkvs, dqs, w_full, slots, core, gain):
    part = dkvs[0].shape[0]
    n = len(slots)
    rows, width = slots[0].shape
    tile = 256
    per_slot = rows // tile
    once = pl.Buffered(1)
    dkv = pl.BlockSpec((part, tile), lambda i, c: (0, i))

    def weight(j):
        return pl.BlockSpec(
            (width, part), lambda i, c, j=j: (0, 2 * j + c[0]), pipeline_mode=once
        )

    specs = [
        dkv, dkv, weight(1), weight(2), pl.BlockSpec((1, width), lambda i, c: (0, 0)),
        *[pl.BlockSpec((rows, width), lambda i, c: (0, 0), pipeline_mode=once)] * n,
    ]
    operands = [*dkvs, w_full, w_full, gain, *slots]
    if dqs:
        specs += [dkv, weight(0)]
        operands += [*dqs, w_full]
    return pl.pallas_call(
        functools.partial(dx_kernel, part, bool(dqs), n),
        grid_spec=pltpu.PrefetchScalarGridSpec(
            num_scalar_prefetch=1,
            grid=(n * rows // tile,),
            in_specs=specs,
            out_specs=[
                *[
                    pl.BlockSpec(
                        (tile, width),
                        lambda i, c, s=s: (jnp.clip(i - s * per_slot, 0, per_slot - 1), 0),
                    )
                    for s in range(n)
                ],
                pl.BlockSpec((1, width), lambda i, c: (0, 0)),
            ],
            scratch_shapes=[pltpu.VMEM((tile, width), F32), pltpu.VMEM((tile, width), BF)],
        ),
        out_shape=[
            *[jax.ShapeDtypeStruct((rows, width), BF)] * n,
            jax.ShapeDtypeStruct((1, width), F32),
        ],
        compiler_params=pltpu.CompilerParams(vmem_limit_bytes=60 << 20),
        cost_estimate=pl.CostEstimate(
            flops=int(COST * 2 * width * n * rows * part * (3 if dqs else 2)),
            bytes_accessed=1 << 16,
            transcendentals=0,
        ),
        name="input_gradient",
    )(core, *operands)


class Plan:
    def __init__(self, dp, ctx):
        self.dp, self.ctx = dp, ctx
        self.half = ctx // 2

    def index(self, pair, core, z):
        return (pair * 2 + core) * self.ctx + z

    def perm(self, to):
        out = []
        for d in range(self.dp):
            for z in range(self.ctx):
                got = to(d // 2, d % 2, z)
                if got is not None:
                    out.append((self.index(d // 2, d % 2, z), self.index(*got)))
        return out

    def home(self, core, z):
        return core == z // self.half

    def turned(self, z, k):
        first = z // self.half * self.half
        return first + (z - first + k) % self.half

    def core_swap(self):
        return self.perm(lambda p, c, z: (p, 1 - c, z))

    def pair_swap(self, mask):
        return self.perm(lambda p, c, z: (p ^ mask, c, z))

    def line_swap(self, mask):
        return self.perm(lambda p, c, z: (p, c, z ^ mask))

    def line_in(self, s):
        last = self.ctx - 1
        to = {s: s + 1, last - s: last - s - 1}
        return self.perm(lambda p, c, z: (p, c, to[z]) if z in to else None)

    def line_out(self, s):
        last = self.ctx - 1
        to = {s + 1: s, last - s - 1: last - s}
        return self.perm(lambda p, c, z: (p, c, to[z]) if z in to else None)

    def line_middle(self):
        to = {self.half - 1: self.half, self.half: self.half - 1}
        return self.perm(lambda p, c, z: (p, c, to[z]) if z in to else None)

    def mirror(self):
        return self.perm(
            lambda p, c, z: None if self.home(c, z) else (p, 1 - c, self.ctx - 1 - z)
        )

    def mirror_or_turn(self, k):
        return self.perm(
            lambda p, c, z: (p, c, self.turned(z, k))
            if self.home(c, z)
            else (p, 1 - c, self.ctx - 1 - z)
        )

    def turn(self, k, away_only):
        return self.perm(
            lambda p, c, z: None
            if away_only and self.home(c, z)
            else (p, c, self.turned(z, k))
        )

    def shard(self, core, z, k, mine):
        chip = self.turned(z, -k)
        at_home = self.home(core, z) if mine else not self.home(core, z)
        return chip if at_home else self.ctx - 1 - chip

    def places(self):
        table = np.zeros((self.dp, self.ctx, 6 * self.ctx), np.int32)
        for d in range(self.dp):
            for z in range(self.ctx):
                slots = [
                    self.shard(d % 2, z, k, mine) for k in range(self.half) for mine in (True, False)
                ]
                stretches = [s for shard in slots for s in (shard, 2 * self.ctx - 1 - shard)]
                for block, stretch in enumerate(stretches):
                    table[d, z, stretch] = block
                    table[d, z, 2 * self.ctx + block] = stretch
                table[d, z, 4 * self.ctx :] = sorted(stretches[:4]) + sorted(stretches[4:])
        return table.reshape(self.dp * self.ctx, 6 * self.ctx)


def send(value, pairs):
    return lax.ppermute(value, AXES, pairs)


def tie(*values):
    return lax.optimization_barrier(values)


def line_inward(value, plan, kind):
    total = value.astype(F32)
    for s in range(plan.half - 2):
        total = total + send(total.astype(kind), plan.line_in(s)).astype(F32)
    if plan.half == 1:
        return total, jnp.zeros_like(total, kind)
    return total, send(total.astype(kind), plan.line_in(plan.half - 2))


def line_across(held, came, plan, kind):
    sent = (held + came.astype(F32)).astype(kind)
    return sent, send(sent, plan.line_middle())


def line_joined(sent, came):
    return (sent.astype(F32) + came.astype(F32)).astype(sent.dtype)


def line_outward(total, plan, z):
    for s in reversed(range(plan.half - 1)):
        back = send(total, plan.line_out(s))
        total = jnp.where((z == s) | (z == plan.ctx - 1 - s), back, total)
    return total


def body(
    tokens_in, block_ids, w_qkv, w_out, w_in, w_down, gain_attn, gain_mlp, bias_in, bias_down,
    query_scale, cotangent,
):
    n = lax.axis_size("ctx")
    plan = Plan(lax.axis_size("dp"), n)
    half = plan.half
    z = lax.axis_index("ctx")
    core = lax.axis_index("dp") % 2
    pair = lax.axis_index("dp") // 2
    pairs = plan.dp // 2
    home = core == z // half
    rows = tokens_in.shape[1]
    width = tokens_in.shape[2]
    hd = query_scale.shape[0]
    heads = width // hd
    part = width // 2
    tile = rows // 2
    wrows = w_qkv.shape[0]
    core_swap = plan.core_swap()

    own = tokens_in[0]
    first = send(own, plan.mirror_or_turn(1))
    token0 = jnp.where(home, own, first)
    second = send(token0, plan.turn(1, True))
    mine = [token0, jnp.where(home, first, second)]
    for k in range(2, half):
        mine.append(send(token0, plan.turn(k, False)))
    theirs = [send(m, core_swap) for m in mine]
    slots = [a for both in zip(mine, theirs) for a in both]

    full_qkv = lax.all_gather(w_qkv, "dp", axis=0, tiled=True)
    at = jnp.stack([pair ^ mask for mask in range(pairs)]).astype(jnp.int32)
    core_at = core.astype(jnp.int32).reshape(1)

    ids = jnp.where(home, block_ids[0], send(block_ids[0], core_swap))
    place = lax.dynamic_index_in_dim(
        jnp.asarray(plan.places()), lax.axis_index("dp") * n + z, 0, False
    )
    col = ids.reshape(-1, 1)

    gain_one = gain_attn.astype(F32)
    gain_two = gain_mlp.astype(F32)
    scale_exp = jnp.exp(query_scale.astype(F32))
    scale_dim = SOFT_FACTOR / math.sqrt(hd) * jnp.log1p(scale_exp)
    scale_vec = jnp.tile(scale_dim, heads // 2)[:, None]
    weights = lax.all_gather(
        jnp.concatenate([w_down, w_in, w_out], 1), "dp", axis=0, tiled=True
    )
    qt, kt, vt, xt = project(
        slots, full_qkv, core_at, gain_one.reshape(1, -1), scale_vec * LOG2E
    )
    grad_low = send(tie(cotangent[0], slots[-1])[0], plan.mirror())
    onear, ofar, lse = attention_forward(ids, col, place, qt, kt, vt, hd, tile)
    onear, ofar, grad_low = tie(onear, ofar, grad_low)
    grad_low = jnp.where(home, cotangent[0], grad_low)
    o_got = send(ofar, core_swap)

    (
        output, to_keep, to_give, grad_middle, hidden_t, normed_t, grad_pre, grad_mid_low,
        grad_gain_two, grad_bin, grad_bdown,
    ) = mlp(
        onear, o_got, weights, token0, grad_low, core_at, gain_two.reshape(1, -1),
        bias_in.astype(F32).reshape(1, -1), bias_down.astype(F32).reshape(1, -1),
    )
    far = send(to_give, core_swap)
    away_output = send(output, plan.mirror())
    joined = mlp_weights(onear, o_got, hidden_t, normed_t, grad_low, grad_pre, grad_mid_low, core_at)
    early_qt, joined, far = tie(qt, joined, far)
    scattered = lax.psum_scatter(joined, "dp", scatter_dimension=0, tiled=True)

    def backward(queries, **rest):
        return attention_backward(
            ids, col, place, queries, kt, vt, to_keep, far, onear, ofar, lse, hd, tile, **rest
        )

    def to_owners(grads):
        return [send(grads[m], plan.pair_swap(m)) for m in range(1, pairs)]

    def add_up(grads, came):
        total = grads[0].astype(F32)
        for one in came:
            total = total + one.astype(F32)
        return total

    gain_row = gain_one.reshape(1, -1)
    dq_part, *late_kv = backward(early_qt)
    *late_dx, gain_late = input_gradient(late_kv, (), full_qkv, slots[2:], core_at, gain_row)
    dq_part, away_output, *late_dx = tie(dq_part, away_output, *late_dx)
    output = jnp.where(home, output, away_output)
    late_got = [
        send(late_dx[2 * k + 1], core_swap) for k in range(half - 1)
    ]
    dq_part, *late_got = tie(dq_part, *late_got)
    turned = []
    for k in range(half - 1):
        mine = late_dx[2 * k].astype(F32)
        turned.append(
            send((mine + late_got[k].astype(F32)).astype(BF), plan.turn(-k - 1, False))
        )
    dqt, dk_early, dv_early, gs = backward(qt, before=dq_part, scale=scale_vec)
    dqt, dk_early, dv_early, scattered, *turned = tie(
        dqt, dk_early, dv_early, scattered, *turned
    )
    held_o, line_o = line_inward(scattered, plan, BF)
    early_kv = (dk_early, dv_early)
    grads_a = weight_gradient(xt, dqt, early_kv, late_kv, at, pairs, 0)
    later_dq, *grads_a = tie(dqt, *grads_a)
    came_a = to_owners(grads_a)
    near_dx, far_dx, gain_early = input_gradient(
        early_kv, (later_dq,), full_qkv, slots[:2], core_at, gain_row
    )
    near_dx, far_dx, gain_early, last_dq, line_o, *came_a = tie(
        near_dx, far_dx, gain_early, dqt, line_o, *came_a
    )
    got = send(far_dx, core_swap)
    held_a, line_a = line_inward(add_up(grads_a, came_a), plan, BF)
    held_o, line_o = line_across(held_o, line_o, plan, BF)
    grads_b = weight_gradient(xt, last_dq, early_kv, late_kv, at, pairs, 1)
    scale_slope = SOFT_FACTOR / math.sqrt(hd) * scale_exp / (1.0 + scale_exp)
    grad_scale = jnp.sum(gs.reshape(heads // 2, hd), 0)
    grad_scale = grad_scale * scale_slope / (scale_dim * LOG2E)
    small = jnp.concatenate(
        [
            *(v.reshape(-1) for v in (gain_late + gain_early, grad_gain_two, grad_bin, grad_bdown)),
            grad_scale,
        ]
    )
    small_size = small.shape[0]
    small = jnp.pad(small, (0, -small_size % 1024)).reshape(-1, 128)
    small = small + send(small, core_swap)
    mask = 1
    while mask < pairs:
        small = small + send(small, plan.pair_swap(mask))
        mask *= 2
    got, line_a, small, *grads_b = tie(got, line_a, small, *grads_b)
    came_b = to_owners(grads_b)
    total = near_dx.astype(F32) + got.astype(F32) + grad_middle
    for one in turned:
        total = total + one.astype(F32)
    last = send(total.astype(BF), plan.mirror())
    held_a, line_a = line_across(held_a, line_a, plan, BF)
    line_a, line_o, *came_b = tie(line_a, line_o, *came_b)
    held_b, line_b = line_inward(add_up(grads_b, came_b), plan, BF)
    line_a = line_outward(line_joined(held_a, line_a), plan, z)
    others = line_outward(line_joined(held_o, line_o), plan, z)

    line_b, line_a = tie(line_b, line_a)
    held_b, line_b = line_across(held_b, line_b, plan, BF)

    def owned_rows(value):
        keep = lax.dynamic_slice_in_dim(value, core * wrows, wrows, 0)
        give = lax.dynamic_slice_in_dim(value, (1 - core) * wrows, wrows, 0)
        came = send(give, core_swap)
        return jnp.where(core == 0, keep, came), jnp.where(core == 0, came, keep)

    line_b, line_a, last, small = tie(line_b, line_a, last, small)
    swapped_a = owned_rows(line_a)
    line_b = line_outward(line_joined(held_b, line_b), plan, z)
    came = send(small, plan.line_swap(1))
    line_b, others, came = tie(line_b, others, came)
    small = small + came
    mask = 2
    while mask < n:
        small = small + send(small, plan.line_swap(mask))
        mask *= 2
    small = small.reshape(-1)
    grad_tokens = jnp.where(home, total, last.astype(F32))
    others = others.astype(F32)
    swapped = (swapped_a, owned_rows(line_b))
    size = part // 2
    owned_qkv = jnp.concatenate(
        [
            swapped[g][c][:, which * size : (which + 1) * size].astype(F32)
            for which in (2, 0, 1)
            for c in range(2)
            for g in range(2)
        ],
        1,
    )

    return (
        output[None],
        grad_tokens[None],
        owned_qkv,
        others[:, 2 * width :],
        others[:, width : 2 * width],
        others[:, :width],
        small[:width],
        small[width : 2 * width],
        small[2 * width : 3 * width],
        small[3 * width : 4 * width],
        small[4 * width : small_size],
    )


def solution(mesh):
    split = P("dp", "ctx", None)
    weight = P("dp", None)
    return jax.shard_map(
        body,
        mesh=mesh,
        in_specs=(split, weight, weight, weight, weight, weight, P(), P(), P(), P(), P(), split),
        out_specs=(split, split, weight, weight, weight, weight, P(), P(), P(), P(), P()),
        check_vma=False,
    )
```

```python
import functools
import math

import jax
import jax.numpy as jnp
import numpy as np
from jax import lax
from jax.experimental import pallas as pl
from jax.experimental.pallas import tpu as pltpu
from jax.sharding import PartitionSpec as P

EPSILON = 1e-06
SOFT_FACTOR = 1.442695041
LOG2E = 1.4426950408889634
MASKED = -1e30
HEADS_AT_ONCE = 4
COST = 1.0
AXES = ("dp", "ctx")
BF = jnp.bfloat16
F32 = jnp.float32


def nn(a, b):
    return lax.dot_general(a, b, (((1,), (0,)), ((), ())), preferred_element_type=F32)


def nt(a, b):
    return lax.dot_general(a, b, (((1,), (1,)), ((), ())), preferred_element_type=F32)


def tile_counts(ids_ref, stretch, tile, tiles):
    low = ids_ref[stretch * tile]
    high = ids_ref[stretch * tile + tile - 1]
    full = jnp.int32(0)
    need = jnp.int32(0)
    for t in range(tiles):
        full += (ids_ref[t * tile + tile - 1] <= low).astype(jnp.int32)
        need += (ids_ref[t * tile] <= high).astype(jnp.int32)
    return full, need


def project_kernel(part, query_slots, n, core_ref, gain_ref, scale_ref, *refs):
    x_refs, w_refs = refs[:n], refs[n : n + 3]
    qt_ref, kt_ref, vt_ref, xt_ref, wt, xs = refs[n + 3 :]
    i = pl.program_id(0)

    @pl.when(i == 0)
    def _():
        for j, ref in enumerate(w_refs):
            wt[j * part : (j + 1) * part, :] = ref[...].T

    for s in range(n):

        @pl.when(i == s)
        def _(s=s):
            xs[...] = x_refs[s][...]

    x = xs[...].astype(F32)
    inverse = lax.rsqrt(jnp.mean(x * x, -1, keepdims=True) + EPSILON)
    xt_ref[...] = (x * inverse * gain_ref[...]).astype(BF).T
    kt_ref[...] = nn(wt[part : 2 * part, :], xt_ref[...]).astype(BF)
    vt_ref[...] = nn(wt[2 * part :, :], xt_ref[...]).astype(BF)

    @pl.when(i < query_slots)
    def _():
        qt_ref[...] = (nn(wt[:part, :], xt_ref[...]) * scale_ref[...]).astype(BF)


def project(slots, w_full, core, gain, scale):
    n = len(slots)
    rows, width = slots[0].shape
    part = width // 2
    query_slots = 2
    once = pl.Buffered(1)
    return pl.pallas_call(
        functools.partial(project_kernel, part, query_slots, n),
        grid_spec=pltpu.PrefetchScalarGridSpec(
            num_scalar_prefetch=1,
            grid=(n,),
            in_specs=[
                pl.BlockSpec((1, width), lambda i, c: (0, 0)),
                pl.BlockSpec((part, 1), lambda i, c: (0, 0)),
                *[pl.BlockSpec((rows, width), lambda i, c: (0, 0), pipeline_mode=once)] * n,
                *[
                    pl.BlockSpec(
                        (width, part), lambda i, c, j=j: (0, 2 * j + c[0]), pipeline_mode=once
                    )
                    for j in range(3)
                ],
            ],
            out_specs=[
                pl.BlockSpec((part, rows), lambda i, c: (0, jnp.minimum(i, query_slots - 1))),
                pl.BlockSpec((part, rows), lambda i, c: (0, i)),
                pl.BlockSpec((part, rows), lambda i, c: (0, i)),
                pl.BlockSpec((width, rows), lambda i, c: (0, i)),
            ],
            scratch_shapes=[pltpu.VMEM((3 * part, width), BF), pltpu.VMEM((rows, width), BF)],
        ),
        out_shape=[
            jax.ShapeDtypeStruct((part, query_slots * rows), BF),
            jax.ShapeDtypeStruct((part, n * rows), BF),
            jax.ShapeDtypeStruct((part, n * rows), BF),
            jax.ShapeDtypeStruct((width, n * rows), BF),
        ],
        compiler_params=pltpu.CompilerParams(vmem_limit_bytes=60 << 20),
        cost_estimate=pl.CostEstimate(
            flops=int(COST * 2 * width * part * rows * (2 * n + query_slots)),
            bytes_accessed=1 << 16,
            transcendentals=0,
        ),
        name="project",
    )(core, gain, scale, *slots, *[w_full] * 3)


def mlp_kernel(
    part, core_ref, near_ref, far_ref, w_ref, x_ref, cot_ref, gain_ref, bin_ref, bdown_ref, out_ref, keep_ref, give_ref,
    gmid_ref, ht_ref, nt_ref, gpre_ref, gml_ref, gain_out, bin_out, bdown_out, middle, normed,
    hidden, slope, g_ref,
):
    width = x_ref.shape[1]
    step = width // 5
    chunks = [slice(c * step, (c + 1) * step) for c in range(5)]
    down, inner, outer = 0, width, 2 * width
    core = core_ref[0]
    near_rows = pl.ds(pl.multiple_of(core * part, part), part)
    far_rows = pl.ds(pl.multiple_of((1 - core) * part, part), part)

    @pl.when(pl.program_id(0) == 0)
    def _():
        for ref in (gain_out, bin_out, bdown_out):
            ref[...] = jnp.zeros(ref.shape, F32)

    near, far = near_ref[...].T, far_ref[...].T
    for cols in chunks:
        at = slice(outer + cols.start, outer + cols.stop)
        middle[:, cols] = (
            x_ref[:, cols].astype(F32) + nn(near, w_ref[near_rows, at]) + nn(far, w_ref[far_rows, at])
        )
    mid = middle[...]
    inverse = lax.rsqrt(jnp.mean(mid * mid, -1, keepdims=True) + EPSILON)
    normed[...] = (mid * inverse * gain_ref[...]).astype(BF)
    nt_ref[...] = normed[...].T
    for cols in chunks:
        at = slice(inner + cols.start, inner + cols.stop)
        pre = nn(normed[...], w_ref[:, at]) + bin_ref[:, cols]
        sigma = 1.0 / (1.0 + jnp.exp(-pre))
        hidden[:, cols] = (pre * sigma).astype(BF)
        slope[:, cols] = sigma * (1.0 + pre * (1.0 - sigma))
    ht_ref[...] = hidden[...].T
    for cols in chunks:
        at = slice(down + cols.start, down + cols.stop)
        out_ref[:, cols] = (
            middle[:, cols] + nn(hidden[...], w_ref[:, at]) + bdown_ref[:, cols]
        ).astype(BF)
    for cols in chunks:
        gpre_ref[:, cols] = (
            nt(cot_ref[...], w_ref[cols, down : down + width]) * slope[:, cols]
        ).astype(BF)
    for cols in chunks:
        g_ref[:, cols] = nt(gpre_ref[...], w_ref[cols, inner : inner + width])
    bin_out[...] += jnp.sum(gpre_ref[...].astype(F32), 0, keepdims=True)
    cot = cot_ref[...].astype(F32)
    bdown_out[...] += jnp.sum(cot, 0, keepdims=True)
    turned = middle[...] * inverse
    gn = g_ref[...] * turned
    gain_out[...] += jnp.sum(gn, 0, keepdims=True)
    mean = jnp.mean(gn * gain_ref[...], -1, keepdims=True)
    gmid = cot + inverse * (g_ref[...] * gain_ref[...] - turned * mean)
    gmid_ref[...] = gmid
    gml_ref[...] = gmid.astype(BF)
    low = gml_ref[...]
    keep_ref[...] = nt(w_ref[near_rows, outer : outer + width], low).astype(BF)
    give_ref[...] = nt(w_ref[far_rows, outer : outer + width], low).astype(BF)


def mlp(near, far, weights, x, cot, core, gain, bias_in, bias_down):
    part, rows = far.shape
    width = x.shape[1]
    tile = 256
    once = pl.Buffered(1)
    row = pl.BlockSpec((tile, width), lambda i, c: (i, 0))
    feature = pl.BlockSpec((part, tile), lambda i, c: (0, i))
    wide = pl.BlockSpec((width, tile), lambda i, c: (0, i))
    vector = pl.BlockSpec((1, width), lambda i, c: (0, 0))
    return pl.pallas_call(
        functools.partial(mlp_kernel, part),
        grid_spec=pltpu.PrefetchScalarGridSpec(
            num_scalar_prefetch=1,
            grid=(rows // tile,),
            in_specs=[
                feature,
                feature,
                pl.BlockSpec(weights.shape, lambda i, c: (0, 0), pipeline_mode=once),
                row, row, vector, vector, vector,
            ],
            out_specs=[
                row, feature, feature, row, wide, wide, row, row, vector, vector, vector
            ],
            scratch_shapes=[
                pltpu.VMEM((tile, width), F32),
                pltpu.VMEM((tile, width), BF),
                pltpu.VMEM((tile, width), BF),
                pltpu.VMEM((tile, width), F32),
                pltpu.VMEM((tile, width), F32),
            ],
        ),
        out_shape=[
            jax.ShapeDtypeStruct((rows, width), BF),
            jax.ShapeDtypeStruct((part, rows), BF),
            jax.ShapeDtypeStruct((part, rows), BF),
            jax.ShapeDtypeStruct((rows, width), F32),
            jax.ShapeDtypeStruct((width, rows), BF),
            jax.ShapeDtypeStruct((width, rows), BF),
            jax.ShapeDtypeStruct((rows, width), BF),
            jax.ShapeDtypeStruct((rows, width), BF),
            jax.ShapeDtypeStruct((1, width), F32),
            jax.ShapeDtypeStruct((1, width), F32),
            jax.ShapeDtypeStruct((1, width), F32),
        ],
        compiler_params=pltpu.CompilerParams(vmem_limit_bytes=60 << 20),
        cost_estimate=pl.CostEstimate(
            flops=int(COST * 12 * rows * width * width), bytes_accessed=1 << 16, transcendentals=0
        ),
        name="mlp",
    )(core, near, far, weights, x, cot, gain, bias_in, bias_down)


def mlp_weight_kernel(
    core_ref, near_ref, far_ref, ht_ref, nt_ref, cot_ref, gpre_ref, gml_ref, out_ref
):
    which, part_at = pl.program_id(0), pl.program_id(1)

    @pl.when(which == 0)
    def _():
        out_ref[...] = nn(ht_ref[...], cot_ref[...]).astype(BF)

    @pl.when(which == 1)
    def _():
        out_ref[...] = nn(nt_ref[...], gpre_ref[...]).astype(BF)

    @pl.when((which == 2) & (part_at == core_ref[0]))
    def _():
        out_ref[...] = nn(near_ref[...], gml_ref[...]).astype(BF)

    @pl.when((which == 2) & (part_at != core_ref[0]))
    def _():
        out_ref[...] = nn(far_ref[...], gml_ref[...]).astype(BF)


def mlp_weights(near, far, ht, nrt, cot, gpre, gml, core):
    part, rows = far.shape
    width = cot.shape[1]
    once = pl.Buffered(1)

    def whole(shape):
        return pl.BlockSpec(shape, lambda j, r, c: (0,) * len(shape), pipeline_mode=once)

    return pl.pallas_call(
        mlp_weight_kernel,
        grid_spec=pltpu.PrefetchScalarGridSpec(
            num_scalar_prefetch=1,
            grid=(3, 2),
            in_specs=[
                whole((part, rows)),
                whole((part, rows)),
                pl.BlockSpec((part, rows), lambda j, r, c: (jnp.where(j == 0, r, 1), 0)),
                pl.BlockSpec((part, rows), lambda j, r, c: (jnp.where(j == 1, r, j // 2), 0)),
                whole((rows, width)),
                whole((rows, width)),
                whole((rows, width)),
            ],
            out_specs=pl.BlockSpec((part, width), lambda j, r, c: (r, j)),
        ),
        out_shape=jax.ShapeDtypeStruct((width, 3 * width), BF),
        compiler_params=pltpu.CompilerParams(vmem_limit_bytes=60 << 20),
        cost_estimate=pl.CostEstimate(
            flops=6 * rows * width * width, bytes_accessed=20 << 20, transcendentals=0
        ),
        name="mlp_weights",
    )(core, near, far, ht, nrt, cot, gpre, gml)


def load_keys(ref, place_ref, hd, tile, group, knat, kt=None):
    tiles = ref.shape[1] // tile
    for b in range(tiles):
        stretch = place_ref[tiles + b]
        piece = ref[:, b * tile : (b + 1) * tile]
        if kt is not None:
            kt[stretch] = piece
        if knat is not None:
            for h in range(group):
                knat[h, stretch] = piece[h * hd : (h + 1) * hd, :].T


def forward_kernel(
    hd, tile, ids_ref, place_ref, row_ref, col_ref, qt_ref, kt_ref, vt_ref, near_ref, far_ref,
    lse_ref, knat, vt, acc, m_ref, l_ref,
):
    group = qt_ref.shape[0] // hd
    tiles = vt.shape[0]
    load_keys(kt_ref, place_ref, hd, tile, group, knat)
    load_keys(vt_ref, place_ref, hd, tile, group, None, vt)
    per_half = near_ref.shape[1] // tile

    def one_tile(qi, carry):
        stretch = place_ref[tiles + qi]
        full, need = tile_counts(ids_ref, stretch, tile, tiles)
        qcol = pl.ds(pl.multiple_of(qi * tile, tile), tile)
        qpos = pl.ds(pl.multiple_of(stretch * tile, tile), tile)
        m_ref[...] = jnp.full(m_ref.shape, MASKED, F32)
        l_ref[...] = jnp.zeros(l_ref.shape, F32)
        acc[...] = jnp.zeros(acc.shape, F32)

        def step(ts, masked):
            if masked:
                allowed = [
                    col_ref[pl.ds(pl.multiple_of(t * tile, tile), tile), :] <= row_ref[:, qpos]
                    for t in ts
                ]
            scores = [
                [nn(knat[h, t], qt_ref[h * hd : (h + 1) * hd, qcol]) for t in ts]
                for h in range(group)
            ]
            for h in range(group):
                s = scores[h]
                if masked:
                    s = [jnp.where(ok, one, MASKED) for ok, one in zip(allowed, s)]
                old = m_ref[h]
                new = old
                for one in s:
                    new = jnp.maximum(new, jnp.max(one, 0, keepdims=True))
                p = [jnp.exp2(one - new) for one in s]
                alpha = jnp.exp2(old - new)
                total = l_ref[h] * alpha
                for one in p:
                    total = total + jnp.sum(one, 0, keepdims=True)
                l_ref[h] = total
                m_ref[h] = new
                out = acc[h] * alpha
                for t, one in zip(ts, p):
                    out = out + nn(vt[t, h * hd : (h + 1) * hd, :], one.astype(BF))
                acc[h] = out

        def full_step(i, c):
            step([2 * i, 2 * i + 1], False)
            return c

        def mask_step(i, c):
            step([2 * i, 2 * i + 1], True)
            return c

        lax.fori_loop(0, full // 2, full_step, 0)
        lax.fori_loop(full // 2, (need + 1) // 2, mask_step, 0)
        inner = pl.ds(pl.multiple_of((qi % per_half) * tile, tile), tile)
        for half, ref in enumerate((near_ref, far_ref)):

            @pl.when(qi // per_half == half)
            def _(ref=ref):
                for h in range(group):
                    ref[h * hd : (h + 1) * hd, inner] = (acc[h] / l_ref[h]).astype(BF)

        for h in range(group):
            lse_ref[h, :, qcol] = m_ref[h] + jnp.log2(l_ref[h])
        return carry

    lax.fori_loop(0, qt_ref.shape[1] // tile, one_tile, 0)


def backward_kernel(hd, tile, base, count, first, last, *refs):
    ids_ref, place_ref, row_ref, col_ref, qt_ref, kt_ref, vt_ref = refs[:7]
    near_ref, far_ref, onear_ref, ofar_ref, lse_ref = refs[7:12]
    if last:
        before_ref, scale_ref, dqt_ref, dkt_ref, dvt_ref, gs_ref = refs[12:18]
        knat, vnat, kt, dq, dk, dv, delta, dot = refs[18:]
    else:
        dqt_ref, dkt_ref, dvt_ref = refs[12:15]
        knat, vnat, kt, dq, dk, dv, delta, dot = refs[15:]
    tiles = kt_ref.shape[1] // tile
    group = qt_ref.shape[0] // hd

    def block_of(i):
        return pl.multiple_of(place_ref[place_ref[base + i]] * tile, tile)

    for i in range(count):
        cols = pl.ds(block_of(i), tile)
        kt[i] = kt_ref[:, cols]
        for h in range(group):
            hs = slice(h * hd, (h + 1) * hd)
            knat[h, i] = kt_ref[hs, cols].T
            vnat[h, i] = vt_ref[hs, cols].T
    per_half = near_ref.shape[1] // tile
    for half, (ref, o_ref) in enumerate(((near_ref, onear_ref), (far_ref, ofar_ref))):
        for b in range(per_half):
            cols = slice(b * tile, (b + 1) * tile)
            dot[half * per_half + b] = ref[:, cols]
            product = ref[:, cols].astype(F32) * o_ref[:, cols].astype(F32)
            for h in range(group):
                delta[half * per_half + b, h] = jnp.sum(
                    product[h * hd : (h + 1) * hd], 0, keepdims=True
                )
    dk[...] = jnp.zeros(dk.shape, F32)
    dv[...] = jnp.zeros(dv.shape, F32)
    if last:
        gs_ref[...] = jnp.zeros(gs_ref.shape, F32)

    def one_tile(qi, carry):
        stretch = place_ref[tiles + qi]
        low = ids_ref[stretch * tile]
        high = ids_ref[stretch * tile + tile - 1]
        full = jnp.int32(0)
        need = jnp.int32(0)
        for i in range(count):
            t = place_ref[base + i]
            full += (ids_ref[t * tile + tile - 1] <= low).astype(jnp.int32)
            need += (ids_ref[t * tile] <= high).astype(jnp.int32)
        qcol = pl.ds(pl.multiple_of(qi * tile, tile), tile)
        qpos = pl.ds(pl.multiple_of(stretch * tile, tile), tile)
        dq[...] = before_ref[:, qcol] if last else jnp.zeros(dq.shape, F32)

        def step(ts, masked):
            if masked:
                allowed = [
                    col_ref[pl.ds(pl.multiple_of(place_ref[base + t] * tile, tile), tile), :]
                    <= row_ref[:, qpos]
                    for t in ts
                ]

            def scores(h, t):
                hs = slice(h * hd, (h + 1) * hd)
                return nn(knat[h, t], qt_ref[hs, qcol]), nn(vnat[h, t], dot[qi, hs, :])

            order = [(h, i) for h in range(group) for i in range(len(ts))]
            ahead = scores(0, ts[0])
            for j, (h, i) in enumerate(order):
                hs = slice(h * hd, (h + 1) * hd)
                t = ts[i]
                s, dp = ahead
                if j + 1 < len(order):
                    ahead = scores(order[j + 1][0], ts[order[j + 1][1]])
                if masked:
                    s = jnp.where(allowed[i], s, MASKED)
                p = jnp.exp2(s - lse_ref[h, :, qcol])
                ds = (p * (dp - delta[qi, h])).astype(BF)
                dv[t, hs, :] += nt(dot[qi, hs, :], p.astype(BF))
                dk[t, hs, :] += nt(qt_ref[hs, qcol], ds)
                dq[hs, :] += nn(kt[t, hs, :], ds)

        def full_step(i, c):
            step([2 * i, 2 * i + 1], False)
            return c

        def mask_step(i, c):
            step([2 * i, 2 * i + 1], True)
            return c

        lax.fori_loop(0, full // 2, full_step, 0)
        lax.fori_loop(full // 2, (need + 1) // 2, mask_step, 0)
        if last:
            gs_ref[...] += jnp.sum(dq[...] * qt_ref[:, qcol].astype(F32), 1, keepdims=True)
            dqt_ref[:, qcol] = (dq[...] * scale_ref[...]).astype(BF)
        else:
            dqt_ref[:, qcol] = dq[...]
        return carry

    lax.fori_loop(0, qt_ref.shape[1] // tile, one_tile, 0)
    for i in range(count):
        cols = pl.ds(pl.multiple_of(block_of(i) - first * tile, tile), tile)
        dkt_ref[:, cols] = (dk[i] * (1.0 / LOG2E)).astype(BF)
        dvt_ref[:, cols] = dv[i].astype(BF)


def attention_specs(nq, nk, hd, group, at):
    size = group * hd
    return (
        [
            pl.BlockSpec(memory_space=pltpu.SMEM),
            pl.BlockSpec(memory_space=pltpu.SMEM),
            pl.BlockSpec((1, nk), lambda i: (0, 0)),
            pl.BlockSpec((nk, 1), lambda i: (0, 0)),
            pl.BlockSpec((size, nq), lambda i: (i + at, 0)),
            pl.BlockSpec((size, nk), lambda i: (i + at, 0)),
            pl.BlockSpec((size, nk), lambda i: (i + at, 0)),
        ],
        pl.BlockSpec((size, nq // 2), lambda i: (i + at, 0)),
        pl.BlockSpec((group, 1, nq), lambda i: (i + at, 0, 0)),
    )


def attention_forward(ids, col, place, qt, kt, vt, hd, tile):
    heads = qt.shape[0] // hd
    nq, nk = qt.shape[1], kt.shape[1]
    group = HEADS_AT_ONCE
    common, halves, rows = attention_specs(nq, nk, hd, group, 0)
    pairs = heads * nq * nk * 0.6
    return pl.pallas_call(
        functools.partial(forward_kernel, hd, tile),
        grid=(heads // group,),
        in_specs=common,
        out_specs=[halves, halves, rows],
        out_shape=[
            jax.ShapeDtypeStruct((heads * hd, nq // 2), BF),
            jax.ShapeDtypeStruct((heads * hd, nq // 2), BF),
            jax.ShapeDtypeStruct((heads, 1, nq), F32),
        ],
        scratch_shapes=[
            pltpu.VMEM((group, nk // tile, tile, hd), BF),
            pltpu.VMEM((nk // tile, group * hd, tile), BF),
            pltpu.VMEM((group, hd, tile), F32),
            pltpu.VMEM((group, 1, tile), F32),
            pltpu.VMEM((group, 1, tile), F32),
        ],
        compiler_params=pltpu.CompilerParams(vmem_limit_bytes=60 << 20),
        cost_estimate=pl.CostEstimate(
            flops=int(COST * pairs * 1024), bytes_accessed=1 << 16, transcendentals=int(COST * pairs)
        ),
        name="attention_forward",
    )(ids, place, ids.reshape(1, -1), col, qt, kt, vt)


def attention_backward(
    ids, col, place, qt, kt, vt, near, far, onear, ofar, lse, hd, tile, before=None, scale=None
):
    heads = qt.shape[0] // hd
    nq, nk = qt.shape[1], kt.shape[1]
    group = HEADS_AT_ONCE
    size = group * hd
    last = before is not None
    early = nq // tile
    tiles = nk // tile
    count, first = (early, 0) if last else (tiles - early, early)
    base = 2 * tiles + (0 if last else early)
    common, halves, rows = attention_specs(nq, nk, hd, group, 0)
    wide = pl.BlockSpec((size, nq), lambda i: (i, 0))
    keys = pl.BlockSpec((size, count * tile), lambda i: (i, 0))
    one = pl.BlockSpec((size, 1), lambda i: (i, 0))
    pairs = heads * nq * count * tile * 0.6
    return pl.pallas_call(
        functools.partial(backward_kernel, hd, tile, base, count, first, last),
        grid=(heads // group,),
        in_specs=[*common, halves, halves, halves, halves, rows, *([wide, one] if last else [])],
        out_specs=[wide, keys, keys, *([one] if last else [])],
        out_shape=[
            jax.ShapeDtypeStruct((heads * hd, nq), BF if last else F32),
            jax.ShapeDtypeStruct((heads * hd, count * tile), BF),
            jax.ShapeDtypeStruct((heads * hd, count * tile), BF),
            *([jax.ShapeDtypeStruct((heads * hd, 1), F32)] if last else []),
        ],
        scratch_shapes=[
            pltpu.VMEM((group, count, tile, hd), BF),
            pltpu.VMEM((group, count, tile, hd), BF),
            pltpu.VMEM((count, size, tile), BF),
            pltpu.VMEM((size, tile), F32),
            pltpu.VMEM((count, size, tile), F32),
            pltpu.VMEM((count, size, tile), F32),
            pltpu.VMEM((nq // tile, group, 1, tile), F32),
            pltpu.VMEM((nq // tile, size, tile), BF),
        ],
        compiler_params=pltpu.CompilerParams(vmem_limit_bytes=60 << 20),
        cost_estimate=pl.CostEstimate(
            flops=int(pairs * 2560), bytes_accessed=16 << 20, transcendentals=int(pairs)
        ),
        name="attention_backward",
    )(
        ids, place, ids.reshape(1, -1), col, qt, kt, vt, near, far, onear, ofar, lse,
        *([before, scale] if last else []),
    )


def weight_kernel(size, nq, at_ref, xt_ref, dqt_ref, dka_ref, dva_ref, dkb_ref, dvb_ref, *out_refs):
    for m, ref in enumerate(out_refs):

        @pl.when(pl.program_id(0) == m)
        def _(ref=ref):
            early = jnp.concatenate([dka_ref[...], dva_ref[...]], 0)
            late = jnp.concatenate([dkb_ref[...], dvb_ref[...]], 0)
            ref[:, : 2 * size] = (nt(xt_ref[:, :nq], early) + nt(xt_ref[:, nq:], late)).astype(BF)
            ref[:, 2 * size :] = nt(xt_ref[:, :nq], dqt_ref[...]).astype(BF)


def weight_gradient(xt, dqt, early, late, at, pieces, which):
    width, nk = xt.shape
    part, nq = dqt.shape
    size = part // 2
    rows = width // pieces
    once = pl.Buffered(1)

    def heads(cols):
        return pl.BlockSpec((size, cols), lambda i, a: (which, 0), pipeline_mode=once)

    return pl.pallas_call(
        functools.partial(weight_kernel, size, nq),
        grid_spec=pltpu.PrefetchScalarGridSpec(
            num_scalar_prefetch=1,
            grid=(pieces,),
            in_specs=[
                pl.BlockSpec((rows, nk), lambda i, a: (a[i], 0)),
                heads(nq), heads(nq), heads(nq), heads(nk - nq), heads(nk - nq),
            ],
            out_specs=[pl.BlockSpec((rows, 3 * size), lambda i, a: (0, 0))] * pieces,
        ),
        out_shape=[jax.ShapeDtypeStruct((rows, 3 * size), BF)] * pieces,
        compiler_params=pltpu.CompilerParams(vmem_limit_bytes=60 << 20),
        cost_estimate=pl.CostEstimate(
            flops=2 * width * size * (2 * nk + nq), bytes_accessed=12 << 20, transcendentals=0
        ),
        name="weight_gradient",
    )(at, xt, dqt, *early, *late)


def dx_kernel(part, queries, n, core_ref, *refs):
    dk_ref, dv_ref, wk_ref, wv_ref, gain_ref = refs[:5]
    x_refs = refs[5 : 5 + n]
    rest = refs[5 + n :]
    if queries:
        dq_ref, wq_ref = rest[:2]
        rest = rest[2:]
    dx_refs, (gg_ref, g_ref, xs) = rest[:n], rest[n:]
    i = pl.program_id(0)
    tile, width = xs.shape
    step = width // 5
    dk = dk_ref[...].T
    dv = dv_ref[...].T
    if queries:
        dq = dq_ref[...].T
    for c in range(5):
        cols = slice(c * step, (c + 1) * step)
        g = nt(dk, wk_ref[cols, :]) + nt(dv, wv_ref[cols, :])
        if queries:
            g = g + nt(dq, wq_ref[cols, :])
        g_ref[:, cols] = g

    @pl.when(i == 0)
    def _():
        gg_ref[...] = jnp.zeros(gg_ref.shape, F32)

    per_slot = x_refs[0].shape[0] // tile
    for s in range(n):

        @pl.when(i // per_slot == s)
        def _(s=s):
            xs[...] = x_refs[s][pl.ds(pl.multiple_of((i % per_slot) * tile, tile), tile), :]

    x = xs[...].astype(F32)
    inverse = lax.rsqrt(jnp.mean(x * x, -1, keepdims=True) + EPSILON)
    normed = x * inverse
    g = g_ref[...]
    gn = g * normed
    gg_ref[...] += jnp.sum(gn, 0, keepdims=True)
    scaled = g * gain_ref[...]
    mean = jnp.mean(gn * gain_ref[...], -1, keepdims=True)
    out = (inverse * (scaled - normed * mean)).astype(BF)
    for s in range(n):

        @pl.when(i // per_slot == s)
        def _(s=s):
            dx_refs[s][...] = out


def input_gradient(dkvs, dqs, w_full, slots, core, gain):
    part = dkvs[0].shape[0]
    n = len(slots)
    rows, width = slots[0].shape
    tile = rows
    per_slot = rows // tile
    once = pl.Buffered(1)
    dkv = pl.BlockSpec((part, tile), lambda i, c: (0, i))

    def weight(j):
        return pl.BlockSpec(
            (width, part), lambda i, c, j=j: (0, 2 * j + c[0]), pipeline_mode=once
        )

    specs = [
        dkv, dkv, weight(1), weight(2), pl.BlockSpec((1, width), lambda i, c: (0, 0)),
        *[pl.BlockSpec((rows, width), lambda i, c: (0, 0), pipeline_mode=once)] * n,
    ]
    operands = [*dkvs, w_full, w_full, gain, *slots]
    if dqs:
        specs += [dkv, weight(0)]
        operands += [*dqs, w_full]
    return pl.pallas_call(
        functools.partial(dx_kernel, part, bool(dqs), n),
        grid_spec=pltpu.PrefetchScalarGridSpec(
            num_scalar_prefetch=1,
            grid=(n * rows // tile,),
            in_specs=specs,
            out_specs=[
                *[
                    pl.BlockSpec(
                        (tile, width),
                        lambda i, c, s=s: (jnp.clip(i - s * per_slot, 0, per_slot - 1), 0),
                    )
                    for s in range(n)
                ],
                pl.BlockSpec((1, width), lambda i, c: (0, 0)),
            ],
            scratch_shapes=[pltpu.VMEM((tile, width), F32), pltpu.VMEM((tile, width), BF)],
        ),
        out_shape=[
            *[jax.ShapeDtypeStruct((rows, width), BF)] * n,
            jax.ShapeDtypeStruct((1, width), F32),
        ],
        compiler_params=pltpu.CompilerParams(vmem_limit_bytes=60 << 20),
        cost_estimate=pl.CostEstimate(
            flops=int(COST * 2 * width * n * rows * part * (3 if dqs else 2)),
            bytes_accessed=1 << 16,
            transcendentals=0,
        ),
        name="input_gradient",
    )(core, *operands)


class Plan:
    def __init__(self, dp, ctx):
        self.dp, self.ctx = dp, ctx
        self.half = ctx // 2

    def index(self, pair, core, z):
        return (pair * 2 + core) * self.ctx + z

    def perm(self, to):
        out = []
        for d in range(self.dp):
            for z in range(self.ctx):
                got = to(d // 2, d % 2, z)
                if got is not None:
                    out.append((self.index(d // 2, d % 2, z), self.index(*got)))
        return out

    def home(self, core, z):
        return core == z // self.half

    def turned(self, z, k):
        first = z // self.half * self.half
        return first + (z - first + k) % self.half

    def core_swap(self):
        return self.perm(lambda p, c, z: (p, 1 - c, z))

    def pair_swap(self, mask):
        return self.perm(lambda p, c, z: (p ^ mask, c, z))

    def line_swap(self, mask):
        return self.perm(lambda p, c, z: (p, c, z ^ mask))

    def line_in(self, s):
        last = self.ctx - 1
        to = {s: s + 1, last - s: last - s - 1}
        return self.perm(lambda p, c, z: (p, c, to[z]) if z in to else None)

    def line_out(self, s):
        last = self.ctx - 1
        to = {s + 1: s, last - s - 1: last - s}
        return self.perm(lambda p, c, z: (p, c, to[z]) if z in to else None)

    def line_middle(self):
        to = {self.half - 1: self.half, self.half: self.half - 1}
        return self.perm(lambda p, c, z: (p, c, to[z]) if z in to else None)

    def mirror(self):
        return self.perm(
            lambda p, c, z: None if self.home(c, z) else (p, 1 - c, self.ctx - 1 - z)
        )

    def mirror_or_turn(self, k):
        return self.perm(
            lambda p, c, z: (p, c, self.turned(z, k))
            if self.home(c, z)
            else (p, 1 - c, self.ctx - 1 - z)
        )

    def turn(self, k, away_only):
        return self.perm(
            lambda p, c, z: None
            if away_only and self.home(c, z)
            else (p, c, self.turned(z, k))
        )

    def shard(self, core, z, k, mine):
        chip = self.turned(z, -k)
        at_home = self.home(core, z) if mine else not self.home(core, z)
        return chip if at_home else self.ctx - 1 - chip

    def places(self):
        table = np.zeros((self.dp, self.ctx, 6 * self.ctx), np.int32)
        for d in range(self.dp):
            for z in range(self.ctx):
                slots = [
                    self.shard(d % 2, z, k, mine) for k in range(self.half) for mine in (True, False)
                ]
                stretches = [s for shard in slots for s in (shard, 2 * self.ctx - 1 - shard)]
                for block, stretch in enumerate(stretches):
                    table[d, z, stretch] = block
                    table[d, z, 2 * self.ctx + block] = stretch
                table[d, z, 4 * self.ctx :] = sorted(stretches[:4]) + sorted(stretches[4:])
        return table.reshape(self.dp * self.ctx, 6 * self.ctx)


def send(value, pairs):
    return lax.ppermute(value, AXES, pairs)


def tie(*values):
    return lax.optimization_barrier(values)


def line_inward(value, plan, kind):
    total = value.astype(F32)
    for s in range(plan.half - 2):
        total = total + send(total.astype(kind), plan.line_in(s)).astype(F32)
    if plan.half == 1:
        return total, jnp.zeros_like(total, kind)
    return total, send(total.astype(kind), plan.line_in(plan.half - 2))


def line_across(held, came, plan, kind):
    sent = (held + came.astype(F32)).astype(kind)
    return sent, send(sent, plan.line_middle())


def line_joined(sent, came):
    return (sent.astype(F32) + came.astype(F32)).astype(sent.dtype)


def line_outward(total, plan, z):
    for s in reversed(range(plan.half - 1)):
        back = send(total, plan.line_out(s))
        total = jnp.where((z == s) | (z == plan.ctx - 1 - s), back, total)
    return total


def body(
    tokens_in, block_ids, w_qkv, w_out, w_in, w_down, gain_attn, gain_mlp, bias_in, bias_down,
    query_scale, cotangent,
):
    n = lax.axis_size("ctx")
    plan = Plan(lax.axis_size("dp"), n)
    half = plan.half
    z = lax.axis_index("ctx")
    core = lax.axis_index("dp") % 2
    pair = lax.axis_index("dp") // 2
    pairs = plan.dp // 2
    home = core == z // half
    rows = tokens_in.shape[1]
    width = tokens_in.shape[2]
    hd = query_scale.shape[0]
    heads = width // hd
    part = width // 2
    tile = rows // 2
    wrows = w_qkv.shape[0]
    core_swap = plan.core_swap()

    own = tokens_in[0]
    first = send(own, plan.mirror_or_turn(1))
    token0 = jnp.where(home, own, first)
    second = send(token0, plan.turn(1, True))
    mine = [token0, jnp.where(home, first, second)]
    for k in range(2, half):
        mine.append(send(token0, plan.turn(k, False)))
    theirs = [send(m, core_swap) for m in mine]
    slots = [a for both in zip(mine, theirs) for a in both]

    full_qkv = lax.all_gather(w_qkv, "dp", axis=0, tiled=True)
    at = jnp.stack([pair ^ mask for mask in range(pairs)]).astype(jnp.int32)
    core_at = core.astype(jnp.int32).reshape(1)

    ids = jnp.where(home, block_ids[0], send(block_ids[0], core_swap))
    place = lax.dynamic_index_in_dim(
        jnp.asarray(plan.places()), lax.axis_index("dp") * n + z, 0, False
    )
    col = ids.reshape(-1, 1)

    gain_one = gain_attn.astype(F32)
    gain_two = gain_mlp.astype(F32)
    scale_exp = jnp.exp(query_scale.astype(F32))
    scale_dim = SOFT_FACTOR / math.sqrt(hd) * jnp.log1p(scale_exp)
    scale_vec = jnp.tile(scale_dim, heads // 2)[:, None]
    weights = lax.all_gather(
        jnp.concatenate([w_down, w_in, w_out], 1), "dp", axis=0, tiled=True
    )
    qt, kt, vt, xt = project(
        slots, full_qkv, core_at, gain_one.reshape(1, -1), scale_vec * LOG2E
    )
    grad_low = send(tie(cotangent[0], slots[-1])[0], plan.mirror())
    onear, ofar, lse = attention_forward(ids, col, place, qt, kt, vt, hd, tile)
    onear, ofar, grad_low = tie(onear, ofar, grad_low)
    grad_low = jnp.where(home, cotangent[0], grad_low)
    o_got = send(ofar, core_swap)

    (
        output, to_keep, to_give, grad_middle, hidden_t, normed_t, grad_pre, grad_mid_low,
        grad_gain_two, grad_bin, grad_bdown,
    ) = mlp(
        onear, o_got, weights, token0, grad_low, core_at, gain_two.reshape(1, -1),
        bias_in.astype(F32).reshape(1, -1), bias_down.astype(F32).reshape(1, -1),
    )
    far = send(to_give, core_swap)
    away_output = send(output, plan.mirror())
    joined = mlp_weights(onear, o_got, hidden_t, normed_t, grad_low, grad_pre, grad_mid_low, core_at)
    early_qt, joined, far = tie(qt, joined, far)
    scattered = lax.psum_scatter(joined, "dp", scatter_dimension=0, tiled=True)

    def backward(queries, **rest):
        return attention_backward(
            ids, col, place, queries, kt, vt, to_keep, far, onear, ofar, lse, hd, tile, **rest
        )

    def to_owners(grads):
        return [send(grads[m], plan.pair_swap(m)) for m in range(1, pairs)]

    def add_up(grads, came):
        total = grads[0].astype(F32)
        for one in came:
            total = total + one.astype(F32)
        return total

    gain_row = gain_one.reshape(1, -1)
    dq_part, *late_kv = backward(early_qt)
    *late_dx, gain_late = input_gradient(late_kv, (), full_qkv, slots[2:], core_at, gain_row)
    dq_part, away_output, *late_dx = tie(dq_part, away_output, *late_dx)
    output = jnp.where(home, output, away_output)
    late_got = [
        send(late_dx[2 * k + 1], core_swap) for k in range(half - 1)
    ]
    dq_part, *late_got = tie(dq_part, *late_got)
    turned = []
    for k in range(half - 1):
        mine = late_dx[2 * k].astype(F32)
        turned.append(
            send((mine + late_got[k].astype(F32)).astype(BF), plan.turn(-k - 1, False))
        )
    dqt, dk_early, dv_early, gs = backward(qt, before=dq_part, scale=scale_vec)
    dqt, dk_early, dv_early, scattered, *turned = tie(
        dqt, dk_early, dv_early, scattered, *turned
    )
    held_o, line_o = line_inward(scattered, plan, BF)
    early_kv = (dk_early, dv_early)
    grads_a = weight_gradient(xt, dqt, early_kv, late_kv, at, pairs, 0)
    later_dq, *grads_a = tie(dqt, *grads_a)
    came_a = to_owners(grads_a)
    near_dx, far_dx, gain_early = input_gradient(
        early_kv, (later_dq,), full_qkv, slots[:2], core_at, gain_row
    )
    near_dx, far_dx, gain_early, last_dq, line_o, *came_a = tie(
        near_dx, far_dx, gain_early, dqt, line_o, *came_a
    )
    got = send(far_dx, core_swap)
    held_a, line_a = line_inward(add_up(grads_a, came_a), plan, BF)
    held_o, line_o = line_across(held_o, line_o, plan, BF)
    grads_b = weight_gradient(xt, last_dq, early_kv, late_kv, at, pairs, 1)
    scale_slope = SOFT_FACTOR / math.sqrt(hd) * scale_exp / (1.0 + scale_exp)
    grad_scale = jnp.sum(gs.reshape(heads // 2, hd), 0)
    grad_scale = grad_scale * scale_slope / (scale_dim * LOG2E)
    small = jnp.concatenate(
        [
            *(v.reshape(-1) for v in (gain_late + gain_early, grad_gain_two, grad_bin, grad_bdown)),
            grad_scale,
        ]
    )
    small_size = small.shape[0]
    small = jnp.pad(small, (0, -small_size % 1024)).reshape(-1, 128)
    small = small + send(small, core_swap)
    mask = 1
    while mask < pairs:
        small = small + send(small, plan.pair_swap(mask))
        mask *= 2
    got, line_a, small, *grads_b = tie(got, line_a, small, *grads_b)
    came_b = to_owners(grads_b)
    total = near_dx.astype(F32) + got.astype(F32) + grad_middle
    for one in turned:
        total = total + one.astype(F32)
    last = send(total.astype(BF), plan.mirror())
    held_a, line_a = line_across(held_a, line_a, plan, BF)
    line_a, line_o, *came_b = tie(line_a, line_o, *came_b)
    held_b, line_b = line_inward(add_up(grads_b, came_b), plan, BF)
    line_a = line_outward(line_joined(held_a, line_a), plan, z)
    others = line_outward(line_joined(held_o, line_o), plan, z)

    line_b, line_a = tie(line_b, line_a)
    held_b, line_b = line_across(held_b, line_b, plan, BF)

    def owned_rows(value):
        keep = lax.dynamic_slice_in_dim(value, core * wrows, wrows, 0)
        give = lax.dynamic_slice_in_dim(value, (1 - core) * wrows, wrows, 0)
        came = send(give, core_swap)
        return jnp.where(core == 0, keep, came), jnp.where(core == 0, came, keep)

    line_b, line_a, last, small = tie(line_b, line_a, last, small)
    swapped_a = owned_rows(line_a)
    line_b = line_outward(line_joined(held_b, line_b), plan, z)
    came = send(small, plan.line_swap(1))
    line_b, others, came = tie(line_b, others, came)
    small = small + came
    mask = 2
    while mask < n:
        small = small + send(small, plan.line_swap(mask))
        mask *= 2
    small = small.reshape(-1)
    grad_tokens = jnp.where(home, total, last.astype(F32))
    others = others.astype(F32)
    swapped = (swapped_a, owned_rows(line_b))
    size = part // 2
    owned_qkv = jnp.concatenate(
        [
            swapped[g][c][:, which * size : (which + 1) * size].astype(F32)
            for which in (2, 0, 1)
            for c in range(2)
            for g in range(2)
        ],
        1,
    )

    return (
        output[None],
        grad_tokens[None],
        owned_qkv,
        others[:, 2 * width :],
        others[:, width : 2 * width],
        others[:, :width],
        small[:width],
        small[width : 2 * width],
        small[2 * width : 3 * width],
        small[3 * width : 4 * width],
        small[4 * width : small_size],
    )


def solution(mesh):
    split = P("dp", "ctx", None)
    weight = P("dp", None)
    return jax.shard_map(
        body,
        mesh=mesh,
        in_specs=(split, weight, weight, weight, weight, weight, P(), P(), P(), P(), P(), split),
        out_specs=(split, split, weight, weight, weight, weight, P(), P(), P(), P(), P()),
        check_vma=False,
    )
```
